32 devices in a mesh: groups: 2 (over x), vocab: 16 (over z, y, core).
Axes of the slice: x: 2, y: 2, z: 4, core: 2. Of those that a mesh axis runs over, the one named last changes fastest.
Arguments:
- initial_residual_vector: bfloat16 [64, 5376], P(('groups', 'vocab')), parts along dimension 0, may hold values from -50 to 50
- later_layer_deltas: bfloat16 [64, 5376], P(('groups', 'vocab')), parts along dimension 0, may hold values from -400 to 400
- closing_rescale_weight: float32 [5376], replicated, may hold values from 0.5 to 1.5
- shared_lexicon_matrix: bfloat16 [16384, 5376], P('vocab'), may hold values from -3 to 3
- class_heat_lookup: float32 [8], replicated, may hold values from 0.3 to 2
- heat_class: int32 [2, 64], P(None, 'groups'), parts along dimension 1, may hold values from 0 to 7
- drawn_identifiers: int32 [2, 64], P(None, 'groups'), parts along dimension 1, may hold values from 0 to 16383
Outputs:
- logprobs: float32 [2, 64, 16384], P(None, 'groups', 'vocab'), parts along dimension 1
- next_embedded: bfloat16 [64, 5376], P(('groups', 'vocab')), parts along dimension 0
The draws below stay inside these ranges and needn't reach their ends.
There are 2 independent parts, one for each index of `groups`. The reference program is written for one: setup_inputs(seed, part) draws one part's arguments, and reference() takes and returns one part's arrays. A program takes and returns all parts, laid end to end along the dimension named above; an argument that names none is the same for every part. Nothing has to cross between parts.
All inputs are finite; a program needn't handle non-finite values.
Results may differ from the reference program's by a relative error of at most 0.0012.
Values may be sent and summed in bfloat16 or wider, within the bound.
No kernel may reach another device: no remote copies, remote signals or barrier semaphores. Data moves between devices by JAX's collectives and lax.ppermute only.
A program may use at most 64 MiB of HBM per device.

```python
import math
import jax
import jax.numpy as jnp
from jax import lax

D = 5376
VOC_DEV = 1024
STEPS = 2
HEAT_LEVELS = 8
ROWS = 32
VOCAB = 16384


def family_signs(column, family):
    parity = (column * (2 * family + 3) + column * column // 3) % 2
    return 1.0 - 2.0 * parity.astype(jnp.float32)


def base_values(key, rows):
    return jnp.clip(jax.random.normal(key, (rows, D), jnp.float32), -6.0, 6.0)


def spiked_rows(key, strength, offset):
    support_width = min(D, 64)
    values = base_values(key, ROWS)
    row_index = jnp.arange(ROWS, dtype=jnp.int32)[:, None]
    column = jnp.arange(D, dtype=jnp.int32)[None, :]
    family = row_index // 16 % 8
    chosen = row_index % 16 == offset
    aligned = strength * family_signs(column, family)
    special = jnp.where(column < support_width, aligned, 0.0)
    return jnp.where(chosen, special, values)


def draw_initial_residual_vector(key, part):
    key = jax.random.fold_in(key, 1)
    return spiked_rows(key, 40.0, 0).astype(jnp.bfloat16)


def draw_later_layer_deltas(key, part):
    key = jax.random.fold_in(key, 2)
    return spiked_rows(key, 300.0, 8).astype(jnp.bfloat16)


def draw_shared_lexicon_matrix(key, part):
    key = jax.random.fold_in(key, 3)
    scale_key = jax.random.fold_in(key, 11)
    value_key = jax.random.fold_in(key, 12)
    support_width = min(D, 64)
    vocab_index = jnp.arange(VOCAB, dtype=jnp.int32)[:, None]
    factor = jnp.exp(jax.random.uniform(scale_key, (VOCAB, 1), jnp.float32, 0.0, 1.3862944))
    spread = 0.5 * D ** (-0.5) * factor * (1.0 + 2.0 * vocab_index.astype(jnp.float32) / VOCAB)
    values = base_values(value_key, VOCAB) * spread
    within = vocab_index % VOC_DEV
    shard = vocab_index // VOC_DEV
    column = jnp.arange(D, dtype=jnp.int32)[None, :]
    family = shard % 8
    level = 3.0 - 0.75 * (shard // 8 % 3).astype(jnp.float32)
    aligned = level * family_signs(column, family)
    lowered = jnp.where((within == 1) & (column == 0), aligned * (1.0 - (support_width / D) ** 0.5), aligned)
    special_row = jnp.where(column < support_width, lowered, 0.0)
    values = jnp.where(within < 2, special_row, values)
    return values.astype(jnp.bfloat16)


def place_ends(entries, own_key, smallest, high):
    index_at = [jax.random.randint(jax.random.fold_in(own_key, axis), (), 0, length) for axis, length in enumerate(entries.shape)]
    main_axis = entries.shape.index(max(entries.shape))
    beside = index_at[:main_axis] + [(index_at[main_axis] + 1) % entries.shape[main_axis]] + index_at[main_axis + 1:]
    return entries.at[tuple(index_at)].set(smallest).at[tuple(beside)].set(high)


def setup_inputs(seed: int = 0, part: int = 0) -> dict:
    key_list = jax.random.split(jax.random.key(seed), 8)
    part_keys = jax.random.split(jax.random.fold_in(key_list[7], part), 8)
    initial_residual_vector = draw_initial_residual_vector(jax.random.fold_in(jax.random.fold_in(key_list[7], part), 71), part)
    later_layer_deltas = draw_later_layer_deltas(jax.random.fold_in(jax.random.fold_in(key_list[7], part), 71), part)
    closing_rescale_weight = jnp.clip(1.0 + 0.1 * jax.random.normal(key_list[2], (D,), jnp.float32), 0.5, 1.5)
    shared_lexicon_matrix = draw_shared_lexicon_matrix(jax.random.fold_in(key_list[7], 71), part)
    class_heat_lookup = jnp.clip(jnp.exp(jax.random.uniform(key_list[4], (HEAT_LEVELS,), jnp.float32, math.log(0.3), math.log(2.0))), 0.3, 2.0)
    heat_class = place_ends(jax.random.randint(part_keys[5], (STEPS, ROWS), 0, HEAT_LEVELS), jax.random.fold_in(part_keys[5], 1), 0, HEAT_LEVELS - 1).astype(jnp.int32)
    drawn_identifiers = place_ends(jax.random.randint(part_keys[6], (STEPS, ROWS), 0, VOCAB), jax.random.fold_in(part_keys[6], 1), 0, VOCAB - 1).astype(jnp.int32)
    return dict(initial_residual_vector=initial_residual_vector, later_layer_deltas=later_layer_deltas, closing_rescale_weight=closing_rescale_weight, shared_lexicon_matrix=shared_lexicon_matrix, class_heat_lookup=class_heat_lookup, heat_class=heat_class, drawn_identifiers=drawn_identifiers)


def quadratic_rescaled(hidden, closing_rescale_weight):
    squares = lax.optimization_barrier(jnp.mean(hidden * hidden, axis=-1, keepdims=True))
    return (hidden * lax.rsqrt(squares + 1e-06) * closing_rescale_weight).astype(jnp.bfloat16)

def sequence_heat_factors(class_for_sequence, class_heat_lookup):
    check_agreement = class_for_sequence[:, None] == jnp.arange(HEAT_LEVELS, dtype=jnp.int32)[None, :]
    return lax.optimization_barrier(jnp.sum(jnp.where(check_agreement, class_heat_lookup[None, :], jnp.zeros_like(class_heat_lookup)[None, :]), axis=1))

def logarithmic_likelihood(normed_rows, shared_lexicon_matrix, row_temps):
    logits = lax.dot_general(normed_rows, shared_lexicon_matrix, (((1,), (1,)), ((), ())), preferred_element_type=jnp.float32)
    scaled = logits / row_temps[:, None]
    peak = lax.optimization_barrier(jnp.max(scaled, axis=1, keepdims=True))
    total = lax.optimization_barrier(jnp.sum(jnp.exp(scaled - peak), axis=1, keepdims=True))
    return scaled - peak - jnp.log(total)

def embedded(token_ids, shared_lexicon_matrix):
    picked = jnp.take(shared_lexicon_matrix, token_ids.astype(jnp.int32), axis=0).astype(jnp.float32)
    return (picked * math.sqrt(D)).astype(jnp.bfloat16)

def reference(initial_residual_vector, later_layer_deltas, closing_rescale_weight, shared_lexicon_matrix, class_heat_lookup, heat_class, drawn_identifiers):
    opening_draw = logarithmic_likelihood(quadratic_rescaled(initial_residual_vector.astype(jnp.float32), closing_rescale_weight), shared_lexicon_matrix, sequence_heat_factors(heat_class[0], class_heat_lookup))
    input_two = embedded(drawn_identifiers[0], shared_lexicon_matrix)
    later_residual_vector = input_two.astype(jnp.float32) + later_layer_deltas.astype(jnp.float32)
    subsequent_draw = logarithmic_likelihood(quadratic_rescaled(later_residual_vector, closing_rescale_weight), shared_lexicon_matrix, sequence_heat_factors(heat_class[1], class_heat_lookup))
    return (jnp.stack([opening_draw, subsequent_draw]), embedded(drawn_identifiers[1], shared_lexicon_matrix))
```

```python
import functools
import math

import jax
import jax.numpy as jnp
from jax import lax
from jax.experimental import pallas as pl
from jax.experimental.pallas import tpu as pltpu
from jax.sharding import PartitionSpec as P

BLOCK = 16


def gather_kernel(step, ids_ref, table_ref, keep_ref, send_ref, slots, rows, sems):
    count = ids_ref.shape[1]
    half = count // 2
    voc_dev = table_ref.shape[0]
    shards = lax.axis_size("vocab")
    rows_dev = count // shards
    me = lax.axis_index("vocab")
    offset = me * voc_dev

    def copy(r, local):
        base = pl.multiple_of(local // BLOCK * BLOCK, BLOCK)
        return pltpu.make_async_copy(table_ref.at[pl.ds(base, BLOCK)], slots.at[r], sems.at[r])

    for r in range(count):
        local = ids_ref[step, r] - offset

        @pl.when((local >= 0) & (local < voc_dev))
        def _(r=r, local=local):
            copy(r, local).start()

    rows[...] = jnp.zeros_like(rows)
    for r in range(count):
        local = ids_ref[step, r] - offset

        @pl.when((local >= 0) & (local < voc_dev))
        def _(r=r, local=local):
            copy(r, local).wait()
            block = slots[r].astype(jnp.float32)
            lane = lax.broadcasted_iota(jnp.int32, block.shape, 0)
            picked = jnp.sum(jnp.where(lane == local % BLOCK, block, 0.0), axis=0, keepdims=True)
            way = (r // rows_dev) ^ me
            place = (way % 2 * 2 + way // 2 % 2) * (shards // 4) + way // 4
            rows[pl.ds(place * rows_dev + r % rows_dev, 1), :] = picked

    keep_ref[...] = rows[:half].astype(keep_ref.dtype)
    send_ref[...] = rows[half:].astype(send_ref.dtype)


def gathered(ids, table, step):
    count = ids.shape[1]
    width = table.shape[1]
    out = jax.ShapeDtypeStruct((count // 2, width), table.dtype)
    return pl.pallas_call(
        functools.partial(gather_kernel, step),
        out_shape=(out, out),
        in_specs=[pl.BlockSpec(memory_space=pltpu.SMEM), pl.BlockSpec(memory_space=pl.ANY)],
        out_specs=(pl.BlockSpec(memory_space=pltpu.VMEM),) * 2,
        scratch_shapes=[
            pltpu.VMEM((count, BLOCK, width), table.dtype),
            pltpu.VMEM((count, width), jnp.float32),
            pltpu.SemaphoreType.DMA((count,)),
        ],
        compiler_params=pltpu.CompilerParams(vmem_limit_bytes=48 * 2**20),
        name="pick_rows",
    )(ids, table)


def swapped(bit):
    pairs = [(i, i ^ bit) for i in range(lax.axis_size("vocab"))]
    return lambda x: lax.ppermute(x, "vocab", pairs)


def crossed(rows, bit, rows_dev):
    blocks = rows.shape[0] // rows_dev
    parts = rows.reshape(blocks // (2 * bit), 2, bit * rows_dev, rows.shape[1])
    return parts[:, ::-1].reshape(rows.shape)


def norm_kernel(first_ref, picked_ref, delta_ref, gain_ref, out_ref):
    width = first_ref.shape[1]
    quarter = first_ref.shape[0]
    gain = gain_ref[...]

    def rescaled(hidden):
        squares = jnp.mean(hidden * hidden, axis=-1, keepdims=True)
        return hidden * lax.rsqrt(squares + 1e-06) * gain

    one = rescaled(first_ref[...].astype(jnp.float32))
    embedded = (picked_ref[...].astype(jnp.float32) * math.sqrt(width)).astype(jnp.bfloat16)
    two = rescaled(embedded.astype(jnp.float32) + delta_ref[...].astype(jnp.float32))
    out_ref[...] = jnp.concatenate([one, two], axis=0).astype(out_ref.dtype)


def normed(first, picked, delta, gain):
    rows, width = first.shape
    return pl.pallas_call(
        norm_kernel,
        out_shape=jax.ShapeDtypeStruct((2 * rows, width), jnp.bfloat16),
        compiler_params=pltpu.CompilerParams(vmem_limit_bytes=32 * 2**20),
        name="norm",
    )(first, picked, delta, gain.reshape(1, width))


def head_kernel(own_ref, got_ref, table_ref, temps_ref, out_ref, peak_ref, total_ref):
    i = pl.program_id(0)
    rows = out_ref.shape[1]
    shards = lax.axis_size("vocab")
    rows_dev = rows // shards
    quarter = rows // 4
    me = lax.axis_index("vocab")
    dims = (((1,), (1,)), ((), ()))
    states = jnp.concatenate([own_ref[...], got_ref[...]], axis=0)
    logits = lax.dot_general(states, table_ref[...], dims, preferred_element_type=jnp.float32)
    for c in range(2):
        for y in range(2):
            for step in range(2):
                for z in range(shards // 4):
                    place = ((c * 2 + y) * 2 + step) * quarter + z * rows_dev
                    row = ((z * 4 + y * 2 + c) ^ me) * rows_dev
                    for j in range(rows_dev):
                        out_ref[step, pl.ds(row + j, 1), :] = logits[place + j : place + j + 1]
    scaled = out_ref[...] / temps_ref[...]
    out_ref[...] = scaled
    top = jnp.max(scaled, axis=2, keepdims=True)

    @pl.when(i == 0)
    def _():
        peak_ref[...] = jnp.full_like(peak_ref, -jnp.inf)
        total_ref[...] = jnp.zeros_like(total_ref)

    before = peak_ref[...]
    peak = jnp.maximum(before, top)
    total_ref[...] = total_ref[...] * jnp.exp(before - peak) + jnp.sum(
        jnp.exp(scaled - peak), axis=2, keepdims=True
    )
    peak_ref[...] = peak


def head(own, got, table, temps):
    steps, rows = temps.shape[:2]
    voc_dev, width = table.shape
    tile = min(256, voc_dev)
    stat = jax.ShapeDtypeStruct((steps, rows, 1), jnp.float32)
    stat_spec = pl.BlockSpec((steps, rows, 1), lambda i: (0, 0, 0))
    return pl.pallas_call(
        head_kernel,
        grid=(voc_dev // tile,),
        out_shape=(jax.ShapeDtypeStruct((steps, rows, voc_dev), jnp.float32), stat, stat),
        in_specs=[
            pl.BlockSpec(own.shape, lambda i: (0, 0)),
            pl.BlockSpec(got.shape, lambda i: (0, 0)),
            pl.BlockSpec((tile, width), lambda i: (i, 0)),
            stat_spec,
        ],
        out_specs=(
            pl.BlockSpec((steps, rows, tile), lambda i: (0, 0, i)),
            stat_spec,
            stat_spec,
        ),
        compiler_params=pltpu.CompilerParams(vmem_limit_bytes=32 * 2**20),
        name="head",
    )(own, got, table, temps)


def row_temps(classes, lookup):
    levels = jnp.arange(lookup.shape[0], dtype=jnp.int32)
    return jnp.sum(jnp.where(classes[..., None] == levels, lookup, 0.0), axis=-1)


def body(first, deltas, gain, table, lookup, classes, ids):
    shards = lax.axis_size("vocab")
    rows_dev, width = first.shape
    high = [1 << k for k in range(shards.bit_length() - 2, 1, -1)]
    core, chip = swapped(1), swapped(2)

    keep, send = gathered(ids, table, 0)
    keep = keep + core(send)
    quarter = keep.shape[0] // 2
    picked = keep[:quarter] + chip(keep[quarter:])
    for bit in high:
        parcel = jnp.concatenate([picked, first, deltas], axis=0)
        got = swapped(bit)(parcel)
        cut = quarter + first.shape[0]
        picked = picked + crossed(got[:quarter], bit // 4, rows_dev)
        first = jnp.concatenate([first, got[quarter:cut]], axis=0)
        deltas = jnp.concatenate([deltas, got[cut:]], axis=0)
    order = (len(high), rows_dev, width)
    first = ordered(first, len(high), rows_dev)
    deltas = ordered(deltas, len(high), rows_dev)
    states = normed(first, picked, deltas, gain)
    states = jnp.concatenate([states, chip(states)], axis=0)
    others = core(states)
    temps = row_temps(classes, lookup)[..., None]
    scaled, peak, total = head(states, others, table, temps)

    stats = jnp.stack([peak[..., 0], total[..., 0]])
    for bit in high + [2, 1]:
        got = swapped(bit)(stats)
        top = jnp.maximum(stats[0], got[0])
        stats = jnp.stack(
            [top, stats[1] * jnp.exp(stats[0] - top) + got[1] * jnp.exp(got[0] - top)]
        )
    logprobs = scaled - stats[0][..., None] - jnp.log(stats[1])[..., None]

    keep, send = gathered(ids, table, 1)
    keep = keep + core(send)
    keep = keep[:quarter] + chip(keep[quarter:])
    for bit in high:
        half = keep.shape[0] // 2
        keep = keep[:half] + swapped(bit)(keep[half:])
    embedded = (keep.astype(jnp.float32) * math.sqrt(width)).astype(jnp.bfloat16)
    return logprobs, embedded


def ordered(rows, bits, rows_dev):
    width = rows.shape[1]
    blocks = rows.reshape((2,) * bits + (rows_dev, width))
    axes = tuple(range(bits - 1, -1, -1)) + (bits, bits + 1)
    return blocks.transpose(axes).reshape(rows.shape)


def solution(mesh):
    in_specs = (
        P(("groups", "vocab"), None),
        P(("groups", "vocab"), None),
        P(),
        P("vocab", None),
        P(),
        P(None, "groups"),
        P(None, "groups"),
    )
    out_specs = (P(None, "groups", "vocab"), P(("groups", "vocab"), None))
    return jax.shard_map(body, mesh=mesh, in_specs=in_specs, out_specs=out_specs, check_vma=False)
```

```python
import functools
import math

import jax
import jax.numpy as jnp
from jax import lax
from jax.experimental import pallas as pl
from jax.experimental.pallas import tpu as pltpu
from jax.sharding import PartitionSpec as P

BLOCK = 16
MIB = 2**20


def reversed_bits(value, bits):
    out = 0
    for k in range(bits):
        out = out * 2 + (value >> k & 1)
    return out


def table_rows(rows, shards):
    bits = shards.bit_length() - 3
    dev = rows // shards
    return [
        (reversed_bits(q, bits) * 4 + y * 2 + c) * dev + j
        for c in range(2)
        for y in range(2)
        for q in range(shards // 4)
        for j in range(dev)
    ]


def pick_kernel(ids_ref, table_ref, *refs):
    outs, (listed, slots, rows, sems) = refs[:2], refs[2:]
    steps, count = ids_ref.shape
    held = slots.shape[1]
    voc_dev = table_ref.shape[0]
    shards = lax.axis_size("vocab")
    bits = shards.bit_length() - 3
    rows_dev = count // shards
    me = lax.axis_index("vocab")
    offset = me * voc_dev
    low = me % 4

    def copy(step, n):
        local = listed[step, n] // count
        base = pl.multiple_of(local // BLOCK * BLOCK, BLOCK)
        slot = n % held
        return pltpu.make_async_copy(
            table_ref.at[pl.ds(base, BLOCK)], slots.at[step, slot], sems.at[step, slot]
        )

    def start(step, first, found):
        @pl.loop(first, jnp.minimum(found, first + held))
        def _(n):
            copy(step, n).start()

    def finish(step, first, found):
        @pl.loop(first, jnp.minimum(found, first + held))
        def _(n):
            entry = listed[step, n]
            r = entry % count
            copy(step, n).wait()
            block = slots[step, n % held].astype(jnp.float32)
            sub = lax.broadcasted_iota(jnp.int32, block.shape, 0)
            picked = jnp.sum(
                jnp.where(sub == entry // count % BLOCK, block, 0.0), axis=0, keepdims=True
            )
            owner = r // rows_dev
            way = owner % 4 ^ low
            chip = owner // 4 if step == 0 else owner // 4 ^ me // 4
            order = sum((chip >> k) % 2 << (bits - 1 - k) for k in range(bits))
            place = ((way % 2 * steps + step) * 2 + way // 2) * (shards // 4) + order
            rows[pl.ds(place * rows_dev + r % rows_dev, 1), :] = picked

    counts = []
    for step in range(steps):
        found = jnp.int32(0)
        for r in range(count):
            local = ids_ref[step, r] - offset
            listed[step, found] = local * count + r
            found = found + ((local >= 0) & (local < voc_dev)).astype(jnp.int32)
        counts.append(found)
        start(step, 0, found)
    rows[...] = jnp.zeros_like(rows)
    for step, found in enumerate(counts):
        finish(step, 0, found)
        for first in range(held, count, held):
            start(step, first, found)
            finish(step, first, found)

    for half, out in enumerate(outs):
        out[...] = rows[half * count : (half + 1) * count].astype(out.dtype)


def picked_rows(ids, table):
    steps, count = ids.shape
    width = table.shape[1]
    held = min(count, 32)
    out = jax.ShapeDtypeStruct((count * steps // 2, width), table.dtype)
    return pl.pallas_call(
        pick_kernel,
        out_shape=(out, out),
        in_specs=[pl.BlockSpec(memory_space=pltpu.SMEM), pl.BlockSpec(memory_space=pl.ANY)],
        out_specs=(pl.BlockSpec(memory_space=pltpu.VMEM),) * 2,
        scratch_shapes=[
            pltpu.SMEM((steps, count + 1), jnp.int32),
            pltpu.VMEM((steps, held, BLOCK, width), table.dtype),
            pltpu.VMEM((steps * count, width), jnp.float32),
            pltpu.SemaphoreType.DMA((steps, held)),
        ],
        compiler_params=pltpu.CompilerParams(vmem_limit_bytes=24 * MIB),
        name="pick",
    )(ids, pltpu.with_memory_space_constraint(table, pltpu.HBM))


def swapped(rows, bit):
    pairs = [(i, i ^ bit) for i in range(lax.axis_size("vocab"))]
    return lax.ppermute(rows, "vocab", pairs)


def load_kernel(table_ref, after_ref, out_ref, sems):
    parts = sems.shape[0]
    part = table_ref.shape[0] // parts
    copies = [
        pltpu.make_async_copy(
            table_ref.at[pl.ds(k * part, part)], out_ref.at[pl.ds(k * part, part)], sems.at[k]
        )
        for k in range(parts)
    ]
    for copy in copies:
        copy.start()
    for copy in copies:
        copy.wait()


def loaded(table, after):
    return pl.pallas_call(
        load_kernel,
        out_shape=jax.ShapeDtypeStruct(table.shape, table.dtype),
        in_specs=[pl.BlockSpec(memory_space=pl.ANY)] * 2,
        out_specs=pl.BlockSpec(memory_space=pltpu.VMEM),
        scratch_shapes=[pltpu.SemaphoreType.DMA((8,))],
        compiler_params=pltpu.CompilerParams(vmem_limit_bytes=4 * MIB),
        cost_estimate=pl.CostEstimate(
            flops=0, bytes_accessed=table.size * table.dtype.itemsize, transcendentals=0
        ),
        name="load",
    )(pltpu.with_memory_space_constraint(table, pltpu.HBM), after)


def norm_kernel(
    places, first_ref, own_ref, got_ref, delta_ref, gain_ref, class_ref, heat_ref, out_ref, temps_ref
):
    temps = jnp.ones(temps_ref.shape, jnp.float32)
    lane = lax.broadcasted_iota(jnp.int32, temps.shape, 1)
    for place, (step, row) in enumerate(places):
        temps = jnp.where(lane == place, heat_ref[class_ref[step, row]], temps)
    temps_ref[...] = temps
    width = first_ref.shape[1]
    gain = gain_ref[...]

    def rescaled(hidden):
        squares = jnp.mean(hidden * hidden, axis=-1, keepdims=True)
        return hidden * lax.rsqrt(squares + 1e-06) * gain

    me = lax.axis_index("vocab")
    bits = lax.axis_size("vocab").bit_length() - 3

    def in_order(rows):
        for k in range(bits):
            size = rows.shape[0] >> k + 1
            parts = [rows[i * size : (i + 1) * size] for i in range(2 << k)]
            other = [parts[i ^ 1] for i in range(2 << k)]
            rows = jnp.where(
                me // 4 >> k & 1 != 0, jnp.concatenate(other), jnp.concatenate(parts)
            )
        return rows

    one = rescaled(in_order(first_ref[...].astype(jnp.float32)))
    picked = own_ref[...].astype(jnp.float32) + got_ref[...].astype(jnp.float32)
    embedded = (picked * math.sqrt(width)).astype(jnp.bfloat16)
    two = rescaled(
        embedded.astype(jnp.float32) + in_order(delta_ref[...].astype(jnp.float32))
    )
    out_ref[...] = jnp.concatenate([one, two], axis=0).astype(out_ref.dtype)


def normed(first, own, got, delta, gain, classes, lookup, places):
    rows, width = first.shape
    smem, vmem = pl.BlockSpec(memory_space=pltpu.SMEM), pl.BlockSpec(memory_space=pltpu.VMEM)
    return pl.pallas_call(
        functools.partial(norm_kernel, places),
        out_shape=(
            jax.ShapeDtypeStruct((2 * rows, width), jnp.bfloat16),
            jax.ShapeDtypeStruct((1, len(places)), jnp.float32),
        ),
        in_specs=[vmem] * 5 + [smem] * 2,
        out_specs=(vmem, vmem),
        compiler_params=pltpu.CompilerParams(vmem_limit_bytes=8 * MIB),
        name="norm",
    )(first, own, got, delta, gain.reshape(1, width), classes, lookup)


def head_kernel(own_ref, got_ref, table_ref, temps_ref, scaled_ref, stats_ref):
    me = lax.axis_index("vocab")
    half, width = own_ref.shape
    dims = (((1,), (1,)), ((), ()))
    own, got = own_ref[...], got_ref[...]
    block = half // 2

    def chips(rows):
        return jnp.where(
            me // 2 % 2 == 1, jnp.concatenate([rows[block:], rows[:block]], axis=0), rows
        )

    own, got = chips(own), chips(got)
    states = jnp.where(
        me % 2 == 1, jnp.concatenate([got, own], axis=0), jnp.concatenate([own, got], axis=0)
    )
    logits = lax.dot_general(table_ref[...], states, dims, preferred_element_type=jnp.float32)
    scaled = logits / temps_ref[...]
    scaled_ref[...] = scaled
    peak = jnp.max(scaled, axis=0, keepdims=True)
    stats_ref[0:1, :] = peak
    stats_ref[1:2, :] = jnp.sum(jnp.exp(scaled - peak), axis=0, keepdims=True)


def head(own, got, table, temps):
    voc_dev, width = table.shape
    rows = 2 * own.shape[0]
    return pl.pallas_call(
        head_kernel,
        out_shape=(
            jax.ShapeDtypeStruct((voc_dev, rows), jnp.float32),
            jax.ShapeDtypeStruct((2, rows), jnp.float32),
        ),
        compiler_params=pltpu.CompilerParams(vmem_limit_bytes=30 * MIB),
        name="head",
    )(own, got, table, temps)


def turn_kernel(order, scaled_ref, out_ref):
    turned = scaled_ref[...].T
    for place, (step, row) in enumerate(order):
        out_ref[step, row : row + 1, :] = turned[place : place + 1]


def turned(scaled, order, steps):
    voc_dev, rows = scaled.shape
    return pl.pallas_call(
        functools.partial(turn_kernel, order),
        out_shape=jax.ShapeDtypeStruct((steps, rows // steps, voc_dev), jnp.float32),
        compiler_params=pltpu.CompilerParams(vmem_limit_bytes=8 * MIB),
        name="turn",
    )(scaled)


def finish_kernel(order, scaled_ref, own_ref, got_ref, out_ref):
    own, got = own_ref[...], got_ref[...]
    peak = jnp.maximum(own[0:1], got[0:1])
    total = own[1:2] * jnp.exp(own[0:1] - peak) + got[1:2] * jnp.exp(got[0:1] - peak)
    both = jnp.concatenate([peak, jnp.log(total)], axis=0)
    rows = both.shape[1]
    spread = jnp.broadcast_to(both[:, None, :], (2, 128, rows))
    peak, log = spread[0].T, spread[1].T
    voc_dev = out_ref.shape[2]
    peak = jnp.concatenate([peak] * (voc_dev // 128), axis=1)
    log = jnp.concatenate([log] * (voc_dev // 128), axis=1)
    for place, (step, row) in enumerate(order):
        at = slice(place, place + 1)
        out_ref[step, row : row + 1, :] = scaled_ref[step, row : row + 1, :] - peak[at] - log[at]


def finished(scaled, own, got, order):
    return pl.pallas_call(
        functools.partial(finish_kernel, order),
        out_shape=jax.ShapeDtypeStruct(scaled.shape, jnp.float32),
        compiler_params=pltpu.CompilerParams(vmem_limit_bytes=8 * MIB),
        name="finish",
    )(scaled, own, got)


def merged(own, got):
    peak = jnp.maximum(own[0], got[0])
    total = own[1] * jnp.exp(own[0] - peak) + got[1] * jnp.exp(got[0] - peak)
    return jnp.stack([peak, total])


def body(first, deltas, gain, table, lookup, classes, ids):
    shards = lax.axis_size("vocab")
    rows_dev, width = first.shape
    steps, rows = ids.shape
    quarter = rows // 4
    high = [1 << k for k in range(shards.bit_length() - 2, 1, -1)]

    keep, send = picked_rows(ids, table)
    keep = (keep + swapped(send, 1)).reshape(steps, 2, quarter, width)
    own = keep[0, 0] + swapped(keep[0, 1], 2)
    following = keep[1, 0] + swapped(keep[1, 1], 2)
    state, delta = first, deltas
    for k, bit in enumerate(high):
        held = state.shape[0]
        moved = swapped(jnp.concatenate([state, delta], axis=0), bit)
        got = swapped(own, bit)
        state = jnp.concatenate([state, moved[:held]], axis=0)
        delta = jnp.concatenate([delta, moved[held:]], axis=0)
        if k < len(high) - 1:
            own = own + got
    order = table_rows(rows, shards)
    places = [
        (step, order[pair * quarter + k])
        for pair in range(4)
        for step in range(steps)
        for k in range(quarter)
    ]
    states, temps = normed(state, own, got, delta, gain, classes, lookup, places)
    states = jnp.concatenate([states, swapped(states, 2)], axis=0)
    scaled, stats = head(states, swapped(states, 1), loaded(table, temps), temps)
    scaled = turned(scaled, places, steps)
    exchange = high + [2, 1]
    for bit in exchange[:-1]:
        stats = merged(stats, swapped(stats, bit))
    logprobs = finished(scaled, stats, swapped(stats, exchange[-1]), places)

    for bit in reversed(high):
        half = following.shape[0] // 2
        following = following[:half] + swapped(following[half:], bit)
    embedded = (following.astype(jnp.float32) * math.sqrt(width)).astype(jnp.bfloat16)
    return logprobs, embedded


def solution(mesh):
    in_specs = (
        P(("groups", "vocab"), None),
        P(("groups", "vocab"), None),
        P(),
        P("vocab", None),
        P(),
        P(None, "groups"),
        P(None, "groups"),
    )
    out_specs = (P(None, "groups", "vocab"), P(("groups", "vocab"), None))
    return jax.shard_map(body, mesh=mesh, in_specs=in_specs, out_specs=out_specs, check_vma=False)
```

```python
import functools
import math

import jax
import jax.numpy as jnp
from jax import lax
from jax.experimental import pallas as pl
from jax.experimental.pallas import tpu as pltpu
from jax.sharding import PartitionSpec as P

BLOCK = 16
MIB = 2**20


def reversed_bits(value, bits):
    out = 0
    for k in range(bits):
        out = out * 2 + (value >> k & 1)
    return out


def table_rows(rows, shards):
    bits = shards.bit_length() - 3
    dev = rows // shards
    return [
        (reversed_bits(q, bits) * 4 + y * 2 + c) * dev + j
        for c in range(2)
        for y in range(2)
        for q in range(shards // 4)
        for j in range(dev)
    ]


def pick_kernel(step, ids_ref, table_ref, after_ref, *refs):
    outs, (ids, listed, slots, rows, ids_sem, sems) = refs[:2], refs[2:]
    count = ids_ref.shape[1]
    held = slots.shape[0]
    voc_dev = table_ref.shape[0]
    shards = lax.axis_size("vocab")
    bits = shards.bit_length() - 3
    rows_dev = count // shards
    me = lax.axis_index("vocab")
    offset = me * voc_dev
    low = me % 4
    fetch = pltpu.make_async_copy(ids_ref, ids, ids_sem)
    fetch.start()
    rows[...] = jnp.zeros_like(rows)
    fetch.wait()

    def copy(n):
        base = pl.multiple_of(listed[n] // count // BLOCK * BLOCK, BLOCK)
        slot = n % held
        return pltpu.make_async_copy(
            table_ref.at[pl.ds(base, BLOCK)], slots.at[slot], sems.at[slot]
        )

    found = jnp.int32(0)
    for r in range(count):
        local = ids[step, r] - offset
        listed[found] = local * count + r
        found = found + ((local >= 0) & (local < voc_dev)).astype(jnp.int32)

    for first in range(0, count, held):
        last = jnp.minimum(found, first + held)

        @pl.loop(first, last)
        def _(n):
            copy(n).start()

        @pl.loop(first, last)
        def _(n):
            entry = listed[n]
            r = entry % count
            copy(n).wait()
            block = slots[n % held].astype(jnp.float32)
            sub = lax.broadcasted_iota(jnp.int32, block.shape, 0)
            picked = jnp.sum(
                jnp.where(sub == entry // count % BLOCK, block, 0.0), axis=0, keepdims=True
            )
            owner = r // rows_dev
            way = owner % 4 ^ low
            chip = owner // 4 if step == 0 else owner // 4 ^ me // 4
            order = sum((chip >> k) % 2 << (bits - 1 - k) for k in range(bits))
            place = (way % 2 * 2 + way // 2) * (shards // 4) + order
            rows[pl.ds(place * rows_dev + r % rows_dev, 1), :] = picked

    half = count // 2
    for part, out in enumerate(outs):
        out[...] = rows[part * half : (part + 1) * half].astype(out.dtype)


def picked_rows(ids, table, step, after):
    count = ids.shape[1]
    width = table.shape[1]
    held = min(count, 32)
    out = jax.ShapeDtypeStruct((count // 2, width), table.dtype)
    return pl.pallas_call(
        functools.partial(pick_kernel, step),
        out_shape=(out, out),
        in_specs=[pl.BlockSpec(memory_space=pl.ANY)] * 3,
        out_specs=(pl.BlockSpec(memory_space=pltpu.VMEM),) * 2,
        scratch_shapes=[
            pltpu.SMEM(ids.shape, jnp.int32),
            pltpu.SMEM((count + 1,), jnp.int32),
            pltpu.VMEM((held, BLOCK, width), table.dtype),
            pltpu.VMEM((count, width), jnp.float32),
            pltpu.SemaphoreType.DMA,
            pltpu.SemaphoreType.DMA((held,)),
        ],
        compiler_params=pltpu.CompilerParams(vmem_limit_bytes=16 * MIB),
        name="pick",
    )(in_hbm(ids), in_hbm(table), after)


def in_hbm(array):
    return pltpu.with_memory_space_constraint(array, pltpu.HBM)


def fold_kernel(keep_ref, got_ref, first_ref, delta_ref, own_ref, send_ref, beside_ref):
    total = keep_ref[...].astype(jnp.float32) + got_ref[...].astype(jnp.float32)
    half = own_ref.shape[0]
    own_ref[...] = total[:half].astype(own_ref.dtype)
    send_ref[...] = total[half:].astype(send_ref.dtype)
    beside_ref[...] = jnp.concatenate(
        [first_ref[...].astype(jnp.float32), delta_ref[...].astype(jnp.float32)], axis=0
    ).astype(beside_ref.dtype)


def folded(keep, got, first, deltas):
    rows, width = keep.shape
    vmem = pl.BlockSpec(memory_space=pltpu.VMEM)
    part = jax.ShapeDtypeStruct((rows // 2, width), keep.dtype)
    return pl.pallas_call(
        fold_kernel,
        out_shape=(part, part, jax.ShapeDtypeStruct((2 * first.shape[0], width), keep.dtype)),
        in_specs=[vmem] * 4,
        out_specs=(vmem,) * 3,
        compiler_params=pltpu.CompilerParams(vmem_limit_bytes=12 * MIB),
        name="fold",
    )(keep, got, first, deltas)


def swapped(rows, bit):
    pairs = [(i, i ^ bit) for i in range(lax.axis_size("vocab"))]
    return lax.ppermute(rows, "vocab", pairs)


def load_kernel(places, table_ref, class_ref, heat_ref, after_ref, out_ref, temps_ref, sems):
    parts = sems.shape[0]
    part = table_ref.shape[0] // parts
    copies = [
        pltpu.make_async_copy(
            table_ref.at[pl.ds(k * part, part)], out_ref.at[pl.ds(k * part, part)], sems.at[k]
        )
        for k in range(parts)
    ]
    for copy in copies:
        copy.start()
    temps = jnp.ones(temps_ref.shape, jnp.float32)
    lane = lax.broadcasted_iota(jnp.int32, temps.shape, 1)
    for place, (step, row) in enumerate(places):
        temps = jnp.where(lane == place, heat_ref[class_ref[step, row]], temps)
    temps_ref[...] = temps
    for copy in copies:
        copy.wait()


def loaded(table, classes, lookup, places, after):
    hbm, smem, vmem = (pl.BlockSpec(memory_space=m) for m in (pl.ANY, pltpu.SMEM, pltpu.VMEM))
    return pl.pallas_call(
        functools.partial(load_kernel, places),
        out_shape=(
            jax.ShapeDtypeStruct(table.shape, table.dtype),
            jax.ShapeDtypeStruct((1, len(places)), jnp.float32),
        ),
        in_specs=[hbm, smem, smem, hbm],
        out_specs=(vmem, vmem),
        scratch_shapes=[pltpu.SemaphoreType.DMA((8,))],
        compiler_params=pltpu.CompilerParams(vmem_limit_bytes=4 * MIB),
        cost_estimate=pl.CostEstimate(
            flops=0, bytes_accessed=table.size * table.dtype.itemsize, transcendentals=0
        ),
        name="load",
    )(in_hbm(table), classes, lookup, after)


def norm_kernel(first_ref, own_ref, got_ref, delta_ref, gain_ref, after_ref, out_ref):
    width = first_ref.shape[1]
    gain = gain_ref[...]

    def rescaled(hidden):
        squares = jnp.mean(hidden * hidden, axis=-1, keepdims=True)
        return hidden * lax.rsqrt(squares + 1e-06) * gain

    me = lax.axis_index("vocab")
    bits = lax.axis_size("vocab").bit_length() - 3

    def in_order(rows):
        for k in range(bits):
            size = rows.shape[0] >> k + 1
            parts = [rows[i * size : (i + 1) * size] for i in range(2 << k)]
            other = [parts[i ^ 1] for i in range(2 << k)]
            rows = jnp.where(
                me // 4 >> k & 1 != 0, jnp.concatenate(other), jnp.concatenate(parts)
            )
        return rows

    one = rescaled(in_order(first_ref[...].astype(jnp.float32)))
    picked = own_ref[...].astype(jnp.float32) + got_ref[...].astype(jnp.float32)
    embedded = (picked * math.sqrt(width)).astype(jnp.bfloat16)
    two = rescaled(
        embedded.astype(jnp.float32) + in_order(delta_ref[...].astype(jnp.float32))
    )
    out_ref[...] = jnp.concatenate([one, two], axis=0).astype(out_ref.dtype)


def normed(first, own, got, delta, gain, after):
    rows, width = first.shape
    vmem = pl.BlockSpec(memory_space=pltpu.VMEM)
    return pl.pallas_call(
        norm_kernel,
        out_shape=jax.ShapeDtypeStruct((2 * rows, width), jnp.bfloat16),
        in_specs=[vmem] * 5 + [pl.BlockSpec(memory_space=pl.ANY)],
        out_specs=vmem,
        compiler_params=pltpu.CompilerParams(vmem_limit_bytes=12 * MIB),
        name="norm",
    )(first, own, got, delta, gain.reshape(1, width), after)


def head_kernel(own_ref, got_ref, table_ref, temps_ref, after_ref, scaled_ref, stats_ref):
    me = lax.axis_index("vocab")
    half, width = own_ref.shape
    dims = (((1,), (1,)), ((), ()))
    own, got = own_ref[...], got_ref[...]
    block = half // 2

    def chips(rows):
        return jnp.where(
            me // 2 % 2 == 1, jnp.concatenate([rows[block:], rows[:block]], axis=0), rows
        )

    own, got = chips(own), chips(got)
    states = jnp.where(
        me % 2 == 1, jnp.concatenate([got, own], axis=0), jnp.concatenate([own, got], axis=0)
    )
    logits = lax.dot_general(table_ref[...], states, dims, preferred_element_type=jnp.float32)
    scaled = logits / temps_ref[...]
    scaled_ref[...] = scaled
    peak = jnp.max(scaled, axis=0, keepdims=True)
    stats_ref[0:1, :] = peak
    stats_ref[1:2, :] = jnp.sum(jnp.exp(scaled - peak), axis=0, keepdims=True)


def head(own, got, table, temps, after):
    voc_dev, width = table.shape
    rows = 2 * own.shape[0]
    return pl.pallas_call(
        head_kernel,
        out_shape=(
            jax.ShapeDtypeStruct((voc_dev, rows), jnp.float32),
            jax.ShapeDtypeStruct((2, rows), jnp.float32),
        ),
        in_specs=[pl.BlockSpec(memory_space=pltpu.VMEM)] * 4 + [pl.BlockSpec(memory_space=pl.ANY)],
        out_specs=(pl.BlockSpec(memory_space=pltpu.VMEM),) * 2,
        compiler_params=pltpu.CompilerParams(vmem_limit_bytes=30 * MIB),
        name="head",
    )(own, got, table, temps, after)


def turn_kernel(order, scaled_ref, out_ref):
    turned = scaled_ref[...].T
    for place, (step, row) in enumerate(order):
        out_ref[step, row : row + 1, :] = turned[place : place + 1]


def turned(scaled, order, steps):
    voc_dev, rows = scaled.shape
    return pl.pallas_call(
        functools.partial(turn_kernel, order),
        out_shape=jax.ShapeDtypeStruct((steps, rows // steps, voc_dev), jnp.float32),
        compiler_params=pltpu.CompilerParams(vmem_limit_bytes=12 * MIB),
        name="turn",
    )(scaled)


def finish_kernel(order, scaled_ref, own_ref, got_ref, out_ref):
    own, got = own_ref[...], got_ref[...]
    peak = jnp.maximum(own[0:1], got[0:1])
    total = own[1:2] * jnp.exp(own[0:1] - peak) + got[1:2] * jnp.exp(got[0:1] - peak)
    both = jnp.concatenate([peak, jnp.log(total)], axis=0)
    rows = both.shape[1]
    spread = jnp.broadcast_to(both[:, None, :], (2, 128, rows))
    peak, log = spread[0].T, spread[1].T
    voc_dev = out_ref.shape[2]
    peak = jnp.concatenate([peak] * (voc_dev // 128), axis=1)
    log = jnp.concatenate([log] * (voc_dev // 128), axis=1)
    for place, (step, row) in enumerate(order):
        at = slice(place, place + 1)
        out_ref[step, row : row + 1, :] = scaled_ref[step, row : row + 1, :] - peak[at] - log[at]


def finished(scaled, own, got, order):
    return pl.pallas_call(
        functools.partial(finish_kernel, order),
        out_shape=jax.ShapeDtypeStruct(scaled.shape, jnp.float32),
        compiler_params=pltpu.CompilerParams(vmem_limit_bytes=12 * MIB),
        name="finish",
    )(scaled, own, got)


def merged(own, got):
    peak = jnp.maximum(own[0], got[0])
    total = own[1] * jnp.exp(own[0] - peak) + got[1] * jnp.exp(got[0] - peak)
    return jnp.stack([peak, total])


def body(first, deltas, gain, table, lookup, classes, ids):
    shards = lax.axis_size("vocab")
    rows_dev, width = first.shape
    steps, rows = ids.shape
    quarter = rows // 4
    high = [1 << k for k in range(shards.bit_length() - 2, 1, -1)]

    order = table_rows(rows, shards)
    places = [
        (step, order[pair * quarter + k])
        for pair in range(4)
        for step in range(steps)
        for k in range(quarter)
    ]

    keep, send = picked_rows(ids, table, 0, ids)
    own, send, beside = folded(keep, swapped(send, 1), first, deltas)
    keep, away = picked_rows(ids, table, 1, own)
    own = own + swapped(send, 2)
    keep = keep + swapped(away, 1)
    following = keep[:quarter] + swapped(keep[quarter:], 2)
    state, delta = beside[:rows_dev], beside[rows_dev:]
    for k, bit in enumerate(high):
        held = state.shape[0]
        moved = swapped(beside, bit)
        got = swapped(own, bit)
        state = jnp.concatenate([state, moved[:held]], axis=0)
        delta = jnp.concatenate([delta, moved[held:]], axis=0)
        beside = jnp.concatenate([state, delta], axis=0)
        if k < len(high) - 1:
            own = own + got
    head_table, temps = loaded(table, classes, lookup, places, own)
    states = normed(state, own, got, delta, gain, temps)
    states = jnp.concatenate([states, swapped(states, 2)], axis=0)
    others = swapped(states, 1)
    for bit in reversed(high):
        half = following.shape[0] // 2
        following = following[:half] + swapped(following[half:], bit)
    embedded = (following.astype(jnp.float32) * math.sqrt(width)).astype(jnp.bfloat16)
    scaled, stats = head(states, others, head_table, temps, following)
    scaled = turned(scaled, places, steps)
    exchange = high + [2, 1]
    for bit in exchange[:-1]:
        stats = merged(stats, swapped(stats, bit))
    logprobs = finished(scaled, stats, swapped(stats, exchange[-1]), places)
    return logprobs, embedded


def solution(mesh):
    in_specs = (
        P(("groups", "vocab"), None),
        P(("groups", "vocab"), None),
        P(),
        P("vocab", None),
        P(),
        P(None, "groups"),
        P(None, "groups"),
    )
    out_specs = (P(None, "groups", "vocab"), P(("groups", "vocab"), None))
    return jax.shard_map(body, mesh=mesh, in_specs=in_specs, out_specs=out_specs, check_vma=False)
```

```python
import functools
import math

import jax
import jax.numpy as jnp
from jax import lax
from jax.experimental import pallas as pl
from jax.experimental.pallas import tpu as pltpu
from jax.sharding import PartitionSpec as P

BLOCK = 16
MIB = 2**20


def reversed_bits(value, bits):
    out = 0
    for k in range(bits):
        out = out * 2 + (value >> k & 1)
    return out


def table_rows(rows, shards):
    bits = shards.bit_length() - 3
    dev = rows // shards
    return [
        (reversed_bits(q, bits) * 4 + y * 2 + c) * dev + j
        for c in range(2)
        for y in range(2)
        for q in range(shards // 4)
        for j in range(dev)
    ]


def pick_kernel(step, ids_ref, table_ref, after_ref, *refs):
    outs, (ids, listed, slots, rows, ids_sem, sems) = refs[:2], refs[2:]
    count = ids_ref.shape[1]
    held = slots.shape[0]
    voc_dev = table_ref.shape[0]
    shards = lax.axis_size("vocab")
    bits = shards.bit_length() - 3
    rows_dev = count // shards
    me = lax.axis_index("vocab")
    offset = me * voc_dev
    low = me % 4
    fetch = pltpu.make_async_copy(ids_ref, ids, ids_sem)
    fetch.start()
    rows[...] = jnp.zeros_like(rows)
    fetch.wait()

    def copy(n):
        base = pl.multiple_of(listed[n] // count // BLOCK * BLOCK, BLOCK)
        slot = n % held
        return pltpu.make_async_copy(
            table_ref.at[pl.ds(base, BLOCK)], slots.at[slot], sems.at[slot]
        )

    found = jnp.int32(0)
    for r in range(count):
        local = ids[step, r] - offset
        listed[found] = local * count + r
        found = found + ((local >= 0) & (local < voc_dev)).astype(jnp.int32)

    for first in range(0, count, held):
        last = jnp.minimum(found, first + held)

        @pl.loop(first, last)
        def _(n):
            copy(n).start()

        @pl.loop(first, last)
        def _(n):
            entry = listed[n]
            r = entry % count
            copy(n).wait()
            block = slots[n % held].astype(jnp.float32)
            sub = lax.broadcasted_iota(jnp.int32, block.shape, 0)
            picked = jnp.sum(
                jnp.where(sub == entry // count % BLOCK, block, 0.0), axis=0, keepdims=True
            )
            owner = r // rows_dev
            way = owner % 4 ^ low
            order = owner // 4 ^ me // 4
            if step == 0:
                order = sum((owner // 4 >> k) % 2 << (bits - 1 - k) for k in range(bits))
            place = (way % 2 * 2 + way // 2) * (shards // 4) + order
            rows[pl.ds(place * rows_dev + r % rows_dev, 1), :] = picked

    half = count // 2
    for part, out in enumerate(outs):
        out[...] = rows[part * half : (part + 1) * half].astype(out.dtype)


def picked_rows(ids, table, step, after):
    count = ids.shape[1]
    width = table.shape[1]
    held = min(count, 32)
    out = jax.ShapeDtypeStruct((count // 2, width), table.dtype)
    return pl.pallas_call(
        functools.partial(pick_kernel, step),
        out_shape=(out, out),
        in_specs=[pl.BlockSpec(memory_space=pl.ANY)] * 3,
        out_specs=(pl.BlockSpec(memory_space=pltpu.VMEM),) * 2,
        scratch_shapes=[
            pltpu.SMEM(ids.shape, jnp.int32),
            pltpu.SMEM((count + 1,), jnp.int32),
            pltpu.VMEM((held, BLOCK, width), table.dtype),
            pltpu.VMEM((count, width), jnp.float32),
            pltpu.SemaphoreType.DMA,
            pltpu.SemaphoreType.DMA((held,)),
        ],
        compiler_params=pltpu.CompilerParams(vmem_limit_bytes=16 * MIB),
        name="pick",
    )(in_hbm(ids), in_hbm(table), after)


def in_hbm(array):
    return pltpu.with_memory_space_constraint(array, pltpu.HBM)


def fold_kernel(keep_ref, got_ref, first_ref, delta_ref, own_ref, send_ref, beside_ref):
    total = keep_ref[...].astype(jnp.float32) + got_ref[...].astype(jnp.float32)
    half = own_ref.shape[0]
    own_ref[...] = total[:half].astype(own_ref.dtype)
    send_ref[...] = total[half:].astype(send_ref.dtype)
    beside_ref[...] = jnp.concatenate(
        [first_ref[...].astype(jnp.float32), delta_ref[...].astype(jnp.float32)], axis=0
    ).astype(beside_ref.dtype)


def folded(keep, got, first, deltas):
    rows, width = keep.shape
    vmem = pl.BlockSpec(memory_space=pltpu.VMEM)
    part = jax.ShapeDtypeStruct((rows // 2, width), keep.dtype)
    return pl.pallas_call(
        fold_kernel,
        out_shape=(part, part, jax.ShapeDtypeStruct((2 * first.shape[0], width), keep.dtype)),
        in_specs=[vmem] * 4,
        out_specs=(vmem,) * 3,
        compiler_params=pltpu.CompilerParams(vmem_limit_bytes=12 * MIB),
        name="fold",
    )(keep, got, first, deltas)


def plus_kernel(own_ref, got_ref, after_ref, out_ref):
    out_ref[...] = own_ref[...] + got_ref[...]


def join_kernel(own_ref, got_ref, after_ref, out_ref):
    half = own_ref.shape[0] // 2
    own, got = own_ref[...].astype(jnp.float32), got_ref[...].astype(jnp.float32)
    parts = [own[:half], got[:half], own[half:], got[half:]]
    out_ref[...] = jnp.concatenate(parts, axis=0).astype(out_ref.dtype)


def merge_kernel(own_ref, got_ref, after_ref, out_ref):
    own, got = own_ref[...], got_ref[...]
    peak = jnp.maximum(own[0:1], got[0:1])
    out_ref[0:1, :] = peak
    out_ref[1:2, :] = own[1:2] * jnp.exp(own[0:1] - peak) + got[1:2] * jnp.exp(got[0:1] - peak)


def paired(kernel, own, got, after, rows, name):
    vmem = pl.BlockSpec(memory_space=pltpu.VMEM)
    return pl.pallas_call(
        kernel,
        out_shape=jax.ShapeDtypeStruct((rows, own.shape[1]), own.dtype),
        in_specs=[vmem, vmem, pl.BlockSpec(memory_space=pl.ANY)],
        out_specs=vmem,
        compiler_params=pltpu.CompilerParams(vmem_limit_bytes=12 * MIB),
        name=name,
    )(own, got, after)


def swapped(rows, bit):
    pairs = [(i, i ^ bit) for i in range(lax.axis_size("vocab"))]
    return lax.ppermute(rows, "vocab", pairs)


def load_kernel(places, table_ref, class_ref, heat_ref, after_ref, out_ref, temps_ref, sems):
    parts = sems.shape[0]
    part = out_ref.shape[0] // parts
    copies = [
        pltpu.make_async_copy(
            table_ref.at[pl.ds(k * part, part)], out_ref.at[pl.ds(k * part, part)], sems.at[k]
        )
        for k in range(parts)
    ]
    for copy in copies:
        copy.start()
    temps = jnp.ones(temps_ref.shape, jnp.float32)
    lane = lax.broadcasted_iota(jnp.int32, temps.shape, 1)
    for place, (step, row) in enumerate(places):
        temps = jnp.where(lane == place, heat_ref[class_ref[step, row]], temps)
    temps_ref[...] = temps
    for copy in copies:
        copy.wait()


def loaded(table, classes, lookup, places, after):
    held = table.shape[0] // 8 * 5
    hbm, smem, vmem = (pl.BlockSpec(memory_space=m) for m in (pl.ANY, pltpu.SMEM, pltpu.VMEM))
    return pl.pallas_call(
        functools.partial(load_kernel, places),
        out_shape=(
            jax.ShapeDtypeStruct((held, table.shape[1]), table.dtype),
            jax.ShapeDtypeStruct((1, len(places)), jnp.float32),
        ),
        in_specs=[hbm, smem, smem, hbm],
        out_specs=(vmem, vmem),
        scratch_shapes=[pltpu.SemaphoreType.DMA((5,))],
        compiler_params=pltpu.CompilerParams(vmem_limit_bytes=4 * MIB),
        cost_estimate=pl.CostEstimate(
            flops=0,
            bytes_accessed=held * table.shape[1] * table.dtype.itemsize,
            transcendentals=0,
        ),
        name="load",
    )(in_hbm(table), classes, lookup, after)


def norm_kernel(first_ref, own_ref, got_ref, delta_ref, gain_ref, after_ref, out_ref):
    width = first_ref.shape[1]
    gain = gain_ref[...]

    def rescaled(hidden):
        squares = jnp.mean(hidden * hidden, axis=-1, keepdims=True)
        return hidden * lax.rsqrt(squares + 1e-06) * gain

    me = lax.axis_index("vocab")
    bits = lax.axis_size("vocab").bit_length() - 3

    def in_order(rows):
        for k in range(bits):
            size = rows.shape[0] >> k + 1
            parts = [rows[i * size : (i + 1) * size] for i in range(2 << k)]
            other = [parts[i ^ 1] for i in range(2 << k)]
            rows = jnp.where(
                me // 4 >> k & 1 != 0, jnp.concatenate(other), jnp.concatenate(parts)
            )
        return rows

    one = rescaled(in_order(first_ref[...].astype(jnp.float32)))
    picked = own_ref[...].astype(jnp.float32) + got_ref[...].astype(jnp.float32)
    embedded = (picked * math.sqrt(width)).astype(jnp.bfloat16)
    two = rescaled(
        embedded.astype(jnp.float32) + in_order(delta_ref[...].astype(jnp.float32))
    )
    out_ref[...] = jnp.concatenate([one, two], axis=0).astype(out_ref.dtype)


def normed(first, own, got, delta, gain, after):
    rows, width = first.shape
    vmem = pl.BlockSpec(memory_space=pltpu.VMEM)
    return pl.pallas_call(
        norm_kernel,
        out_shape=jax.ShapeDtypeStruct((2 * rows, width), jnp.bfloat16),
        in_specs=[vmem] * 5 + [pl.BlockSpec(memory_space=pl.ANY)],
        out_specs=vmem,
        compiler_params=pltpu.CompilerParams(vmem_limit_bytes=12 * MIB),
        name="norm",
    )(first, own, got, delta, gain.reshape(1, width), after)


def head_kernel(
    own_ref, got_ref, held_ref, table_ref, temps_ref, after_ref, scaled_ref, stats_ref, rest, sems
):
    me = lax.axis_index("vocab")
    half, width = own_ref.shape
    first = held_ref.shape[0]
    parts = sems.shape[0]
    part = rest.shape[0] // parts
    copies = [
        pltpu.make_async_copy(
            table_ref.at[pl.ds(first + k * part, part)], rest.at[pl.ds(k * part, part)], sems.at[k]
        )
        for k in range(parts)
    ]
    for copy in copies:
        copy.start()
    dims = (((1,), (1,)), ((), ()))
    own, got = own_ref[...], got_ref[...]
    block = half // 2

    def chips(rows):
        return jnp.where(
            me // 2 % 2 == 1, jnp.concatenate([rows[block:], rows[:block]], axis=0), rows
        )

    own, got = chips(own), chips(got)
    states = jnp.where(
        me % 2 == 1, jnp.concatenate([got, own], axis=0), jnp.concatenate([own, got], axis=0)
    )

    def scaled_part(rows):
        logits = lax.dot_general(rows, states, dims, preferred_element_type=jnp.float32)
        return logits / temps_ref[...]

    scaled_ref[:first, :] = scaled_part(held_ref[...])
    for copy in copies:
        copy.wait()
    scaled_ref[first:, :] = scaled_part(rest[...])
    scaled = scaled_ref[...]
    peak = jnp.max(scaled, axis=0, keepdims=True)
    stats_ref[0:1, :] = peak
    stats_ref[1:2, :] = jnp.sum(jnp.exp(scaled - peak), axis=0, keepdims=True)


def head(own, got, held, table, temps, after):
    voc_dev, width = table.shape
    rows = 2 * own.shape[0]
    vmem, anywhere = pl.BlockSpec(memory_space=pltpu.VMEM), pl.BlockSpec(memory_space=pl.ANY)
    return pl.pallas_call(
        head_kernel,
        out_shape=(
            jax.ShapeDtypeStruct((voc_dev, rows), jnp.float32),
            jax.ShapeDtypeStruct((2, rows), jnp.float32),
        ),
        in_specs=[vmem] * 3 + [anywhere, vmem, anywhere],
        out_specs=(vmem,) * 2,
        scratch_shapes=[
            pltpu.VMEM((voc_dev - held.shape[0], width), table.dtype),
            pltpu.SemaphoreType.DMA((3,)),
        ],
        compiler_params=pltpu.CompilerParams(vmem_limit_bytes=30 * MIB),
        name="head",
    )(own, got, held, in_hbm(table), temps, after)


def turn_kernel(order, scaled_ref, out_ref):
    turned = scaled_ref[...].T
    for place, (step, row) in enumerate(order):
        out_ref[step, row : row + 1, :] = turned[place : place + 1]


def turned(scaled, order, steps):
    voc_dev, rows = scaled.shape
    return pl.pallas_call(
        functools.partial(turn_kernel, order),
        out_shape=jax.ShapeDtypeStruct((steps, rows // steps, voc_dev), jnp.float32),
        compiler_params=pltpu.CompilerParams(vmem_limit_bytes=12 * MIB),
        name="turn",
    )(scaled)


def finish_kernel(order, scaled_ref, own_ref, got_ref, out_ref):
    own, got = own_ref[...], got_ref[...]
    peak = jnp.maximum(own[0:1], got[0:1])
    total = own[1:2] * jnp.exp(own[0:1] - peak) + got[1:2] * jnp.exp(got[0:1] - peak)
    both = jnp.concatenate([peak, jnp.log(total)], axis=0)
    rows = both.shape[1]
    spread = jnp.broadcast_to(both[:, None, :], (2, 128, rows))
    peak, log = spread[0].T, spread[1].T
    voc_dev = out_ref.shape[2]
    peak = jnp.concatenate([peak] * (voc_dev // 128), axis=1)
    log = jnp.concatenate([log] * (voc_dev // 128), axis=1)
    for place, (step, row) in enumerate(order):
        at = slice(place, place + 1)
        out_ref[step, row : row + 1, :] = scaled_ref[step, row : row + 1, :] - peak[at] - log[at]


def finished(scaled, own, got, order):
    return pl.pallas_call(
        functools.partial(finish_kernel, order),
        out_shape=jax.ShapeDtypeStruct(scaled.shape, jnp.float32),
        compiler_params=pltpu.CompilerParams(vmem_limit_bytes=12 * MIB),
        name="finish",
    )(scaled, own, got)


def merged(own, got):
    peak = jnp.maximum(own[0], got[0])
    total = own[1] * jnp.exp(own[0] - peak) + got[1] * jnp.exp(got[0] - peak)
    return jnp.stack([peak, total])


def body(first, deltas, gain, table, lookup, classes, ids):
    shards = lax.axis_size("vocab")
    rows_dev, width = first.shape
    steps, rows = ids.shape
    quarter = rows // 4
    high = [1 << k for k in range(shards.bit_length() - 2, 1, -1)]

    order = table_rows(rows, shards)
    places = [
        (step, order[pair * quarter + k])
        for pair in range(4)
        for step in range(steps)
        for k in range(quarter)
    ]

    keep, send = picked_rows(ids, table, 0, ids)
    own, send, beside = folded(keep, swapped(send, 1), first, deltas)
    own = own + swapped(send, 2)
    held_table, temps = loaded(table, classes, lookup, places, own)
    for k, bit in enumerate(high):
        held = beside.shape[0] // 2
        moved = swapped(beside, bit)
        got = swapped(own, bit)
        if k < len(high) - 1:
            beside = paired(join_kernel, beside, moved, own, 4 * held, "join")
            own = paired(plus_kernel, own, got, temps, quarter, "plus")
    state = jnp.concatenate([beside[:held], moved[:held]], axis=0)
    delta = jnp.concatenate([beside[held:], moved[held:]], axis=0)
    keep, send = picked_rows(ids, table, 1, own)
    states = normed(state, own, got, delta, gain, send)
    keep = keep + swapped(send, 1)
    following = keep[:quarter] + swapped(keep[quarter:], 2)
    states = jnp.concatenate([states, swapped(states, 2)], axis=0)
    others = swapped(states, 1)
    scaled, stats = head(states, others, held_table, table, temps, following)
    scaled = turned(scaled, places, steps)
    for bit in high:
        half = following.shape[0] // 2
        following = following[:half] + swapped(following[half:], bit)
    embedded = (following.astype(jnp.float32) * math.sqrt(width)).astype(jnp.bfloat16)
    for bit in high[:-1]:
        stats = merged(stats, swapped(stats, bit))
    stats = paired(merge_kernel, stats, swapped(stats, high[-1]), following, 2, "merge")
    stats = merged(stats, swapped(stats, 2))
    logprobs = finished(scaled, stats, swapped(stats, 1), places)
    return logprobs, embedded


def solution(mesh):
    in_specs = (
        P(("groups", "vocab"), None),
        P(("groups", "vocab"), None),
        P(),
        P("vocab", None),
        P(),
        P(None, "groups"),
        P(None, "groups"),
    )
    out_specs = (P(None, "groups", "vocab"), P(("groups", "vocab"), None))
    return jax.shard_map(body, mesh=mesh, in_specs=in_specs, out_specs=out_specs, check_vma=False)
```

```python
import functools
import math

import jax
import jax.numpy as jnp
from jax import lax
from jax.experimental import pallas as pl
from jax.experimental.pallas import tpu as pltpu
from jax.sharding import PartitionSpec as P

BLOCK = 16
MIB = 2**20


def reversed_bits(value, bits):
    out = 0
    for k in range(bits):
        out = out * 2 + (value >> k & 1)
    return out


def table_rows(rows, shards):
    bits = shards.bit_length() - 3
    dev = rows // shards
    return [
        (reversed_bits(q, bits) * 4 + y * 2 + c) * dev + j
        for c in range(2)
        for y in range(2)
        for q in range(shards // 4)
        for j in range(dev)
    ]


def pick_kernel(step, ids_ref, table_ref, after_ref, *refs):
    outs, (ids, listed, slots, rows, ids_sem, sems) = refs[:2], refs[2:]
    count = ids_ref.shape[1]
    held = slots.shape[0]
    voc_dev = table_ref.shape[0]
    shards = lax.axis_size("vocab")
    bits = shards.bit_length() - 3
    rows_dev = count // shards
    me = lax.axis_index("vocab")
    offset = me * voc_dev
    low = me % 4
    fetch = pltpu.make_async_copy(ids_ref, ids, ids_sem)
    fetch.start()
    rows[...] = jnp.zeros_like(rows)
    fetch.wait()

    def copy(n):
        base = pl.multiple_of(listed[n] // count // BLOCK * BLOCK, BLOCK)
        slot = n % held
        return pltpu.make_async_copy(
            table_ref.at[pl.ds(base, BLOCK)], slots.at[slot], sems.at[slot]
        )

    found = jnp.int32(0)
    for r in range(count):
        local = ids[step, r] - offset
        listed[found] = local * count + r
        found = found + ((local >= 0) & (local < voc_dev)).astype(jnp.int32)

    for first in range(0, count, held):
        last = jnp.minimum(found, first + held)

        @pl.loop(first, last)
        def _(n):
            copy(n).start()

        @pl.loop(first, last)
        def _(n):
            entry = listed[n]
            r = entry % count
            copy(n).wait()
            block = slots[n % held].astype(jnp.float32)
            sub = lax.broadcasted_iota(jnp.int32, block.shape, 0)
            picked = jnp.sum(
                jnp.where(sub == entry // count % BLOCK, block, 0.0), axis=0, keepdims=True
            )
            owner = r // rows_dev
            way = owner % 4 ^ low
            order = owner // 4 ^ me // 4
            if step == 0:
                order = sum((owner // 4 >> k) % 2 << (bits - 1 - k) for k in range(bits))
            place = (way % 2 * 2 + way // 2) * (shards // 4) + order
            rows[pl.ds(place * rows_dev + r % rows_dev, 1), :] = picked

    half = count // 2
    for part, out in enumerate(outs):
        out[...] = rows[part * half : (part + 1) * half].astype(out.dtype)


def picked_rows(ids, table, step, after):
    count = ids.shape[1]
    width = table.shape[1]
    held = min(count, 32)
    out = jax.ShapeDtypeStruct((count // 2, width), table.dtype)
    return pl.pallas_call(
        functools.partial(pick_kernel, step),
        out_shape=(out, out),
        in_specs=[pl.BlockSpec(memory_space=pl.ANY)] * 3,
        out_specs=(pl.BlockSpec(memory_space=pltpu.VMEM),) * 2,
        scratch_shapes=[
            pltpu.SMEM(ids.shape, jnp.int32),
            pltpu.SMEM((count + 1,), jnp.int32),
            pltpu.VMEM((held, BLOCK, width), table.dtype),
            pltpu.VMEM((count, width), jnp.float32),
            pltpu.SemaphoreType.DMA,
            pltpu.SemaphoreType.DMA((held,)),
        ],
        compiler_params=pltpu.CompilerParams(vmem_limit_bytes=16 * MIB),
        name="pick",
    )(in_hbm(ids), in_hbm(table), after)


def in_hbm(array):
    return pltpu.with_memory_space_constraint(array, pltpu.HBM)


def fold_kernel(keep_ref, got_ref, first_ref, delta_ref, own_ref, send_ref, beside_ref):
    total = keep_ref[...].astype(jnp.float32) + got_ref[...].astype(jnp.float32)
    half = own_ref.shape[0]
    own_ref[...] = total[:half].astype(own_ref.dtype)
    send_ref[...] = total[half:].astype(send_ref.dtype)
    beside_ref[...] = jnp.concatenate(
        [first_ref[...].astype(jnp.float32), delta_ref[...].astype(jnp.float32)], axis=0
    ).astype(beside_ref.dtype)


def folded(keep, got, first, deltas):
    rows, width = keep.shape
    vmem = pl.BlockSpec(memory_space=pltpu.VMEM)
    part = jax.ShapeDtypeStruct((rows // 2, width), keep.dtype)
    return pl.pallas_call(
        fold_kernel,
        out_shape=(part, part, jax.ShapeDtypeStruct((2 * first.shape[0], width), keep.dtype)),
        in_specs=[vmem] * 4,
        out_specs=(vmem,) * 3,
        compiler_params=pltpu.CompilerParams(vmem_limit_bytes=12 * MIB),
        name="fold",
    )(keep, got, first, deltas)


def plus_kernel(own_ref, got_ref, *refs):
    out_ref = refs[-1]
    out_ref[...] = own_ref[...] + got_ref[...]


def join_kernel(own_ref, got_ref, *refs):
    out_ref = refs[-1]
    half = own_ref.shape[0] // 2
    own, got = own_ref[...].astype(jnp.float32), got_ref[...].astype(jnp.float32)
    parts = [own[:half], got[:half], own[half:], got[half:]]
    out_ref[...] = jnp.concatenate(parts, axis=0).astype(out_ref.dtype)


def chips_kernel(own_ref, got_ref, *refs):
    out_ref = refs[-1]
    own, got = own_ref[...], got_ref[...]
    upper = lax.axis_index("vocab") // 2 % 2 == 1
    rows = own.shape[0]
    out_ref[:rows, :] = jnp.where(upper, got, own)
    out_ref[rows:, :] = jnp.where(upper, own, got)


def merge_kernel(own_ref, got_ref, *refs):
    out_ref = refs[-1]
    own, got = own_ref[...], got_ref[...]
    peak = jnp.maximum(own[0:1], got[0:1])
    out_ref[0:1, :] = peak
    out_ref[1:2, :] = own[1:2] * jnp.exp(own[0:1] - peak) + got[1:2] * jnp.exp(got[0:1] - peak)


def paired(kernel, own, got, rows, name, *after):
    vmem = pl.BlockSpec(memory_space=pltpu.VMEM)
    return pl.pallas_call(
        kernel,
        out_shape=jax.ShapeDtypeStruct((rows, own.shape[1]), own.dtype),
        in_specs=[vmem] * 2 + [pl.BlockSpec(memory_space=pl.ANY)] * len(after),
        out_specs=vmem,
        compiler_params=pltpu.CompilerParams(vmem_limit_bytes=12 * MIB),
        name=name,
    )(own, got, *after)


def swapped(rows, bit):
    pairs = [(i, i ^ bit) for i in range(lax.axis_size("vocab"))]
    return lax.ppermute(rows, "vocab", pairs)


def load_kernel(places, table_ref, class_ref, heat_ref, after_ref, out_ref, temps_ref, sems):
    copies = part_copies(table_ref, out_ref, sems, 0)
    for copy in copies:
        copy.start()
    temps = jnp.ones(temps_ref.shape, jnp.float32)
    lane = lax.broadcasted_iota(jnp.int32, temps.shape, 1)
    for place, (step, row) in enumerate(places):
        temps = jnp.where(lane == place, heat_ref[class_ref[step, row]], temps)
    temps_ref[...] = temps
    for copy in copies:
        copy.wait()


def more_kernel(table_ref, held_ref, after_ref, out_ref, token_ref, sems):
    copies = part_copies(table_ref, out_ref, sems, table_ref.shape[0] // 2)
    for copy in copies:
        copy.start()
    token_ref[...] = jnp.zeros_like(token_ref)
    for copy in copies:
        copy.wait()


def part_copies(table_ref, out_ref, sems, first):
    parts = sems.shape[0]
    part = table_ref.shape[0] // 2 // parts
    rows = [pl.ds(first + k * part, part) for k in range(parts)]
    return [
        pltpu.make_async_copy(table_ref.at[at], out_ref.at[at], sems.at[k])
        for k, at in enumerate(rows)
    ]


def loaded(table, classes, lookup, places, after):
    hbm, smem, vmem = (pl.BlockSpec(memory_space=m) for m in (pl.ANY, pltpu.SMEM, pltpu.VMEM))
    return pl.pallas_call(
        functools.partial(load_kernel, places),
        out_shape=(
            jax.ShapeDtypeStruct(table.shape, table.dtype),
            jax.ShapeDtypeStruct((1, len(places)), jnp.float32),
        ),
        in_specs=[hbm, smem, smem, hbm],
        out_specs=(vmem, vmem),
        scratch_shapes=[pltpu.SemaphoreType.DMA((4,))],
        compiler_params=pltpu.CompilerParams(vmem_limit_bytes=4 * MIB),
        name="load",
    )(in_hbm(table), classes, lookup, after)


def loaded_more(table, held, after):
    anywhere, vmem = pl.BlockSpec(memory_space=pl.ANY), pl.BlockSpec(memory_space=pltpu.VMEM)
    return pl.pallas_call(
        more_kernel,
        out_shape=(
            jax.ShapeDtypeStruct(table.shape, table.dtype),
            jax.ShapeDtypeStruct((8, 128), jnp.float32),
        ),
        in_specs=[anywhere, vmem, anywhere],
        out_specs=(vmem, vmem),
        input_output_aliases={1: 0},
        scratch_shapes=[pltpu.SemaphoreType.DMA((4,))],
        compiler_params=pltpu.CompilerParams(vmem_limit_bytes=4 * MIB),
        name="more",
    )(in_hbm(table), held, after)


def norm_kernel(
    first_ref, own_ref, got_ref, delta_ref, gain_ref, after_ref, also_ref, out_ref
):
    width = first_ref.shape[1]
    gain = gain_ref[...]

    def rescaled(hidden):
        squares = jnp.mean(hidden * hidden, axis=-1, keepdims=True)
        return hidden * lax.rsqrt(squares + 1e-06) * gain

    me = lax.axis_index("vocab")
    bits = lax.axis_size("vocab").bit_length() - 3

    def in_order(rows):
        for k in range(bits):
            size = rows.shape[0] >> k + 1
            parts = [rows[i * size : (i + 1) * size] for i in range(2 << k)]
            other = [parts[i ^ 1] for i in range(2 << k)]
            rows = jnp.where(
                me // 4 >> k & 1 != 0, jnp.concatenate(other), jnp.concatenate(parts)
            )
        return rows

    one = rescaled(in_order(first_ref[...].astype(jnp.float32)))
    picked = own_ref[...].astype(jnp.float32) + got_ref[...].astype(jnp.float32)
    embedded = (picked * math.sqrt(width)).astype(jnp.bfloat16)
    two = rescaled(
        embedded.astype(jnp.float32) + in_order(delta_ref[...].astype(jnp.float32))
    )
    out_ref[...] = jnp.concatenate([one, two], axis=0).astype(out_ref.dtype)


def normed(first, own, got, delta, gain, after, also):
    rows, width = first.shape
    vmem = pl.BlockSpec(memory_space=pltpu.VMEM)
    return pl.pallas_call(
        norm_kernel,
        out_shape=jax.ShapeDtypeStruct((2 * rows, width), jnp.bfloat16),
        in_specs=[vmem] * 5 + [pl.BlockSpec(memory_space=pl.ANY)] * 2,
        out_specs=vmem,
        compiler_params=pltpu.CompilerParams(vmem_limit_bytes=12 * MIB),
        name="norm",
    )(first, own, got, delta, gain.reshape(1, width), after, also)


def head_kernel(own_ref, got_ref, table_ref, temps_ref, scaled_ref, stats_ref):
    me = lax.axis_index("vocab")
    dims = (((1,), (1,)), ((), ()))
    own, got = own_ref[...], got_ref[...]
    states = jnp.where(
        me % 2 == 1, jnp.concatenate([got, own], axis=0), jnp.concatenate([own, got], axis=0)
    )
    logits = lax.dot_general(table_ref[...], states, dims, preferred_element_type=jnp.float32)
    scaled = logits / temps_ref[...]
    scaled_ref[...] = scaled
    peak = jnp.max(scaled, axis=0, keepdims=True)
    stats_ref[0:1, :] = peak
    stats_ref[1:2, :] = jnp.sum(jnp.exp(scaled - peak), axis=0, keepdims=True)


def head(own, got, table, temps):
    voc_dev, width = table.shape
    rows = 2 * own.shape[0]
    return pl.pallas_call(
        head_kernel,
        out_shape=(
            jax.ShapeDtypeStruct((voc_dev, rows), jnp.float32),
            jax.ShapeDtypeStruct((2, rows), jnp.float32),
        ),
        in_specs=[pl.BlockSpec(memory_space=pltpu.VMEM)] * 4,
        out_specs=(pl.BlockSpec(memory_space=pltpu.VMEM),) * 2,
        compiler_params=pltpu.CompilerParams(vmem_limit_bytes=30 * MIB),
        name="head",
    )(own, got, table, temps)


def turn_kernel(order, scaled_ref, out_ref):
    turned = scaled_ref[...].T
    for place, (step, row) in enumerate(order):
        out_ref[step, row : row + 1, :] = turned[place : place + 1]


def turned(scaled, order, steps):
    voc_dev, rows = scaled.shape
    return pl.pallas_call(
        functools.partial(turn_kernel, order),
        out_shape=jax.ShapeDtypeStruct((steps, rows // steps, voc_dev), jnp.float32),
        compiler_params=pltpu.CompilerParams(vmem_limit_bytes=12 * MIB),
        name="turn",
    )(scaled)


def finish_kernel(order, scaled_ref, own_ref, got_ref, out_ref):
    own, got = own_ref[...], got_ref[...]
    peak = jnp.maximum(own[0:1], got[0:1])
    total = own[1:2] * jnp.exp(own[0:1] - peak) + got[1:2] * jnp.exp(got[0:1] - peak)
    both = jnp.concatenate([peak, jnp.log(total)], axis=0)
    rows = both.shape[1]
    spread = jnp.broadcast_to(both[:, None, :], (2, 128, rows))
    peak, log = spread[0].T, spread[1].T
    voc_dev = out_ref.shape[2]
    peak = jnp.concatenate([peak] * (voc_dev // 128), axis=1)
    log = jnp.concatenate([log] * (voc_dev // 128), axis=1)
    for place, (step, row) in enumerate(order):
        at = slice(place, place + 1)
        out_ref[step, row : row + 1, :] = scaled_ref[step, row : row + 1, :] - peak[at] - log[at]


def finished(scaled, own, got, order):
    return pl.pallas_call(
        functools.partial(finish_kernel, order),
        out_shape=jax.ShapeDtypeStruct(scaled.shape, jnp.float32),
        compiler_params=pltpu.CompilerParams(vmem_limit_bytes=12 * MIB),
        name="finish",
    )(scaled, own, got)


def merged(own, got):
    peak = jnp.maximum(own[0], got[0])
    total = own[1] * jnp.exp(own[0] - peak) + got[1] * jnp.exp(got[0] - peak)
    return jnp.stack([peak, total])


def body(first, deltas, gain, table, lookup, classes, ids):
    shards = lax.axis_size("vocab")
    rows_dev, width = first.shape
    steps, rows = ids.shape
    quarter = rows // 4
    high = [1 << k for k in range(shards.bit_length() - 2, 1, -1)]

    order = table_rows(rows, shards)
    places = [
        (step, order[pair * quarter + k])
        for pair in range(4)
        for step in range(steps)
        for k in range(quarter)
    ]

    keep, send = picked_rows(ids, table, 0, ids)
    own, send, beside = folded(keep, swapped(send, 1), first, deltas)
    own = own + swapped(send, 2)
    keep, send = picked_rows(ids, table, 1, own)
    keep = keep + swapped(send, 1)
    following = keep[:quarter] + swapped(keep[quarter:], 2)
    for k, bit in enumerate(high):
        held = beside.shape[0] // 2
        moved = swapped(beside, bit)
        got = swapped(own, bit)
        if k < len(high) - 1:
            beside = paired(join_kernel, beside, moved, 4 * held, "join", own)
            own = paired(plus_kernel, own, got, quarter, "plus", send)
    state = jnp.concatenate([beside[:held], moved[:held]], axis=0)
    delta = jnp.concatenate([beside[held:], moved[held:]], axis=0)
    held_table, temps = loaded(table, classes, lookup, places, own)
    states = normed(state, own, got, delta, gain, temps, following)
    held_table, token = loaded_more(table, held_table, states)
    half = quarter // 2
    away = swapped(following[half:], high[0])
    states = paired(chips_kernel, states, swapped(states, 2), rows, "chips", token, away)
    others = swapped(states, 1)
    scaled, stats = head(states, others, held_table, temps)
    following = paired(plus_kernel, following[:half], away, half, "plus", stats)
    scaled = turned(scaled, places, steps)
    for bit in high[1:]:
        half = following.shape[0] // 2
        following = following[:half] + swapped(following[half:], bit)
    embedded = (following.astype(jnp.float32) * math.sqrt(width)).astype(jnp.bfloat16)
    for bit in high[:-1]:
        stats = merged(stats, swapped(stats, bit))
    stats = paired(merge_kernel, stats, swapped(stats, high[-1]), 2, "merge", following)
    stats = merged(stats, swapped(stats, 2))
    logprobs = finished(scaled, stats, swapped(stats, 1), places)
    return logprobs, embedded


def solution(mesh):
    in_specs = (
        P(("groups", "vocab"), None),
        P(("groups", "vocab"), None),
        P(),
        P("vocab", None),
        P(),
        P(None, "groups"),
        P(None, "groups"),
    )
    out_specs = (P(None, "groups", "vocab"), P(("groups", "vocab"), None))
    return jax.shard_map(body, mesh=mesh, in_specs=in_specs, out_specs=out_specs, check_vma=False)
```

```python
import functools
import math

import jax
import jax.numpy as jnp
from jax import lax
from jax.experimental import pallas as pl
from jax.experimental.pallas import tpu as pltpu
from jax.sharding import PartitionSpec as P

BLOCK = 16
MIB = 2**20


def reversed_bits(value, bits):
    out = 0
    for k in range(bits):
        out = out * 2 + (value >> k & 1)
    return out


def table_rows(rows, shards):
    bits = shards.bit_length() - 3
    dev = rows // shards
    return [
        (reversed_bits(q, bits) * 4 + y * 2 + c) * dev + j
        for c in range(2)
        for y in range(2)
        for q in range(shards // 4)
        for j in range(dev)
    ]


def pick_kernel(step, places, ids_ref, table_ref, *refs):
    *refs, ids, listed, slots, rows, ids_sem, sems = refs
    if places:
        class_ref, heat_ref, *outs, temps_ref, classes, heat, heat_sems = refs
        heat_copies = [
            pltpu.make_async_copy(class_ref, classes, heat_sems.at[0]),
            pltpu.make_async_copy(heat_ref, heat, heat_sems.at[1]),
        ]
    else:
        outs = refs[-2:]
    count = ids_ref.shape[1]
    held = slots.shape[0]
    voc_dev = table_ref.shape[0]
    shards = lax.axis_size("vocab")
    bits = shards.bit_length() - 3
    rows_dev = count // shards
    me = lax.axis_index("vocab")
    offset = me * voc_dev
    low = me % 4
    fetch = pltpu.make_async_copy(ids_ref, ids, ids_sem)
    fetch.start()
    if places:
        for fetched in heat_copies:
            fetched.start()
    rows[...] = jnp.zeros_like(rows)
    fetch.wait()

    def copy(n):
        base = pl.multiple_of(listed[n] // count // BLOCK * BLOCK, BLOCK)
        slot = n % held
        return pltpu.make_async_copy(
            table_ref.at[pl.ds(base, BLOCK)], slots.at[slot], sems.at[slot]
        )

    found = jnp.int32(0)
    for r in range(count):
        local = ids[step, r] - offset
        listed[found] = local * count + r
        found = found + ((local >= 0) & (local < voc_dev)).astype(jnp.int32)

    for first in range(0, count, held):
        last = jnp.minimum(found, first + held)

        @pl.loop(first, last)
        def _(n):
            copy(n).start()

        if places and first == 0:
            for fetched in heat_copies:
                fetched.wait()
            temps = jnp.ones(temps_ref.shape, jnp.float32)
            lane = lax.broadcasted_iota(jnp.int32, temps.shape, 1)
            for place, (at, row) in enumerate(places):
                temps = jnp.where(lane == place, heat[classes[at, row]], temps)
            temps_ref[...] = temps

        @pl.loop(first, last)
        def _(n):
            entry = listed[n]
            r = entry % count
            copy(n).wait()
            block = slots[n % held].astype(jnp.float32)
            sub = lax.broadcasted_iota(jnp.int32, block.shape, 0)
            picked = jnp.sum(
                jnp.where(sub == entry // count % BLOCK, block, 0.0), axis=0, keepdims=True
            )
            owner = r // rows_dev
            way = owner % 4 ^ low
            order = owner // 4 ^ me // 4
            if step == 0:
                order = sum((owner // 4 >> k) % 2 << (bits - 1 - k) for k in range(bits))
            place = (way % 2 * 2 + way // 2) * (shards // 4) + order
            rows[pl.ds(place * rows_dev + r % rows_dev, 1), :] = picked

    half = count // 2
    for part, out in enumerate(outs):
        out[...] = rows[part * half : (part + 1) * half].astype(out.dtype)


def picked_rows(ids, table, step, places, *others):
    count = ids.shape[1]
    width = table.shape[1]
    held = min(count, 32)
    out = (jax.ShapeDtypeStruct((count // 2, width), table.dtype),) * 2
    heat = []
    if places:
        out += (jax.ShapeDtypeStruct((1, len(places)), jnp.float32),)
        others = [in_hbm(other) for other in others]
        heat = [pltpu.SMEM(other.shape, other.dtype) for other in others]
        heat += [pltpu.SemaphoreType.DMA((2,))]
    anywhere, vmem = pl.BlockSpec(memory_space=pl.ANY), pl.BlockSpec(memory_space=pltpu.VMEM)
    return pl.pallas_call(
        functools.partial(pick_kernel, step, places),
        out_shape=out,
        in_specs=[anywhere] * (2 + len(others)),
        out_specs=(vmem,) * len(out),
        scratch_shapes=heat
        + [
            pltpu.SMEM(ids.shape, jnp.int32),
            pltpu.SMEM((count + 1,), jnp.int32),
            pltpu.VMEM((held, BLOCK, width), table.dtype),
            pltpu.VMEM((count, width), jnp.float32),
            pltpu.SemaphoreType.DMA,
            pltpu.SemaphoreType.DMA((held,)),
        ],
        compiler_params=pltpu.CompilerParams(vmem_limit_bytes=16 * MIB),
        name="pick",
    )(in_hbm(ids), in_hbm(table), *others)


def in_hbm(array):
    return pltpu.with_memory_space_constraint(array, pltpu.HBM)


def fold_kernel(keep_ref, got_ref, first_ref, delta_ref, own_ref, send_ref, beside_ref):
    total = keep_ref[...].astype(jnp.float32) + got_ref[...].astype(jnp.float32)
    half = own_ref.shape[0]
    own_ref[...] = total[:half].astype(own_ref.dtype)
    send_ref[...] = total[half:].astype(send_ref.dtype)
    beside_ref[...] = jnp.concatenate(
        [first_ref[...].astype(jnp.float32), delta_ref[...].astype(jnp.float32)], axis=0
    ).astype(beside_ref.dtype)


def folded(keep, got, first, deltas):
    rows, width = keep.shape
    vmem = pl.BlockSpec(memory_space=pltpu.VMEM)
    part = jax.ShapeDtypeStruct((rows // 2, width), keep.dtype)
    return pl.pallas_call(
        fold_kernel,
        out_shape=(part, part, jax.ShapeDtypeStruct((2 * first.shape[0], width), keep.dtype)),
        in_specs=[vmem] * 4,
        out_specs=(vmem,) * 3,
        compiler_params=pltpu.CompilerParams(vmem_limit_bytes=12 * MIB),
        name="fold",
    )(keep, got, first, deltas)


def plus_kernel(own_ref, got_ref, *refs):
    out_ref = refs[-1]
    out_ref[...] = own_ref[...] + got_ref[...]


def join_kernel(own_ref, got_ref, *refs):
    out_ref = refs[-1]
    half = own_ref.shape[0] // 2
    own, got = own_ref[...].astype(jnp.float32), got_ref[...].astype(jnp.float32)
    parts = [own[:half], got[:half], own[half:], got[half:]]
    out_ref[...] = jnp.concatenate(parts, axis=0).astype(out_ref.dtype)


def chips_kernel(own_ref, got_ref, *refs):
    out_ref = refs[-1]
    own, got = own_ref[...], got_ref[...]
    upper = lax.axis_index("vocab") // 2 % 2 == 1
    rows = own.shape[0]
    out_ref[:rows, :] = jnp.where(upper, got, own)
    out_ref[rows:, :] = jnp.where(upper, own, got)


def merge_kernel(own_ref, got_ref, *refs):
    out_ref = refs[-1]
    own, got = own_ref[...], got_ref[...]
    peak = jnp.maximum(own[0:1], got[0:1])
    out_ref[0:1, :] = peak
    out_ref[1:2, :] = own[1:2] * jnp.exp(own[0:1] - peak) + got[1:2] * jnp.exp(got[0:1] - peak)


def paired(kernel, own, got, rows, name, *after):
    vmem = pl.BlockSpec(memory_space=pltpu.VMEM)
    return pl.pallas_call(
        kernel,
        out_shape=jax.ShapeDtypeStruct((rows, own.shape[1]), own.dtype),
        in_specs=[vmem] * 2 + [pl.BlockSpec(memory_space=pl.ANY)] * len(after),
        out_specs=vmem,
        compiler_params=pltpu.CompilerParams(vmem_limit_bytes=12 * MIB),
        name=name,
    )(own, got, *after)


def swapped(rows, bit):
    pairs = [(i, i ^ bit) for i in range(lax.axis_size("vocab"))]
    return lax.ppermute(rows, "vocab", pairs)


def load_kernel(part, table_ref, *refs):
    out_ref, token_ref, sems = refs[-3:]
    copies = part_copies(table_ref, out_ref, sems, table_ref.shape[0] // 2 * part)
    for copy in copies:
        copy.start()
    token_ref[...] = jnp.zeros_like(token_ref)
    for copy in copies:
        copy.wait()


def part_copies(table_ref, out_ref, sems, first):
    parts = sems.shape[0]
    part = table_ref.shape[0] // 2 // parts
    rows = [pl.ds(first + k * part, part) for k in range(parts)]
    return [
        pltpu.make_async_copy(table_ref.at[at], out_ref.at[at], sems.at[k])
        for k, at in enumerate(rows)
    ]


def loaded(table, after, held=None):
    anywhere, vmem = pl.BlockSpec(memory_space=pl.ANY), pl.BlockSpec(memory_space=pltpu.VMEM)
    part = 0 if held is None else 1
    return pl.pallas_call(
        functools.partial(load_kernel, part),
        out_shape=(
            jax.ShapeDtypeStruct(table.shape, table.dtype),
            jax.ShapeDtypeStruct((8, 128), jnp.float32),
        ),
        in_specs=[anywhere] * 2 + [vmem] * part,
        out_specs=(vmem, vmem),
        input_output_aliases={2: 0} if part else {},
        scratch_shapes=[pltpu.SemaphoreType.DMA((4,))],
        compiler_params=pltpu.CompilerParams(vmem_limit_bytes=4 * MIB),
        name="load",
    )(in_hbm(table), after, *([held] if part else []))


def norm_kernel(first_ref, own_ref, got_ref, delta_ref, gain_ref, after_ref, out_ref):
    width = first_ref.shape[1]
    gain = gain_ref[...]

    def rescaled(hidden):
        squares = jnp.mean(hidden * hidden, axis=-1, keepdims=True)
        return hidden * lax.rsqrt(squares + 1e-06) * gain

    me = lax.axis_index("vocab")
    bits = lax.axis_size("vocab").bit_length() - 3

    def in_order(rows):
        for k in range(bits):
            size = rows.shape[0] >> k + 1
            parts = [rows[i * size : (i + 1) * size] for i in range(2 << k)]
            other = [parts[i ^ 1] for i in range(2 << k)]
            rows = jnp.where(
                me // 4 >> k & 1 != 0, jnp.concatenate(other), jnp.concatenate(parts)
            )
        return rows

    one = rescaled(in_order(first_ref[...].astype(jnp.float32)))
    picked = own_ref[...].astype(jnp.float32) + got_ref[...].astype(jnp.float32)
    embedded = (picked * math.sqrt(width)).astype(jnp.bfloat16)
    two = rescaled(
        embedded.astype(jnp.float32) + in_order(delta_ref[...].astype(jnp.float32))
    )
    out_ref[...] = jnp.concatenate([one, two], axis=0).astype(out_ref.dtype)


def normed(first, own, got, delta, gain, after):
    rows, width = first.shape
    vmem = pl.BlockSpec(memory_space=pltpu.VMEM)
    return pl.pallas_call(
        norm_kernel,
        out_shape=jax.ShapeDtypeStruct((2 * rows, width), jnp.bfloat16),
        in_specs=[vmem] * 5 + [pl.BlockSpec(memory_space=pl.ANY)],
        out_specs=vmem,
        compiler_params=pltpu.CompilerParams(vmem_limit_bytes=12 * MIB),
        name="norm",
    )(first, own, got, delta, gain.reshape(1, width), after)


def head_kernel(own_ref, got_ref, table_ref, temps_ref, scaled_ref, stats_ref):
    me = lax.axis_index("vocab")
    dims = (((1,), (1,)), ((), ()))
    own, got = own_ref[...], got_ref[...]
    states = jnp.where(
        me % 2 == 1, jnp.concatenate([got, own], axis=0), jnp.concatenate([own, got], axis=0)
    )
    logits = lax.dot_general(table_ref[...], states, dims, preferred_element_type=jnp.float32)
    scaled = logits / temps_ref[...]
    scaled_ref[...] = scaled
    peak = jnp.max(scaled, axis=0, keepdims=True)
    stats_ref[0:1, :] = peak
    stats_ref[1:2, :] = jnp.sum(jnp.exp(scaled - peak), axis=0, keepdims=True)


def head(own, got, table, temps):
    voc_dev, width = table.shape
    rows = 2 * own.shape[0]
    return pl.pallas_call(
        head_kernel,
        out_shape=(
            jax.ShapeDtypeStruct((voc_dev, rows), jnp.float32),
            jax.ShapeDtypeStruct((2, rows), jnp.float32),
        ),
        in_specs=[pl.BlockSpec(memory_space=pltpu.VMEM)] * 4,
        out_specs=(pl.BlockSpec(memory_space=pltpu.VMEM),) * 2,
        compiler_params=pltpu.CompilerParams(vmem_limit_bytes=30 * MIB),
        name="head",
    )(own, got, table, temps)


def turn_kernel(order, scaled_ref, out_ref):
    turned = scaled_ref[...].T
    for place, (step, row) in enumerate(order):
        out_ref[step, row : row + 1, :] = turned[place : place + 1]


def turned(scaled, order, steps):
    voc_dev, rows = scaled.shape
    return pl.pallas_call(
        functools.partial(turn_kernel, order),
        out_shape=jax.ShapeDtypeStruct((steps, rows // steps, voc_dev), jnp.float32),
        compiler_params=pltpu.CompilerParams(vmem_limit_bytes=12 * MIB),
        name="turn",
    )(scaled)


def finish_kernel(order, scaled_ref, own_ref, got_ref, out_ref):
    own, got = own_ref[...], got_ref[...]
    peak = jnp.maximum(own[0:1], got[0:1])
    total = own[1:2] * jnp.exp(own[0:1] - peak) + got[1:2] * jnp.exp(got[0:1] - peak)
    both = jnp.concatenate([peak, jnp.log(total)], axis=0)
    rows = both.shape[1]
    spread = jnp.broadcast_to(both[:, None, :], (2, 128, rows))
    peak, log = spread[0].T, spread[1].T
    voc_dev = out_ref.shape[2]
    peak = jnp.concatenate([peak] * (voc_dev // 128), axis=1)
    log = jnp.concatenate([log] * (voc_dev // 128), axis=1)
    for place, (step, row) in enumerate(order):
        at = slice(place, place + 1)
        out_ref[step, row : row + 1, :] = scaled_ref[step, row : row + 1, :] - peak[at] - log[at]


def finished(scaled, own, got, order):
    return pl.pallas_call(
        functools.partial(finish_kernel, order),
        out_shape=jax.ShapeDtypeStruct(scaled.shape, jnp.float32),
        compiler_params=pltpu.CompilerParams(vmem_limit_bytes=12 * MIB),
        name="finish",
    )(scaled, own, got)


def merged(own, got):
    peak = jnp.maximum(own[0], got[0])
    total = own[1] * jnp.exp(own[0] - peak) + got[1] * jnp.exp(got[0] - peak)
    return jnp.stack([peak, total])


def body(first, deltas, gain, table, lookup, classes, ids):
    shards = lax.axis_size("vocab")
    rows_dev, width = first.shape
    steps, rows = ids.shape
    quarter = rows // 4
    high = [1 << k for k in range(shards.bit_length() - 2, 1, -1)]

    order = table_rows(rows, shards)
    places = [
        (step, order[pair * quarter + k])
        for pair in range(4)
        for step in range(steps)
        for k in range(quarter)
    ]

    keep, send, temps = picked_rows(ids, table, 0, places, classes, lookup)
    own, send, beside = folded(keep, swapped(send, 1), first, deltas)
    own = own + swapped(send, 2)
    keep, send = picked_rows(ids, table, 1, (), own)
    keep = keep + swapped(send, 1)
    for k, bit in enumerate(high):
        held = beside.shape[0] // 2
        moved = swapped(beside, bit)
        got = swapped(own, bit)
        if k < len(high) - 1:
            beside = paired(join_kernel, beside, moved, 4 * held, "join", own)
            own = paired(plus_kernel, own, got, quarter, "plus", send)
    state = jnp.concatenate([beside[:held], moved[:held]], axis=0)
    delta = jnp.concatenate([beside[held:], moved[held:]], axis=0)
    head_table, token = loaded(table, own)
    states = normed(state, own, got, delta, gain, token)
    head_table, token = loaded(table, states, head_table)
    states = paired(chips_kernel, states, swapped(states, 2), rows, "chips", token, keep)
    others = swapped(states, 1)
    scaled, stats = head(states, others, head_table, temps)
    scaled = turned(scaled, places, steps)
    following = paired(plus_kernel, keep[:quarter], swapped(keep[quarter:], 2), quarter, "plus", stats)
    if len(high) < 3:
        parts = [following[k * rows_dev : (k + 1) * rows_dev] for k in range(shards // 4)]
        following = sum((swapped(parts[k], 4 * k) for k in range(1, shards // 4)), parts[0])
    for bit in high:
        if following.shape[0] > rows_dev:
            half = following.shape[0] // 2
            following = following[:half] + swapped(following[half:], bit)
        stats = merged(stats, swapped(stats, bit))
    embedded = (following.astype(jnp.float32) * math.sqrt(width)).astype(jnp.bfloat16)
    stats = paired(merge_kernel, stats, swapped(stats, 2), 2, "merge", following)
    logprobs = finished(scaled, stats, swapped(stats, 1), places)
    return logprobs, embedded


def solution(mesh):
    in_specs = (
        P(("groups", "vocab"), None),
        P(("groups", "vocab"), None),
        P(),
        P("vocab", None),
        P(),
        P(None, "groups"),
        P(None, "groups"),
    )
    out_specs = (P(None, "groups", "vocab"), P(("groups", "vocab"), None))
    return jax.shard_map(body, mesh=mesh, in_specs=in_specs, out_specs=out_specs, check_vma=False)
```

```python
import functools
import math

import jax
import jax.numpy as jnp
from jax import lax
from jax.experimental import pallas as pl
from jax.experimental.pallas import tpu as pltpu
from jax.sharding import PartitionSpec as P

BLOCK = 16
MIB = 2**20


def reversed_bits(value, bits):
    out = 0
    for k in range(bits):
        out = out * 2 + (value >> k & 1)
    return out


def table_rows(rows, shards):
    bits = shards.bit_length() - 3
    dev = rows // shards
    return [
        (reversed_bits(q, bits) * 4 + y * 2 + c) * dev + j
        for c in range(2)
        for y in range(2)
        for q in range(shards // 4)
        for j in range(dev)
    ]


def pick_kernel(step, places, ids_ref, table_ref, *refs):
    *refs, ids, listed, slots, rows, ids_sem, sems = refs
    if places:
        class_ref, heat_ref, *outs, temps_ref, classes, heat, heat_sems = refs
        heat_copies = [
            pltpu.make_async_copy(class_ref, classes, heat_sems.at[0]),
            pltpu.make_async_copy(heat_ref, heat, heat_sems.at[1]),
        ]
    else:
        outs = refs[-2:]
    count = ids_ref.shape[1]
    held = slots.shape[0]
    voc_dev = table_ref.shape[0]
    shards = lax.axis_size("vocab")
    bits = shards.bit_length() - 3
    rows_dev = count // shards
    me = lax.axis_index("vocab")
    offset = me * voc_dev
    low = me % 4
    fetch = pltpu.make_async_copy(ids_ref, ids, ids_sem)
    fetch.start()
    if places:
        for fetched in heat_copies:
            fetched.start()
    rows[...] = jnp.zeros_like(rows)
    fetch.wait()

    def copy(n):
        base = pl.multiple_of(listed[n] // count // BLOCK * BLOCK, BLOCK)
        slot = n % held
        return pltpu.make_async_copy(
            table_ref.at[pl.ds(base, BLOCK)], slots.at[slot], sems.at[slot]
        )

    found = jnp.int32(0)
    for r in range(count):
        local = ids[step, r] - offset
        listed[found] = local * count + r
        found = found + ((local >= 0) & (local < voc_dev)).astype(jnp.int32)

    for first in range(0, count, held):
        last = jnp.minimum(found, first + held)

        @pl.loop(first, last)
        def _(n):
            copy(n).start()

        if places and first == 0:
            for fetched in heat_copies:
                fetched.wait()
            temps = jnp.ones(temps_ref.shape, jnp.float32)
            lane = lax.broadcasted_iota(jnp.int32, temps.shape, 1)
            for place, (at, row) in enumerate(places):
                temps = jnp.where(lane == place, heat[classes[at, row]], temps)
            temps_ref[...] = temps

        @pl.loop(first, last)
        def _(n):
            entry = listed[n]
            r = entry % count
            copy(n).wait()
            block = slots[n % held].astype(jnp.float32)
            sub = lax.broadcasted_iota(jnp.int32, block.shape, 0)
            picked = jnp.sum(
                jnp.where(sub == entry // count % BLOCK, block, 0.0), axis=0, keepdims=True
            )
            owner = r // rows_dev
            way = owner % 4 ^ low
            order = owner // 4 ^ me // 4
            if step == 0:
                order = sum((owner // 4 >> k) % 2 << (bits - 1 - k) for k in range(bits))
            place = (way % 2 * 2 + way // 2) * (shards // 4) + order
            rows[pl.ds(place * rows_dev + r % rows_dev, 1), :] = picked

    half = count // 2
    for part, out in enumerate(outs):
        out[...] = rows[part * half : (part + 1) * half].astype(out.dtype)


def picked_rows(ids, table, step, places, *others):
    count = ids.shape[1]
    width = table.shape[1]
    held = min(count, 32)
    out = (jax.ShapeDtypeStruct((count // 2, width), table.dtype),) * 2
    heat = []
    if places:
        out += (jax.ShapeDtypeStruct((1, len(places)), jnp.float32),)
        others = [in_hbm(other) for other in others]
        heat = [pltpu.SMEM(other.shape, other.dtype) for other in others]
        heat += [pltpu.SemaphoreType.DMA((2,))]
    anywhere, vmem = pl.BlockSpec(memory_space=pl.ANY), pl.BlockSpec(memory_space=pltpu.VMEM)
    return pl.pallas_call(
        functools.partial(pick_kernel, step, places),
        out_shape=out,
        in_specs=[anywhere] * (2 + len(others)),
        out_specs=(vmem,) * len(out),
        scratch_shapes=heat
        + [
            pltpu.SMEM(ids.shape, jnp.int32),
            pltpu.SMEM((count + 1,), jnp.int32),
            pltpu.VMEM((held, BLOCK, width), table.dtype),
            pltpu.VMEM((count, width), jnp.float32),
            pltpu.SemaphoreType.DMA,
            pltpu.SemaphoreType.DMA((held,)),
        ],
        compiler_params=pltpu.CompilerParams(vmem_limit_bytes=16 * MIB),
        name="pick",
    )(in_hbm(ids), in_hbm(table), *others)


def in_hbm(array):
    return pltpu.with_memory_space_constraint(array, pltpu.HBM)


def fold_kernel(keep_ref, got_ref, first_ref, delta_ref, own_ref, send_ref, beside_ref):
    total = keep_ref[...].astype(jnp.float32) + got_ref[...].astype(jnp.float32)
    half = own_ref.shape[0]
    own_ref[...] = total[:half].astype(own_ref.dtype)
    send_ref[...] = total[half:].astype(send_ref.dtype)
    beside_ref[...] = jnp.concatenate(
        [first_ref[...].astype(jnp.float32), delta_ref[...].astype(jnp.float32)], axis=0
    ).astype(beside_ref.dtype)


def folded(keep, got, first, deltas):
    rows, width = keep.shape
    vmem = pl.BlockSpec(memory_space=pltpu.VMEM)
    part = jax.ShapeDtypeStruct((rows // 2, width), keep.dtype)
    return pl.pallas_call(
        fold_kernel,
        out_shape=(part, part, jax.ShapeDtypeStruct((2 * first.shape[0], width), keep.dtype)),
        in_specs=[vmem] * 4,
        out_specs=(vmem,) * 3,
        compiler_params=pltpu.CompilerParams(vmem_limit_bytes=12 * MIB),
        name="fold",
    )(keep, got, first, deltas)


def plus_kernel(own_ref, got_ref, *refs):
    out_ref = refs[-1]
    out_ref[...] = own_ref[...] + got_ref[...]


def join_kernel(own_ref, got_ref, *refs):
    out_ref = refs[-1]
    half = own_ref.shape[0] // 2
    own, got = own_ref[...].astype(jnp.float32), got_ref[...].astype(jnp.float32)
    parts = [own[:half], got[:half], own[half:], got[half:]]
    out_ref[...] = jnp.concatenate(parts, axis=0).astype(out_ref.dtype)


def chips_kernel(own_ref, got_ref, *refs):
    out_ref = refs[-1]
    own, got = own_ref[...], got_ref[...]
    upper = lax.axis_index("vocab") // 2 % 2 == 1
    rows = own.shape[0]
    out_ref[:rows, :] = jnp.where(upper, got, own)
    out_ref[rows:, :] = jnp.where(upper, own, got)


def merge_kernel(own_ref, got_ref, *refs):
    out_ref = refs[-1]
    own, got = own_ref[...], got_ref[...]
    peak = jnp.maximum(own[0:1], got[0:1])
    out_ref[0:1, :] = peak
    out_ref[1:2, :] = own[1:2] * jnp.exp(own[0:1] - peak) + got[1:2] * jnp.exp(got[0:1] - peak)


def paired(kernel, own, got, rows, name, *after):
    vmem = pl.BlockSpec(memory_space=pltpu.VMEM)
    return pl.pallas_call(
        kernel,
        out_shape=jax.ShapeDtypeStruct((rows, own.shape[1]), own.dtype),
        in_specs=[vmem] * 2 + [pl.BlockSpec(memory_space=pl.ANY)] * len(after),
        out_specs=vmem,
        compiler_params=pltpu.CompilerParams(vmem_limit_bytes=12 * MIB),
        name=name,
    )(own, got, *after)


def swapped(rows, bit):
    pairs = [(i, i ^ bit) for i in range(lax.axis_size("vocab"))]
    return lax.ppermute(rows, "vocab", pairs)


def load_kernel(part, table_ref, *refs):
    out_ref, token_ref, sems = refs[-3:]
    copies = part_copies(table_ref, out_ref, sems, table_ref.shape[0] // 2 * part)
    for copy in copies:
        copy.start()
    token_ref[...] = jnp.zeros_like(token_ref)
    for copy in copies:
        copy.wait()


def part_copies(table_ref, out_ref, sems, first):
    parts = sems.shape[0]
    part = table_ref.shape[0] // 2 // parts
    rows = [pl.ds(first + k * part, part) for k in range(parts)]
    return [
        pltpu.make_async_copy(table_ref.at[at], out_ref.at[at], sems.at[k])
        for k, at in enumerate(rows)
    ]


def loaded(table, after, held=None):
    anywhere, vmem = pl.BlockSpec(memory_space=pl.ANY), pl.BlockSpec(memory_space=pltpu.VMEM)
    part = 0 if held is None else 1
    return pl.pallas_call(
        functools.partial(load_kernel, part),
        out_shape=(
            jax.ShapeDtypeStruct(table.shape, table.dtype),
            jax.ShapeDtypeStruct((8, 128), jnp.float32),
        ),
        in_specs=[anywhere] * 2 + [vmem] * part,
        out_specs=(vmem, vmem),
        input_output_aliases={2: 0} if part else {},
        scratch_shapes=[pltpu.SemaphoreType.DMA((4,))],
        compiler_params=pltpu.CompilerParams(vmem_limit_bytes=4 * MIB),
        name="load",
    )(in_hbm(table), after, *([held] if part else []))


def norm_kernel(first_ref, own_ref, got_ref, delta_ref, gain_ref, *refs):
    out_ref = refs[-1]
    width = first_ref.shape[1]
    gain = gain_ref[...]

    def rescaled(hidden):
        squares = jnp.mean(hidden * hidden, axis=-1, keepdims=True)
        return hidden * lax.rsqrt(squares + 1e-06) * gain

    me = lax.axis_index("vocab")
    bits = lax.axis_size("vocab").bit_length() - 3

    def in_order(rows):
        for k in range(bits):
            size = rows.shape[0] >> k + 1
            parts = [rows[i * size : (i + 1) * size] for i in range(2 << k)]
            other = [parts[i ^ 1] for i in range(2 << k)]
            rows = jnp.where(
                me // 4 >> k & 1 != 0, jnp.concatenate(other), jnp.concatenate(parts)
            )
        return rows

    one = rescaled(in_order(first_ref[...].astype(jnp.float32)))
    picked = own_ref[...].astype(jnp.float32) + got_ref[...].astype(jnp.float32)
    embedded = (picked * math.sqrt(width)).astype(jnp.bfloat16)
    two = rescaled(
        embedded.astype(jnp.float32) + in_order(delta_ref[...].astype(jnp.float32))
    )
    out_ref[...] = jnp.concatenate([one, two], axis=0).astype(out_ref.dtype)


def normed(first, own, got, delta, gain, *after):
    rows, width = first.shape
    vmem = pl.BlockSpec(memory_space=pltpu.VMEM)
    return pl.pallas_call(
        norm_kernel,
        out_shape=jax.ShapeDtypeStruct((2 * rows, width), jnp.bfloat16),
        in_specs=[vmem] * 5 + [pl.BlockSpec(memory_space=pl.ANY)] * len(after),
        out_specs=vmem,
        compiler_params=pltpu.CompilerParams(vmem_limit_bytes=12 * MIB),
        name="norm",
    )(first, own, got, delta, gain.reshape(1, width), *after)


def head_kernel(own_ref, got_ref, table_ref, temps_ref, scaled_ref, stats_ref):
    me = lax.axis_index("vocab")
    dims = (((1,), (1,)), ((), ()))
    own, got = own_ref[...], got_ref[...]
    states = jnp.where(
        me % 2 == 1, jnp.concatenate([got, own], axis=0), jnp.concatenate([own, got], axis=0)
    )
    logits = lax.dot_general(table_ref[...], states, dims, preferred_element_type=jnp.float32)
    scaled = logits / temps_ref[...]
    scaled_ref[...] = scaled
    peak = jnp.max(scaled, axis=0, keepdims=True)
    stats_ref[0:1, :] = peak
    stats_ref[1:2, :] = jnp.sum(jnp.exp(scaled - peak), axis=0, keepdims=True)


def head(own, got, table, temps):
    voc_dev, width = table.shape
    rows = 2 * own.shape[0]
    return pl.pallas_call(
        head_kernel,
        out_shape=(
            jax.ShapeDtypeStruct((voc_dev, rows), jnp.float32),
            jax.ShapeDtypeStruct((2, rows), jnp.float32),
        ),
        in_specs=[pl.BlockSpec(memory_space=pltpu.VMEM)] * 4,
        out_specs=(pl.BlockSpec(memory_space=pltpu.VMEM),) * 2,
        compiler_params=pltpu.CompilerParams(vmem_limit_bytes=30 * MIB),
        name="head",
    )(own, got, table, temps)


def turn_kernel(order, scaled_ref, out_ref):
    turned = scaled_ref[...].T
    for place, (step, row) in enumerate(order):
        out_ref[step, row : row + 1, :] = turned[place : place + 1]


def turned(scaled, order, steps):
    voc_dev, rows = scaled.shape
    return pl.pallas_call(
        functools.partial(turn_kernel, order),
        out_shape=jax.ShapeDtypeStruct((steps, rows // steps, voc_dev), jnp.float32),
        compiler_params=pltpu.CompilerParams(vmem_limit_bytes=12 * MIB),
        name="turn",
    )(scaled)


def finish_kernel(order, scaled_ref, own_ref, got_ref, out_ref):
    own, got = own_ref[...], got_ref[...]
    peak = jnp.maximum(own[0:1], got[0:1])
    total = own[1:2] * jnp.exp(own[0:1] - peak) + got[1:2] * jnp.exp(got[0:1] - peak)
    both = jnp.concatenate([peak, jnp.log(total)], axis=0)
    rows = both.shape[1]
    spread = jnp.broadcast_to(both[:, None, :], (2, 128, rows))
    peak, log = spread[0].T, spread[1].T
    voc_dev = out_ref.shape[2]
    peak = jnp.concatenate([peak] * (voc_dev // 128), axis=1)
    log = jnp.concatenate([log] * (voc_dev // 128), axis=1)
    for place, (step, row) in enumerate(order):
        at = slice(place, place + 1)
        out_ref[step, row : row + 1, :] = scaled_ref[step, row : row + 1, :] - peak[at] - log[at]


def finished(scaled, own, got, order):
    return pl.pallas_call(
        functools.partial(finish_kernel, order),
        out_shape=jax.ShapeDtypeStruct(scaled.shape, jnp.float32),
        compiler_params=pltpu.CompilerParams(vmem_limit_bytes=12 * MIB),
        name="finish",
    )(scaled, own, got)


def merged(own, got):
    peak = jnp.maximum(own[0], got[0])
    total = own[1] * jnp.exp(own[0] - peak) + got[1] * jnp.exp(got[0] - peak)
    return jnp.stack([peak, total])


def body(first, deltas, gain, table, lookup, classes, ids):
    shards = lax.axis_size("vocab")
    rows_dev, width = first.shape
    steps, rows = ids.shape
    quarter = rows // 4
    high = [1 << k for k in range(shards.bit_length() - 2, 1, -1)]

    order = table_rows(rows, shards)
    places = [
        (step, order[pair * quarter + k])
        for pair in range(4)
        for step in range(steps)
        for k in range(quarter)
    ]

    keep, send, temps = picked_rows(ids, table, 0, places, classes, lookup)
    own, send, beside = folded(keep, swapped(send, 1), first, deltas)
    own = own + swapped(send, 2)
    keep, send = picked_rows(ids, table, 1, (), own)
    keep = keep + swapped(send, 1)
    following = keep[:quarter] + swapped(keep[quarter:], 2)
    for k, bit in enumerate(high):
        held = beside.shape[0] // 2
        moved = swapped(beside, bit)
        got = swapped(own, bit)
        if k < len(high) - 1:
            beside = paired(join_kernel, beside, moved, 4 * held, "join", own)
            own = paired(plus_kernel, own, got, quarter, "plus", send)
    state = jnp.concatenate([beside[:held], moved[:held]], axis=0)
    delta = jnp.concatenate([beside[held:], moved[held:]], axis=0)
    head_table, token = loaded(table, own)
    states = normed(state, own, got, delta, gain, token, following)
    head_table, token = loaded(table, states, head_table)
    states = paired(chips_kernel, states, swapped(states, 2), rows, "chips", token)
    others = swapped(states, 1)
    scaled, stats = head(states, others, head_table, temps)
    scaled = turned(scaled, places, steps)
    for bit in high:
        half = following.shape[0] // 2
        following = following[:half] + swapped(following[half:], bit)
    embedded = (following.astype(jnp.float32) * math.sqrt(width)).astype(jnp.bfloat16)
    for bit in high[:-1]:
        stats = merged(stats, swapped(stats, bit))
    stats = paired(merge_kernel, stats, swapped(stats, high[-1]), 2, "merge", following)
    stats = merged(stats, swapped(stats, 2))
    logprobs = finished(scaled, stats, swapped(stats, 1), places)
    return logprobs, embedded


def solution(mesh):
    in_specs = (
        P(("groups", "vocab"), None),
        P(("groups", "vocab"), None),
        P(),
        P("vocab", None),
        P(),
        P(None, "groups"),
        P(None, "groups"),
    )
    out_specs = (P(None, "groups", "vocab"), P(("groups", "vocab"), None))
    return jax.shard_map(body, mesh=mesh, in_specs=in_specs, out_specs=out_specs, check_vma=False)
```

```python
import functools
import math

import jax
import jax.numpy as jnp
from jax import lax
from jax.experimental import pallas as pl
from jax.experimental.pallas import tpu as pltpu
from jax.sharding import PartitionSpec as P

BLOCK = 16
MIB = 2**20


def reversed_bits(value, bits):
    out = 0
    for k in range(bits):
        out = out * 2 + (value >> k & 1)
    return out


def table_rows(rows, shards):
    bits = shards.bit_length() - 3
    dev = rows // shards
    return [
        (reversed_bits(q, bits) * 4 + y * 2 + c) * dev + j
        for c in range(2)
        for y in range(2)
        for q in range(shards // 4)
        for j in range(dev)
    ]


def pick_kernel(step, places, ids_ref, table_ref, *refs):
    *refs, ids, listed, slots, rows, ids_sem, sems = refs
    if places:
        class_ref, heat_ref, *outs, temps_ref, classes, heat, heat_sems = refs
        heat_copies = [
            pltpu.make_async_copy(class_ref, classes, heat_sems.at[0]),
            pltpu.make_async_copy(heat_ref, heat, heat_sems.at[1]),
        ]
    else:
        after_ref, *outs, head_ref, head_sems = refs
        head_copies = part_copies(table_ref, head_ref, head_sems, 0)
    count = ids_ref.shape[1]
    held = slots.shape[0]
    voc_dev = table_ref.shape[0]
    shards = lax.axis_size("vocab")
    bits = shards.bit_length() - 3
    rows_dev = count // shards
    me = lax.axis_index("vocab")
    offset = me * voc_dev
    low = me % 4
    fetch = pltpu.make_async_copy(ids_ref, ids, ids_sem)
    fetch.start()
    if places:
        for fetched in heat_copies:
            fetched.start()
    rows[...] = jnp.zeros_like(rows)
    fetch.wait()

    def copy(n):
        base = pl.multiple_of(listed[n] // count // BLOCK * BLOCK, BLOCK)
        slot = n % held
        return pltpu.make_async_copy(
            table_ref.at[pl.ds(base, BLOCK)], slots.at[slot], sems.at[slot]
        )

    found = jnp.int32(0)
    for r in range(count):
        local = ids[step, r] - offset
        listed[found] = local * count + r
        found = found + ((local >= 0) & (local < voc_dev)).astype(jnp.int32)

    for first in range(0, count, held):
        last = jnp.minimum(found, first + held)

        @pl.loop(first, last)
        def _(n):
            copy(n).start()

        if not places and first == 0:
            for part in head_copies:
                part.start()
        if places and first == 0:
            for fetched in heat_copies:
                fetched.wait()
            temps = jnp.ones(temps_ref.shape, jnp.float32)
            lane = lax.broadcasted_iota(jnp.int32, temps.shape, 1)
            for place, (at, row) in enumerate(places):
                temps = jnp.where(lane == place, heat[classes[at, row]], temps)
            temps_ref[...] = temps

        @pl.loop(first, last)
        def _(n):
            entry = listed[n]
            r = entry % count
            copy(n).wait()
            block = slots[n % held].astype(jnp.float32)
            sub = lax.broadcasted_iota(jnp.int32, block.shape, 0)
            picked = jnp.sum(
                jnp.where(sub == entry // count % BLOCK, block, 0.0), axis=0, keepdims=True
            )
            owner = r // rows_dev
            way = owner % 4 ^ low
            order = owner // 4 ^ me // 4
            if step == 0:
                order = sum((owner // 4 >> k) % 2 << (bits - 1 - k) for k in range(bits))
            place = (way % 2 * 2 + way // 2) * (shards // 4) + order
            rows[pl.ds(place * rows_dev + r % rows_dev, 1), :] = picked

    half = count // 2
    for part, out in enumerate(outs):
        out[...] = rows[part * half : (part + 1) * half].astype(out.dtype)
    if not places:
        for part in head_copies:
            part.wait()


def picked_rows(ids, table, step, places, *others):
    count = ids.shape[1]
    width = table.shape[1]
    held = min(count, 32)
    out = (jax.ShapeDtypeStruct((count // 2, width), table.dtype),) * 2
    heat = []
    if places:
        out += (jax.ShapeDtypeStruct((1, len(places)), jnp.float32),)
        others = [in_hbm(other) for other in others]
        heat = [pltpu.SMEM(other.shape, other.dtype) for other in others]
        heat += [pltpu.SemaphoreType.DMA((2,))]
    else:
        out += (jax.ShapeDtypeStruct(table.shape, table.dtype),)
        heat = [pltpu.SemaphoreType.DMA((4,))]
    anywhere, vmem = pl.BlockSpec(memory_space=pl.ANY), pl.BlockSpec(memory_space=pltpu.VMEM)
    return pl.pallas_call(
        functools.partial(pick_kernel, step, places),
        out_shape=out,
        in_specs=[anywhere] * (2 + len(others)),
        out_specs=(vmem,) * len(out),
        scratch_shapes=heat
        + [
            pltpu.SMEM(ids.shape, jnp.int32),
            pltpu.SMEM((count + 1,), jnp.int32),
            pltpu.VMEM((held, BLOCK, width), table.dtype),
            pltpu.VMEM((count, width), jnp.float32),
            pltpu.SemaphoreType.DMA,
            pltpu.SemaphoreType.DMA((held,)),
        ],
        compiler_params=pltpu.CompilerParams(vmem_limit_bytes=16 * MIB),
        name="pick",
    )(in_hbm(ids), in_hbm(table), *others)


def in_hbm(array):
    return pltpu.with_memory_space_constraint(array, pltpu.HBM)


def fold_kernel(keep_ref, got_ref, first_ref, delta_ref, own_ref, send_ref, beside_ref):
    total = keep_ref[...].astype(jnp.float32) + got_ref[...].astype(jnp.float32)
    half = own_ref.shape[0]
    own_ref[...] = total[:half].astype(own_ref.dtype)
    send_ref[...] = total[half:].astype(send_ref.dtype)
    beside_ref[...] = jnp.concatenate(
        [first_ref[...].astype(jnp.float32), delta_ref[...].astype(jnp.float32)], axis=0
    ).astype(beside_ref.dtype)


def folded(keep, got, first, deltas):
    rows, width = keep.shape
    vmem = pl.BlockSpec(memory_space=pltpu.VMEM)
    part = jax.ShapeDtypeStruct((rows // 2, width), keep.dtype)
    return pl.pallas_call(
        fold_kernel,
        out_shape=(part, part, jax.ShapeDtypeStruct((2 * first.shape[0], width), keep.dtype)),
        in_specs=[vmem] * 4,
        out_specs=(vmem,) * 3,
        compiler_params=pltpu.CompilerParams(vmem_limit_bytes=12 * MIB),
        name="fold",
    )(keep, got, first, deltas)


def plus_kernel(own_ref, got_ref, *refs):
    out_ref = refs[-1]
    out_ref[...] = own_ref[...] + got_ref[...]


def join_kernel(own_ref, got_ref, *refs):
    out_ref = refs[-1]
    half = own_ref.shape[0] // 2
    own, got = own_ref[...].astype(jnp.float32), got_ref[...].astype(jnp.float32)
    parts = [own[:half], got[:half], own[half:], got[half:]]
    out_ref[...] = jnp.concatenate(parts, axis=0).astype(out_ref.dtype)


def chips_kernel(own_ref, got_ref, *refs):
    out_ref = refs[-1]
    own, got = own_ref[...], got_ref[...]
    upper = lax.axis_index("vocab") // 2 % 2 == 1
    rows = own.shape[0]
    out_ref[:rows, :] = jnp.where(upper, got, own)
    out_ref[rows:, :] = jnp.where(upper, own, got)


def merge_kernel(own_ref, got_ref, *refs):
    out_ref = refs[-1]
    own, got = own_ref[...], got_ref[...]
    peak = jnp.maximum(own[0:1], got[0:1])
    out_ref[0:1, :] = peak
    out_ref[1:2, :] = own[1:2] * jnp.exp(own[0:1] - peak) + got[1:2] * jnp.exp(got[0:1] - peak)


def paired(kernel, own, got, rows, name, *after):
    vmem = pl.BlockSpec(memory_space=pltpu.VMEM)
    return pl.pallas_call(
        kernel,
        out_shape=jax.ShapeDtypeStruct((rows, own.shape[1]), own.dtype),
        in_specs=[vmem] * 2 + [pl.BlockSpec(memory_space=pl.ANY)] * len(after),
        out_specs=vmem,
        compiler_params=pltpu.CompilerParams(vmem_limit_bytes=12 * MIB),
        name=name,
    )(own, got, *after)


def swapped(rows, bit):
    pairs = [(i, i ^ bit) for i in range(lax.axis_size("vocab"))]
    return lax.ppermute(rows, "vocab", pairs)


def load_kernel(table_ref, after_ref, held_ref, out_ref, token_ref, sems):
    copies = part_copies(table_ref, out_ref, sems, table_ref.shape[0] // 2)
    for copy in copies:
        copy.start()
    token_ref[...] = jnp.zeros_like(token_ref)
    for copy in copies:
        copy.wait()


def part_copies(table_ref, out_ref, sems, first):
    parts = sems.shape[0]
    part = table_ref.shape[0] // 2 // parts
    rows = [pl.ds(first + k * part, part) for k in range(parts)]
    return [
        pltpu.make_async_copy(table_ref.at[at], out_ref.at[at], sems.at[k])
        for k, at in enumerate(rows)
    ]


def loaded(table, held, after):
    anywhere, vmem = pl.BlockSpec(memory_space=pl.ANY), pl.BlockSpec(memory_space=pltpu.VMEM)
    return pl.pallas_call(
        load_kernel,
        out_shape=(
            jax.ShapeDtypeStruct(table.shape, table.dtype),
            jax.ShapeDtypeStruct((8, 128), jnp.float32),
        ),
        in_specs=[anywhere, anywhere, vmem],
        out_specs=(vmem, vmem),
        input_output_aliases={2: 0},
        scratch_shapes=[pltpu.SemaphoreType.DMA((4,))],
        compiler_params=pltpu.CompilerParams(vmem_limit_bytes=4 * MIB),
        name="load",
    )(in_hbm(table), after, held)


def norm_kernel(first_ref, own_ref, got_ref, delta_ref, gain_ref, *refs):
    out_ref = refs[-1]
    width = first_ref.shape[1]
    gain = gain_ref[...]

    def rescaled(hidden):
        squares = jnp.mean(hidden * hidden, axis=-1, keepdims=True)
        return hidden * lax.rsqrt(squares + 1e-06) * gain

    me = lax.axis_index("vocab")
    bits = lax.axis_size("vocab").bit_length() - 3

    def in_order(rows):
        for k in range(bits):
            size = rows.shape[0] >> k + 1
            parts = [rows[i * size : (i + 1) * size] for i in range(2 << k)]
            other = [parts[i ^ 1] for i in range(2 << k)]
            rows = jnp.where(
                me // 4 >> k & 1 != 0, jnp.concatenate(other), jnp.concatenate(parts)
            )
        return rows

    one = rescaled(in_order(first_ref[...].astype(jnp.float32)))
    picked = own_ref[...].astype(jnp.float32) + got_ref[...].astype(jnp.float32)
    embedded = (picked * math.sqrt(width)).astype(jnp.bfloat16)
    two = rescaled(
        embedded.astype(jnp.float32) + in_order(delta_ref[...].astype(jnp.float32))
    )
    out_ref[...] = jnp.concatenate([one, two], axis=0).astype(out_ref.dtype)


def normed(first, own, got, delta, gain, *after):
    rows, width = first.shape
    vmem = pl.BlockSpec(memory_space=pltpu.VMEM)
    return pl.pallas_call(
        norm_kernel,
        out_shape=jax.ShapeDtypeStruct((2 * rows, width), jnp.bfloat16),
        in_specs=[vmem] * 5 + [pl.BlockSpec(memory_space=pl.ANY)] * len(after),
        out_specs=vmem,
        compiler_params=pltpu.CompilerParams(vmem_limit_bytes=12 * MIB),
        name="norm",
    )(first, own, got, delta, gain.reshape(1, width), *after)


def head_kernel(own_ref, got_ref, table_ref, temps_ref, scaled_ref, stats_ref):
    me = lax.axis_index("vocab")
    dims = (((1,), (1,)), ((), ()))
    own, got = own_ref[...], got_ref[...]
    states = jnp.where(
        me % 2 == 1, jnp.concatenate([got, own], axis=0), jnp.concatenate([own, got], axis=0)
    )
    logits = lax.dot_general(table_ref[...], states, dims, preferred_element_type=jnp.float32)
    scaled = logits / temps_ref[...]
    scaled_ref[...] = scaled
    peak = jnp.max(scaled, axis=0, keepdims=True)
    stats_ref[0:1, :] = peak
    stats_ref[1:2, :] = jnp.sum(jnp.exp(scaled - peak), axis=0, keepdims=True)


def head(own, got, table, temps):
    voc_dev, width = table.shape
    rows = 2 * own.shape[0]
    return pl.pallas_call(
        head_kernel,
        out_shape=(
            jax.ShapeDtypeStruct((voc_dev, rows), jnp.float32),
            jax.ShapeDtypeStruct((2, rows), jnp.float32),
        ),
        in_specs=[pl.BlockSpec(memory_space=pltpu.VMEM)] * 4,
        out_specs=(pl.BlockSpec(memory_space=pltpu.VMEM),) * 2,
        compiler_params=pltpu.CompilerParams(vmem_limit_bytes=30 * MIB),
        name="head",
    )(own, got, table, temps)


def turn_kernel(order, scaled_ref, out_ref):
    turned = scaled_ref[...].T
    for place, (step, row) in enumerate(order):
        out_ref[step, row : row + 1, :] = turned[place : place + 1]


def turned(scaled, order, steps):
    voc_dev, rows = scaled.shape
    return pl.pallas_call(
        functools.partial(turn_kernel, order),
        out_shape=jax.ShapeDtypeStruct((steps, rows // steps, voc_dev), jnp.float32),
        compiler_params=pltpu.CompilerParams(vmem_limit_bytes=12 * MIB),
        name="turn",
    )(scaled)


def finish_kernel(order, scaled_ref, own_ref, got_ref, out_ref):
    own, got = own_ref[...], got_ref[...]
    peak = jnp.maximum(own[0:1], got[0:1])
    total = own[1:2] * jnp.exp(own[0:1] - peak) + got[1:2] * jnp.exp(got[0:1] - peak)
    both = jnp.concatenate([peak, jnp.log(total)], axis=0)
    rows = both.shape[1]
    spread = jnp.broadcast_to(both[:, None, :], (2, 128, rows))
    peak, log = spread[0].T, spread[1].T
    voc_dev = out_ref.shape[2]
    peak = jnp.concatenate([peak] * (voc_dev // 128), axis=1)
    log = jnp.concatenate([log] * (voc_dev // 128), axis=1)
    for place, (step, row) in enumerate(order):
        at = slice(place, place + 1)
        out_ref[step, row : row + 1, :] = scaled_ref[step, row : row + 1, :] - peak[at] - log[at]


def finished(scaled, own, got, order):
    return pl.pallas_call(
        functools.partial(finish_kernel, order),
        out_shape=jax.ShapeDtypeStruct(scaled.shape, jnp.float32),
        compiler_params=pltpu.CompilerParams(vmem_limit_bytes=12 * MIB),
        name="finish",
    )(scaled, own, got)


def merged(own, got):
    peak = jnp.maximum(own[0], got[0])
    total = own[1] * jnp.exp(own[0] - peak) + got[1] * jnp.exp(got[0] - peak)
    return jnp.stack([peak, total])


def body(first, deltas, gain, table, lookup, classes, ids):
    shards = lax.axis_size("vocab")
    rows_dev, width = first.shape
    steps, rows = ids.shape
    quarter = rows // 4
    high = [1 << k for k in range(shards.bit_length() - 2, 1, -1)]

    order = table_rows(rows, shards)
    places = [
        (step, order[pair * quarter + k])
        for pair in range(4)
        for step in range(steps)
        for k in range(quarter)
    ]

    keep, send, temps = picked_rows(ids, table, 0, places, classes, lookup)
    own, send, beside = folded(keep, swapped(send, 1), first, deltas)
    own = own + swapped(send, 2)
    keep, send, head_table = picked_rows(ids, table, 1, (), own)
    keep = keep + swapped(send, 1)
    following = keep[:quarter] + swapped(keep[quarter:], 2)
    for k, bit in enumerate(high):
        held = beside.shape[0] // 2
        moved = swapped(beside, bit)
        got = swapped(own, bit)
        if k < len(high) - 1:
            beside = paired(join_kernel, beside, moved, 4 * held, "join", own)
            own = paired(plus_kernel, own, got, quarter, "plus", send)
    state = jnp.concatenate([beside[:held], moved[:held]], axis=0)
    delta = jnp.concatenate([beside[held:], moved[held:]], axis=0)
    states = normed(state, own, got, delta, gain, following)
    head_table, token = loaded(table, head_table, states)
    states = paired(chips_kernel, states, swapped(states, 2), rows, "chips", token)
    others = swapped(states, 1)
    scaled, stats = head(states, others, head_table, temps)
    scaled = turned(scaled, places, steps)
    for bit in high:
        half = following.shape[0] // 2
        following = following[:half] + swapped(following[half:], bit)
    embedded = (following.astype(jnp.float32) * math.sqrt(width)).astype(jnp.bfloat16)
    for bit in high[:-1]:
        stats = merged(stats, swapped(stats, bit))
    stats = paired(merge_kernel, stats, swapped(stats, high[-1]), 2, "merge", following)
    stats = merged(stats, swapped(stats, 2))
    logprobs = finished(scaled, stats, swapped(stats, 1), places)
    return logprobs, embedded


def solution(mesh):
    in_specs = (
        P(("groups", "vocab"), None),
        P(("groups", "vocab"), None),
        P(),
        P("vocab", None),
        P(),
        P(None, "groups"),
        P(None, "groups"),
    )
    out_specs = (P(None, "groups", "vocab"), P(("groups", "vocab"), None))
    return jax.shard_map(body, mesh=mesh, in_specs=in_specs, out_specs=out_specs, check_vma=False)
```

```python
import functools
import math

import jax
import jax.numpy as jnp
from jax import lax
from jax.experimental import pallas as pl
from jax.experimental.pallas import tpu as pltpu
from jax.sharding import PartitionSpec as P

BLOCK = 16
MIB = 2**20


def reversed_bits(value, bits):
    out = 0
    for k in range(bits):
        out = out * 2 + (value >> k & 1)
    return out


def table_rows(rows, shards):
    bits = shards.bit_length() - 3
    dev = rows // shards
    return [
        (reversed_bits(q, bits) * 4 + y * 2 + c) * dev + j
        for c in range(2)
        for y in range(2)
        for q in range(shards // 4)
        for j in range(dev)
    ]


def pick_kernel(step, places, ids_ref, table_ref, *refs):
    *refs, ids, listed, slots, rows, ids_sem, sems = refs
    if places:
        class_ref, heat_ref, *outs, temps_ref, classes, heat, heat_sems = refs
        heat_copies = [
            pltpu.make_async_copy(class_ref, classes, heat_sems.at[0]),
            pltpu.make_async_copy(heat_ref, heat, heat_sems.at[1]),
        ]
    else:
        outs = refs[-2:]
    count = ids_ref.shape[1]
    held = slots.shape[0]
    voc_dev = table_ref.shape[0]
    shards = lax.axis_size("vocab")
    bits = shards.bit_length() - 3
    rows_dev = count // shards
    me = lax.axis_index("vocab")
    offset = me * voc_dev
    low = me % 4
    fetch = pltpu.make_async_copy(ids_ref, ids, ids_sem)
    fetch.start()
    if places:
        for fetched in heat_copies:
            fetched.start()
    rows[...] = jnp.zeros_like(rows)
    fetch.wait()

    def copy(n):
        base = pl.multiple_of(listed[n] // count // BLOCK * BLOCK, BLOCK)
        slot = n % held
        return pltpu.make_async_copy(
            table_ref.at[pl.ds(base, BLOCK)], slots.at[slot], sems.at[slot]
        )

    found = jnp.int32(0)
    for r in range(count):
        local = ids[step, r] - offset
        listed[found] = local * count + r
        found = found + ((local >= 0) & (local < voc_dev)).astype(jnp.int32)

    for first in range(0, count, held):
        last = jnp.minimum(found, first + held)

        @pl.loop(first, last)
        def _(n):
            copy(n).start()

        if places and first == 0:
            for fetched in heat_copies:
                fetched.wait()
            temps = jnp.ones(temps_ref.shape, jnp.float32)
            lane = lax.broadcasted_iota(jnp.int32, temps.shape, 1)
            for place, (at, row) in enumerate(places):
                temps = jnp.where(lane == place, heat[classes[at, row]], temps)
            temps_ref[...] = temps

        @pl.loop(first, last)
        def _(n):
            entry = listed[n]
            r = entry % count
            copy(n).wait()
            block = slots[n % held].astype(jnp.float32)
            sub = lax.broadcasted_iota(jnp.int32, block.shape, 0)
            picked = jnp.sum(
                jnp.where(sub == entry // count % BLOCK, block, 0.0), axis=0, keepdims=True
            )
            owner = r // rows_dev
            way = owner % 4 ^ low
            order = owner // 4 ^ me // 4
            if step == 0:
                order = sum((owner // 4 >> k) % 2 << (bits - 1 - k) for k in range(bits))
            place = (way % 2 * 2 + way // 2) * (shards // 4) + order
            rows[pl.ds(place * rows_dev + r % rows_dev, 1), :] = picked

    half = count // 2
    for part, out in enumerate(outs):
        out[...] = rows[part * half : (part + 1) * half].astype(out.dtype)


def picked_rows(ids, table, step, places, *others):
    count = ids.shape[1]
    width = table.shape[1]
    held = min(count, 32)
    out = (jax.ShapeDtypeStruct((count // 2, width), table.dtype),) * 2
    heat = []
    if places:
        out += (jax.ShapeDtypeStruct((1, len(places)), jnp.float32),)
        others = [in_hbm(other) for other in others]
        heat = [pltpu.SMEM(other.shape, other.dtype) for other in others]
        heat += [pltpu.SemaphoreType.DMA((2,))]
    anywhere, vmem = pl.BlockSpec(memory_space=pl.ANY), pl.BlockSpec(memory_space=pltpu.VMEM)
    return pl.pallas_call(
        functools.partial(pick_kernel, step, places),
        out_shape=out,
        in_specs=[anywhere] * (2 + len(others)),
        out_specs=(vmem,) * len(out),
        scratch_shapes=heat
        + [
            pltpu.SMEM(ids.shape, jnp.int32),
            pltpu.SMEM((count + 1,), jnp.int32),
            pltpu.VMEM((held, BLOCK, width), table.dtype),
            pltpu.VMEM((count, width), jnp.float32),
            pltpu.SemaphoreType.DMA,
            pltpu.SemaphoreType.DMA((held,)),
        ],
        compiler_params=pltpu.CompilerParams(vmem_limit_bytes=16 * MIB),
        name="pick",
    )(in_hbm(ids), in_hbm(table), *others)


def in_hbm(array):
    return pltpu.with_memory_space_constraint(array, pltpu.HBM)


def fold_kernel(keep_ref, got_ref, first_ref, delta_ref, own_ref, send_ref, beside_ref):
    total = keep_ref[...].astype(jnp.float32) + got_ref[...].astype(jnp.float32)
    half = own_ref.shape[0]
    own_ref[...] = total[:half].astype(own_ref.dtype)
    send_ref[...] = total[half:].astype(send_ref.dtype)
    beside_ref[...] = jnp.concatenate(
        [first_ref[...].astype(jnp.float32), delta_ref[...].astype(jnp.float32)], axis=0
    ).astype(beside_ref.dtype)


def folded(keep, got, first, deltas):
    rows, width = keep.shape
    vmem = pl.BlockSpec(memory_space=pltpu.VMEM)
    part = jax.ShapeDtypeStruct((rows // 2, width), keep.dtype)
    return pl.pallas_call(
        fold_kernel,
        out_shape=(part, part, jax.ShapeDtypeStruct((2 * first.shape[0], width), keep.dtype)),
        in_specs=[vmem] * 4,
        out_specs=(vmem,) * 3,
        compiler_params=pltpu.CompilerParams(vmem_limit_bytes=12 * MIB),
        name="fold",
    )(keep, got, first, deltas)


def plus_kernel(own_ref, got_ref, *refs):
    out_ref = refs[-1]
    out_ref[...] = own_ref[...] + got_ref[...]


def join_kernel(own_ref, got_ref, *refs):
    out_ref = refs[-1]
    half = own_ref.shape[0] // 2
    own, got = own_ref[...].astype(jnp.float32), got_ref[...].astype(jnp.float32)
    parts = [own[:half], got[:half], own[half:], got[half:]]
    out_ref[...] = jnp.concatenate(parts, axis=0).astype(out_ref.dtype)


def chips_kernel(own_ref, got_ref, *refs):
    out_ref = refs[-1]
    own, got = own_ref[...], got_ref[...]
    upper = lax.axis_index("vocab") // 2 % 2 == 1
    rows = own.shape[0]
    out_ref[:rows, :] = jnp.where(upper, got, own)
    out_ref[rows:, :] = jnp.where(upper, own, got)


def merge_kernel(own_ref, got_ref, *refs):
    out_ref = refs[-1]
    own, got = own_ref[...], got_ref[...]
    peak = jnp.maximum(own[0:1], got[0:1])
    out_ref[0:1, :] = peak
    out_ref[1:2, :] = own[1:2] * jnp.exp(own[0:1] - peak) + got[1:2] * jnp.exp(got[0:1] - peak)


def paired(kernel, own, got, rows, name, *after):
    vmem = pl.BlockSpec(memory_space=pltpu.VMEM)
    return pl.pallas_call(
        kernel,
        out_shape=jax.ShapeDtypeStruct((rows, own.shape[1]), own.dtype),
        in_specs=[vmem] * 2 + [pl.BlockSpec(memory_space=pl.ANY)] * len(after),
        out_specs=vmem,
        compiler_params=pltpu.CompilerParams(vmem_limit_bytes=12 * MIB),
        name=name,
    )(own, got, *after)


def swapped(rows, bit):
    pairs = [(i, i ^ bit) for i in range(lax.axis_size("vocab"))]
    return lax.ppermute(rows, "vocab", pairs)


def load_kernel(first, last, table_ref, *refs):
    out_ref, token_ref, sems = refs[-3:]
    parts = sems.shape[0]
    part = (last - first) // parts
    rows = [pl.ds(first + k * part, part) for k in range(parts)]
    copies = [
        pltpu.make_async_copy(table_ref.at[at], out_ref.at[at], sems.at[k])
        for k, at in enumerate(rows)
    ]
    for copy in copies:
        copy.start()
    token_ref[...] = jnp.zeros_like(token_ref)
    for copy in copies:
        copy.wait()


def loaded(table, first, last, held, *after):
    anywhere, vmem = pl.BlockSpec(memory_space=pl.ANY), pl.BlockSpec(memory_space=pltpu.VMEM)
    held = [] if held is None else [held]
    return pl.pallas_call(
        functools.partial(load_kernel, first, last),
        out_shape=(
            jax.ShapeDtypeStruct(table.shape, table.dtype),
            jax.ShapeDtypeStruct((8, 128), jnp.float32),
        ),
        in_specs=[anywhere] * (1 + len(after)) + [vmem] * len(held),
        out_specs=(vmem, vmem),
        input_output_aliases={1 + len(after): 0} if held else {},
        scratch_shapes=[pltpu.SemaphoreType.DMA((4,))],
        compiler_params=pltpu.CompilerParams(vmem_limit_bytes=4 * MIB),
        name="load",
    )(in_hbm(table), *after, *held)


def norm_kernel(first_ref, own_ref, got_ref, delta_ref, gain_ref, *refs):
    out_ref = refs[-1]
    width = first_ref.shape[1]
    gain = gain_ref[...]

    def rescaled(hidden):
        squares = jnp.mean(hidden * hidden, axis=-1, keepdims=True)
        return hidden * lax.rsqrt(squares + 1e-06) * gain

    me = lax.axis_index("vocab")
    bits = lax.axis_size("vocab").bit_length() - 3

    def in_order(rows):
        for k in range(bits):
            size = rows.shape[0] >> k + 1
            parts = [rows[i * size : (i + 1) * size] for i in range(2 << k)]
            other = [parts[i ^ 1] for i in range(2 << k)]
            rows = jnp.where(
                me // 4 >> k & 1 != 0, jnp.concatenate(other), jnp.concatenate(parts)
            )
        return rows

    one = rescaled(in_order(first_ref[...].astype(jnp.float32)))
    picked = own_ref[...].astype(jnp.float32) + got_ref[...].astype(jnp.float32)
    embedded = (picked * math.sqrt(width)).astype(jnp.bfloat16)
    two = rescaled(
        embedded.astype(jnp.float32) + in_order(delta_ref[...].astype(jnp.float32))
    )
    out_ref[...] = jnp.concatenate([one, two], axis=0).astype(out_ref.dtype)


def normed(first, own, got, delta, gain, *after):
    rows, width = first.shape
    vmem = pl.BlockSpec(memory_space=pltpu.VMEM)
    return pl.pallas_call(
        norm_kernel,
        out_shape=jax.ShapeDtypeStruct((2 * rows, width), jnp.bfloat16),
        in_specs=[vmem] * 5 + [pl.BlockSpec(memory_space=pl.ANY)] * len(after),
        out_specs=vmem,
        compiler_params=pltpu.CompilerParams(vmem_limit_bytes=12 * MIB),
        name="norm",
    )(first, own, got, delta, gain.reshape(1, width), *after)


def head_kernel(own_ref, got_ref, table_ref, temps_ref, scaled_ref, stats_ref):
    me = lax.axis_index("vocab")
    dims = (((1,), (1,)), ((), ()))
    own, got = own_ref[...], got_ref[...]
    states = jnp.where(
        me % 2 == 1, jnp.concatenate([got, own], axis=0), jnp.concatenate([own, got], axis=0)
    )
    logits = lax.dot_general(table_ref[...], states, dims, preferred_element_type=jnp.float32)
    scaled = logits / temps_ref[...]
    scaled_ref[...] = scaled
    peak = jnp.max(scaled, axis=0, keepdims=True)
    stats_ref[0:1, :] = peak
    stats_ref[1:2, :] = jnp.sum(jnp.exp(scaled - peak), axis=0, keepdims=True)


def head(own, got, table, temps):
    voc_dev, width = table.shape
    rows = 2 * own.shape[0]
    return pl.pallas_call(
        head_kernel,
        out_shape=(
            jax.ShapeDtypeStruct((voc_dev, rows), jnp.float32),
            jax.ShapeDtypeStruct((2, rows), jnp.float32),
        ),
        in_specs=[pl.BlockSpec(memory_space=pltpu.VMEM)] * 4,
        out_specs=(pl.BlockSpec(memory_space=pltpu.VMEM),) * 2,
        compiler_params=pltpu.CompilerParams(vmem_limit_bytes=30 * MIB),
        name="head",
    )(own, got, table, temps)


def turn_kernel(order, scaled_ref, out_ref):
    turned = scaled_ref[...].T
    for place, (step, row) in enumerate(order):
        out_ref[step, row : row + 1, :] = turned[place : place + 1]


def turned(scaled, order, steps):
    voc_dev, rows = scaled.shape
    return pl.pallas_call(
        functools.partial(turn_kernel, order),
        out_shape=jax.ShapeDtypeStruct((steps, rows // steps, voc_dev), jnp.float32),
        compiler_params=pltpu.CompilerParams(vmem_limit_bytes=12 * MIB),
        name="turn",
    )(scaled)


def finish_kernel(order, scaled_ref, own_ref, got_ref, out_ref):
    own, got = own_ref[...], got_ref[...]
    peak = jnp.maximum(own[0:1], got[0:1])
    total = own[1:2] * jnp.exp(own[0:1] - peak) + got[1:2] * jnp.exp(got[0:1] - peak)
    both = jnp.concatenate([peak, jnp.log(total)], axis=0)
    rows = both.shape[1]
    spread = jnp.broadcast_to(both[:, None, :], (2, 128, rows))
    peak, log = spread[0].T, spread[1].T
    voc_dev = out_ref.shape[2]
    peak = jnp.concatenate([peak] * (voc_dev // 128), axis=1)
    log = jnp.concatenate([log] * (voc_dev // 128), axis=1)
    for place, (step, row) in enumerate(order):
        at = slice(place, place + 1)
        out_ref[step, row : row + 1, :] = scaled_ref[step, row : row + 1, :] - peak[at] - log[at]


def finished(scaled, own, got, order):
    return pl.pallas_call(
        functools.partial(finish_kernel, order),
        out_shape=jax.ShapeDtypeStruct(scaled.shape, jnp.float32),
        compiler_params=pltpu.CompilerParams(vmem_limit_bytes=12 * MIB),
        name="finish",
    )(scaled, own, got)


def merged(own, got):
    peak = jnp.maximum(own[0], got[0])
    total = own[1] * jnp.exp(own[0] - peak) + got[1] * jnp.exp(got[0] - peak)
    return jnp.stack([peak, total])


def body(first, deltas, gain, table, lookup, classes, ids):
    shards = lax.axis_size("vocab")
    rows_dev, width = first.shape
    steps, rows = ids.shape
    quarter = rows // 4
    high = [1 << k for k in range(shards.bit_length() - 2, 1, -1)]

    order = table_rows(rows, shards)
    places = [
        (step, order[pair * quarter + k])
        for pair in range(4)
        for step in range(steps)
        for k in range(quarter)
    ]

    keep, send, temps = picked_rows(ids, table, 0, places, classes, lookup)
    own, send, beside = folded(keep, swapped(send, 1), first, deltas)
    own = own + swapped(send, 2)
    keep, send = picked_rows(ids, table, 1, (), own)
    keep = keep + swapped(send, 1)
    following = keep[:quarter] + swapped(keep[quarter:], 2)
    for k, bit in enumerate(high):
        held = beside.shape[0] // 2
        moved = swapped(beside, bit)
        got = swapped(own, bit)
        if k < len(high) - 1:
            beside = paired(join_kernel, beside, moved, 4 * held, "join", own)
            own = paired(plus_kernel, own, got, quarter, "plus", send)
    state = jnp.concatenate([beside[:held], moved[:held]], axis=0)
    delta = jnp.concatenate([beside[held:], moved[held:]], axis=0)
    voc_dev = table.shape[0]
    head_table, token = loaded(table, 0, voc_dev // 4, None, own)
    states = normed(state, own, got, delta, gain, token)
    head_table, token = loaded(table, voc_dev // 4, voc_dev, head_table, states, following)
    states = paired(chips_kernel, states, swapped(states, 2), rows, "chips", token)
    others = swapped(states, 1)
    scaled, stats = head(states, others, head_table, temps)
    scaled = turned(scaled, places, steps)
    for bit in high:
        half = following.shape[0] // 2
        following = following[:half] + swapped(following[half:], bit)
    embedded = (following.astype(jnp.float32) * math.sqrt(width)).astype(jnp.bfloat16)
    for bit in high[:-1]:
        stats = merged(stats, swapped(stats, bit))
    stats = paired(merge_kernel, stats, swapped(stats, high[-1]), 2, "merge", following)
    stats = merged(stats, swapped(stats, 2))
    logprobs = finished(scaled, stats, swapped(stats, 1), places)
    return logprobs, embedded


def solution(mesh):
    in_specs = (
        P(("groups", "vocab"), None),
        P(("groups", "vocab"), None),
        P(),
        P("vocab", None),
        P(),
        P(None, "groups"),
        P(None, "groups"),
    )
    out_specs = (P(None, "groups", "vocab"), P(("groups", "vocab"), None))
    return jax.shard_map(body, mesh=mesh, in_specs=in_specs, out_specs=out_specs, check_vma=False)
```

```python
import functools
import math

import jax
import jax.numpy as jnp
from jax import lax
from jax.experimental import pallas as pl
from jax.experimental.pallas import tpu as pltpu
from jax.sharding import PartitionSpec as P

BLOCK = 16
MIB = 2**20


def table_rows(rows, shards):
    dev = rows // shards
    return [
        (q * 4 + y * 2 + c) * dev + j
        for c in range(2)
        for y in range(2)
        for q in range(shards // 4)
        for j in range(dev)
    ]


def pick_kernel(step, places, ids_ref, table_ref, *refs):
    *refs, ids, listed, slots, rows, ids_sem, sems = refs
    if places:
        class_ref, heat_ref, *outs, temps_ref, classes, heat, heat_sems = refs
        heat_copies = [
            pltpu.make_async_copy(class_ref, classes, heat_sems.at[0]),
            pltpu.make_async_copy(heat_ref, heat, heat_sems.at[1]),
        ]
    else:
        outs = refs[-2:]
    count = ids_ref.shape[1]
    held = slots.shape[0]
    voc_dev = table_ref.shape[0]
    shards = lax.axis_size("vocab")
    bits = shards.bit_length() - 3
    rows_dev = count // shards
    me = lax.axis_index("vocab")
    offset = me * voc_dev
    low = me % 4
    fetch = pltpu.make_async_copy(ids_ref, ids, ids_sem)
    fetch.start()
    if places:
        for fetched in heat_copies:
            fetched.start()
    rows[...] = jnp.zeros_like(rows)
    fetch.wait()

    def copy(n):
        base = pl.multiple_of(listed[n] // count // BLOCK * BLOCK, BLOCK)
        slot = n % held
        return pltpu.make_async_copy(
            table_ref.at[pl.ds(base, BLOCK)], slots.at[slot], sems.at[slot]
        )

    found = jnp.int32(0)
    for r in range(count):
        local = ids[step, r] - offset
        listed[found] = local * count + r
        found = found + ((local >= 0) & (local < voc_dev)).astype(jnp.int32)

    for first in range(0, count, held):
        last = jnp.minimum(found, first + held)

        @pl.loop(first, last)
        def _(n):
            copy(n).start()

        if places and first == 0:
            for fetched in heat_copies:
                fetched.wait()
            temps = jnp.ones(temps_ref.shape, jnp.float32)
            lane = lax.broadcasted_iota(jnp.int32, temps.shape, 1)
            for place, (at, row) in enumerate(places):
                temps = jnp.where(lane == place, heat[classes[at, row]], temps)
            temps_ref[...] = temps

        @pl.loop(first, last)
        def _(n):
            entry = listed[n]
            r = entry % count
            copy(n).wait()
            block = slots[n % held].astype(jnp.float32)
            sub = lax.broadcasted_iota(jnp.int32, block.shape, 0)
            picked = jnp.sum(
                jnp.where(sub == entry // count % BLOCK, block, 0.0), axis=0, keepdims=True
            )
            owner = r // rows_dev
            way = owner % 4 ^ low
            order = owner // 4
            if step > 0:
                chip = order ^ me // 4
                order = sum((chip >> k) % 2 << (bits - 1 - k) for k in range(bits))
            place = (way % 2 * 2 + way // 2) * (shards // 4) + order
            rows[pl.ds(place * rows_dev + r % rows_dev, 1), :] = picked

    half = count // 2
    for part, out in enumerate(outs):
        out[...] = rows[part * half : (part + 1) * half].astype(out.dtype)


def picked_rows(ids, table, step, places, *others):
    count = ids.shape[1]
    width = table.shape[1]
    held = min(count, 32)
    out = (jax.ShapeDtypeStruct((count // 2, width), table.dtype),) * 2
    heat = []
    if places:
        out += (jax.ShapeDtypeStruct((1, len(places)), jnp.float32),)
        others = [in_hbm(other) for other in others]
        heat = [pltpu.SMEM(other.shape, other.dtype) for other in others]
        heat += [pltpu.SemaphoreType.DMA((2,))]
    anywhere, vmem = pl.BlockSpec(memory_space=pl.ANY), pl.BlockSpec(memory_space=pltpu.VMEM)
    return pl.pallas_call(
        functools.partial(pick_kernel, step, places),
        out_shape=out,
        in_specs=[anywhere] * (2 + len(others)),
        out_specs=(vmem,) * len(out),
        scratch_shapes=heat
        + [
            pltpu.SMEM(ids.shape, jnp.int32),
            pltpu.SMEM((count + 1,), jnp.int32),
            pltpu.VMEM((held, BLOCK, width), table.dtype),
            pltpu.VMEM((count, width), jnp.float32),
            pltpu.SemaphoreType.DMA,
            pltpu.SemaphoreType.DMA((held,)),
        ],
        compiler_params=pltpu.CompilerParams(vmem_limit_bytes=16 * MIB),
        name="pick",
    )(in_hbm(ids), in_hbm(table), *others)


def in_hbm(array):
    return pltpu.with_memory_space_constraint(array, pltpu.HBM)


def fold_kernel(keep_ref, got_ref, first_ref, delta_ref, own_ref, send_ref, beside_ref):
    total = keep_ref[...].astype(jnp.float32) + got_ref[...].astype(jnp.float32)
    half = own_ref.shape[0]
    own_ref[...] = total[:half].astype(own_ref.dtype)
    send_ref[...] = total[half:].astype(send_ref.dtype)
    beside_ref[...] = jnp.concatenate(
        [first_ref[...].astype(jnp.float32), delta_ref[...].astype(jnp.float32)], axis=0
    ).astype(beside_ref.dtype)


def folded(keep, got, first, deltas):
    rows, width = keep.shape
    vmem = pl.BlockSpec(memory_space=pltpu.VMEM)
    part = jax.ShapeDtypeStruct((rows // 2, width), keep.dtype)
    return pl.pallas_call(
        fold_kernel,
        out_shape=(part, part, jax.ShapeDtypeStruct((2 * first.shape[0], width), keep.dtype)),
        in_specs=[vmem] * 4,
        out_specs=(vmem,) * 3,
        compiler_params=pltpu.CompilerParams(vmem_limit_bytes=12 * MIB),
        name="fold",
    )(keep, got, first, deltas)


def plus_kernel(own_ref, got_ref, *refs):
    out_ref = refs[-1]
    out_ref[...] = own_ref[...] + got_ref[...]


def join_kernel(own_ref, got_ref, *refs):
    out_ref = refs[-1]
    half = own_ref.shape[0] // 2
    own, got = own_ref[...].astype(jnp.float32), got_ref[...].astype(jnp.float32)
    parts = [own[:half], got[:half], own[half:], got[half:]]
    out_ref[...] = jnp.concatenate(parts, axis=0).astype(out_ref.dtype)


def chips_kernel(own_ref, got_ref, *refs):
    out_ref = refs[-1]
    own, got = own_ref[...], got_ref[...]
    upper = lax.axis_index("vocab") // 2 % 2 == 1
    rows = own.shape[0]
    out_ref[:rows, :] = jnp.where(upper, got, own)
    out_ref[rows:, :] = jnp.where(upper, own, got)


def merge_kernel(own_ref, got_ref, *refs):
    out_ref = refs[-1]
    own, got = own_ref[...], got_ref[...]
    peak = jnp.maximum(own[0:1], got[0:1])
    out_ref[0:1, :] = peak
    out_ref[1:2, :] = own[1:2] * jnp.exp(own[0:1] - peak) + got[1:2] * jnp.exp(got[0:1] - peak)


def paired(kernel, own, got, rows, name, *after):
    vmem = pl.BlockSpec(memory_space=pltpu.VMEM)
    return pl.pallas_call(
        kernel,
        out_shape=jax.ShapeDtypeStruct((rows, own.shape[1]), own.dtype),
        in_specs=[vmem] * 2 + [pl.BlockSpec(memory_space=pl.ANY)] * len(after),
        out_specs=vmem,
        compiler_params=pltpu.CompilerParams(vmem_limit_bytes=12 * MIB),
        name=name,
    )(own, got, *after)


def swapped(rows, bit):
    pairs = [(i, i ^ bit) for i in range(lax.axis_size("vocab"))]
    return lax.ppermute(rows, "vocab", pairs)


def load_kernel(first, last, table_ref, *refs):
    out_ref, token_ref, sems = refs[-3:]
    parts = sems.shape[0]
    part = (last - first) // parts
    rows = [pl.ds(first + k * part, part) for k in range(parts)]
    copies = [
        pltpu.make_async_copy(table_ref.at[at], out_ref.at[at], sems.at[k])
        for k, at in enumerate(rows)
    ]
    for copy in copies:
        copy.start()
    token_ref[...] = jnp.zeros_like(token_ref)
    for copy in copies:
        copy.wait()


def loaded(table, first, last, held, *after):
    anywhere, vmem = pl.BlockSpec(memory_space=pl.ANY), pl.BlockSpec(memory_space=pltpu.VMEM)
    held = [] if held is None else [held]
    return pl.pallas_call(
        functools.partial(load_kernel, first, last),
        out_shape=(
            jax.ShapeDtypeStruct(table.shape, table.dtype),
            jax.ShapeDtypeStruct((8, 128), jnp.float32),
        ),
        in_specs=[anywhere] * (1 + len(after)) + [vmem] * len(held),
        out_specs=(vmem, vmem),
        input_output_aliases={1 + len(after): 0} if held else {},
        scratch_shapes=[pltpu.SemaphoreType.DMA((4,))],
        compiler_params=pltpu.CompilerParams(vmem_limit_bytes=4 * MIB),
        name="load",
    )(in_hbm(table), *after, *held)


def norm_kernel(first_ref, own_ref, got_ref, delta_ref, gain_ref, *refs):
    out_ref = refs[-1]
    width = first_ref.shape[1]
    gain = gain_ref[...]

    def rescaled(hidden):
        squares = jnp.mean(hidden * hidden, axis=-1, keepdims=True)
        return hidden * lax.rsqrt(squares + 1e-06) * gain

    me = lax.axis_index("vocab")
    bits = lax.axis_size("vocab").bit_length() - 3

    def in_order(rows):
        for k in range(bits):
            size = rows.shape[0] >> k + 1
            parts = [rows[i * size : (i + 1) * size] for i in range(2 << k)]
            other = [parts[i ^ 1] for i in range(2 << k)]
            rows = jnp.where(
                me // 4 >> bits - 1 - k & 1 != 0, jnp.concatenate(other), jnp.concatenate(parts)
            )
        return rows

    one = rescaled(in_order(first_ref[...].astype(jnp.float32)))
    picked = own_ref[...].astype(jnp.float32) + got_ref[...].astype(jnp.float32)
    embedded = (picked * math.sqrt(width)).astype(jnp.bfloat16)
    two = rescaled(
        embedded.astype(jnp.float32) + in_order(delta_ref[...].astype(jnp.float32))
    )
    out_ref[...] = jnp.concatenate([one, two], axis=0).astype(out_ref.dtype)


def normed(first, own, got, delta, gain, *after):
    rows, width = first.shape
    vmem = pl.BlockSpec(memory_space=pltpu.VMEM)
    return pl.pallas_call(
        norm_kernel,
        out_shape=jax.ShapeDtypeStruct((2 * rows, width), jnp.bfloat16),
        in_specs=[vmem] * 5 + [pl.BlockSpec(memory_space=pl.ANY)] * len(after),
        out_specs=vmem,
        compiler_params=pltpu.CompilerParams(vmem_limit_bytes=12 * MIB),
        name="norm",
    )(first, own, got, delta, gain.reshape(1, width), *after)


def head_kernel(own_ref, got_ref, table_ref, temps_ref, scaled_ref, stats_ref):
    me = lax.axis_index("vocab")
    dims = (((1,), (1,)), ((), ()))
    own, got = own_ref[...], got_ref[...]
    states = jnp.where(
        me % 2 == 1, jnp.concatenate([got, own], axis=0), jnp.concatenate([own, got], axis=0)
    )
    logits = lax.dot_general(table_ref[...], states, dims, preferred_element_type=jnp.float32)
    scaled = logits / temps_ref[...]
    scaled_ref[...] = scaled
    peak = jnp.max(scaled, axis=0, keepdims=True)
    stats_ref[0:1, :] = peak
    stats_ref[1:2, :] = jnp.sum(jnp.exp(scaled - peak), axis=0, keepdims=True)


def head(own, got, table, temps):
    voc_dev, width = table.shape
    rows = 2 * own.shape[0]
    return pl.pallas_call(
        head_kernel,
        out_shape=(
            jax.ShapeDtypeStruct((voc_dev, rows), jnp.float32),
            jax.ShapeDtypeStruct((2, rows), jnp.float32),
        ),
        in_specs=[pl.BlockSpec(memory_space=pltpu.VMEM)] * 4,
        out_specs=(pl.BlockSpec(memory_space=pltpu.VMEM),) * 2,
        compiler_params=pltpu.CompilerParams(vmem_limit_bytes=30 * MIB),
        name="head",
    )(own, got, table, temps)


def turn_kernel(order, scaled_ref, out_ref):
    turned = scaled_ref[...].T
    for place, (step, row) in enumerate(order):
        out_ref[step, row : row + 1, :] = turned[place : place + 1]


def turned(scaled, order, steps):
    voc_dev, rows = scaled.shape
    return pl.pallas_call(
        functools.partial(turn_kernel, order),
        out_shape=jax.ShapeDtypeStruct((steps, rows // steps, voc_dev), jnp.float32),
        compiler_params=pltpu.CompilerParams(vmem_limit_bytes=12 * MIB),
        name="turn",
    )(scaled)


def finish_kernel(order, scaled_ref, own_ref, got_ref, out_ref):
    own, got = own_ref[...], got_ref[...]
    peak = jnp.maximum(own[0:1], got[0:1])
    total = own[1:2] * jnp.exp(own[0:1] - peak) + got[1:2] * jnp.exp(got[0:1] - peak)
    both = jnp.concatenate([peak, jnp.log(total)], axis=0)
    rows = both.shape[1]
    spread = jnp.broadcast_to(both[:, None, :], (2, 128, rows))
    peak, log = spread[0].T, spread[1].T
    voc_dev = out_ref.shape[2]
    peak = jnp.concatenate([peak] * (voc_dev // 128), axis=1)
    log = jnp.concatenate([log] * (voc_dev // 128), axis=1)
    for place, (step, row) in enumerate(order):
        at = slice(place, place + 1)
        out_ref[step, row : row + 1, :] = scaled_ref[step, row : row + 1, :] - peak[at] - log[at]


def finished(scaled, own, got, order):
    return pl.pallas_call(
        functools.partial(finish_kernel, order),
        out_shape=jax.ShapeDtypeStruct(scaled.shape, jnp.float32),
        compiler_params=pltpu.CompilerParams(vmem_limit_bytes=12 * MIB),
        name="finish",
    )(scaled, own, got)


def merged(own, got):
    peak = jnp.maximum(own[0], got[0])
    total = own[1] * jnp.exp(own[0] - peak) + got[1] * jnp.exp(got[0] - peak)
    return jnp.stack([peak, total])


def body(first, deltas, gain, table, lookup, classes, ids):
    shards = lax.axis_size("vocab")
    rows_dev, width = first.shape
    steps, rows = ids.shape
    quarter = rows // 4
    high = [1 << k for k in range(shards.bit_length() - 2, 1, -1)]

    order = table_rows(rows, shards)
    places = [
        (step, order[pair * quarter + k])
        for pair in range(4)
        for step in range(steps)
        for k in range(quarter)
    ]

    keep, send, temps = picked_rows(ids, table, 0, places, classes, lookup)
    own, send, beside = folded(keep, swapped(send, 1), first, deltas)
    own = own + swapped(send, 2)
    keep, send = picked_rows(ids, table, 1, (), own)
    keep = keep + swapped(send, 1)
    following = keep[:quarter] + swapped(keep[quarter:], 2)
    for k, bit in enumerate(high):
        held = beside.shape[0] // 2
        moved = swapped(beside, high[-1 - k])
        got = swapped(own, bit)
        if k < len(high) - 1:
            beside = paired(join_kernel, beside, moved, 4 * held, "join", own)
            own = paired(plus_kernel, own, got, quarter, "plus", send)
    state = jnp.concatenate([beside[:held], moved[:held]], axis=0)
    delta = jnp.concatenate([beside[held:], moved[held:]], axis=0)
    voc_dev = table.shape[0]
    head_table, token = loaded(table, 0, voc_dev // 4, None, own)
    states = normed(state, own, got, delta, gain, token)
    head_table, token = loaded(table, voc_dev // 4, voc_dev, head_table, states, following)
    states = paired(chips_kernel, states, swapped(states, 2), rows, "chips", token)
    others = swapped(states, 1)
    scaled, stats = head(states, others, head_table, temps)
    scaled = turned(scaled, places, steps)
    for bit in reversed(high):
        half = following.shape[0] // 2
        following = following[:half] + swapped(following[half:], bit)
    embedded = (following.astype(jnp.float32) * math.sqrt(width)).astype(jnp.bfloat16)
    for bit in high[:-1]:
        stats = merged(stats, swapped(stats, bit))
    stats = paired(merge_kernel, stats, swapped(stats, high[-1]), 2, "merge", following)
    stats = merged(stats, swapped(stats, 2))
    logprobs = finished(scaled, stats, swapped(stats, 1), places)
    return logprobs, embedded


def solution(mesh):
    in_specs = (
        P(("groups", "vocab"), None),
        P(("groups", "vocab"), None),
        P(),
        P("vocab", None),
        P(),
        P(None, "groups"),
        P(None, "groups"),
    )
    out_specs = (P(None, "groups", "vocab"), P(("groups", "vocab"), None))
    return jax.shard_map(body, mesh=mesh, in_specs=in_specs, out_specs=out_specs, check_vma=False)
```

```python
import functools
import math

import jax
import jax.numpy as jnp
from jax import lax
from jax.experimental import pallas as pl
from jax.experimental.pallas import tpu as pltpu
from jax.sharding import PartitionSpec as P

BLOCK = 16
MIB = 2**20


def reversed_bits(value, bits):
    out = 0
    for k in range(bits):
        out = out * 2 + (value >> k & 1)
    return out


def table_rows(rows, shards):
    bits = shards.bit_length() - 3
    dev = rows // shards
    return [
        (reversed_bits(q, bits) * 4 + y * 2 + c) * dev + j
        for c in range(2)
        for y in range(2)
        for q in range(shards // 4)
        for j in range(dev)
    ]


def pick_kernel(step, places, ids_ref, table_ref, *refs):
    *refs, ids, listed, slots, rows, ids_sem, sems = refs
    if places:
        class_ref, heat_ref, *outs, temps_ref, classes, heat, heat_sems = refs
        heat_copies = [
            pltpu.make_async_copy(class_ref, classes, heat_sems.at[0]),
            pltpu.make_async_copy(heat_ref, heat, heat_sems.at[1]),
        ]
    else:
        outs = refs[-2:]
    count = ids_ref.shape[1]
    held = slots.shape[0]
    voc_dev = table_ref.shape[0]
    shards = lax.axis_size("vocab")
    bits = shards.bit_length() - 3
    rows_dev = count // shards
    me = lax.axis_index("vocab")
    offset = me * voc_dev
    low = me % 4
    fetch = pltpu.make_async_copy(ids_ref, ids, ids_sem)
    fetch.start()
    if places:
        for fetched in heat_copies:
            fetched.start()
    rows[...] = jnp.zeros_like(rows)
    fetch.wait()

    def copy(n):
        base = pl.multiple_of(listed[n] // count // BLOCK * BLOCK, BLOCK)
        slot = n % held
        return pltpu.make_async_copy(
            table_ref.at[pl.ds(base, BLOCK)], slots.at[slot], sems.at[slot]
        )

    found = jnp.int32(0)
    for r in range(count):
        local = ids[step, r] - offset
        listed[found] = local * count + r
        found = found + ((local >= 0) & (local < voc_dev)).astype(jnp.int32)

    for first in range(0, count, held):
        last = jnp.minimum(found, first + held)

        @pl.loop(first, last)
        def _(n):
            copy(n).start()

        if places and first == 0:
            for fetched in heat_copies:
                fetched.wait()
            temps = jnp.ones(temps_ref.shape, jnp.float32)
            lane = lax.broadcasted_iota(jnp.int32, temps.shape, 1)
            for place, (at, row) in enumerate(places):
                temps = jnp.where(lane == place, heat[classes[at, row]], temps)
            temps_ref[...] = temps

        @pl.loop(first, last)
        def _(n):
            entry = listed[n]
            r = entry % count
            copy(n).wait()
            block = slots[n % held].astype(jnp.float32)
            sub = lax.broadcasted_iota(jnp.int32, block.shape, 0)
            picked = jnp.sum(
                jnp.where(sub == entry // count % BLOCK, block, 0.0), axis=0, keepdims=True
            )
            owner = r // rows_dev
            way = owner % 4 ^ low
            chip = owner // 4 if step == 0 else owner // 4 ^ me // 4
            order = sum((chip >> k) % 2 << (bits - 1 - k) for k in range(bits))
            place = (way % 2 * 2 + way // 2) * (shards // 4) + order
            rows[pl.ds(place * rows_dev + r % rows_dev, 1), :] = picked

    half = count // 2
    for part, out in enumerate(outs):
        out[...] = rows[part * half : (part + 1) * half].astype(out.dtype)


def picked_rows(ids, table, step, places, *others):
    count = ids.shape[1]
    width = table.shape[1]
    held = min(count, 32)
    out = (jax.ShapeDtypeStruct((count // 2, width), table.dtype),) * 2
    heat = []
    if places:
        out += (jax.ShapeDtypeStruct((1, len(places)), jnp.float32),)
        others = [in_hbm(other) for other in others]
        heat = [pltpu.SMEM(other.shape, other.dtype) for other in others]
        heat += [pltpu.SemaphoreType.DMA((2,))]
    anywhere, vmem = pl.BlockSpec(memory_space=pl.ANY), pl.BlockSpec(memory_space=pltpu.VMEM)
    return pl.pallas_call(
        functools.partial(pick_kernel, step, places),
        out_shape=out,
        in_specs=[anywhere] * (2 + len(others)),
        out_specs=(vmem,) * len(out),
        scratch_shapes=heat
        + [
            pltpu.SMEM(ids.shape, jnp.int32),
            pltpu.SMEM((count + 1,), jnp.int32),
            pltpu.VMEM((held, BLOCK, width), table.dtype),
            pltpu.VMEM((count, width), jnp.float32),
            pltpu.SemaphoreType.DMA,
            pltpu.SemaphoreType.DMA((held,)),
        ],
        compiler_params=pltpu.CompilerParams(vmem_limit_bytes=16 * MIB),
        name="pick",
    )(in_hbm(ids), in_hbm(table), *others)


def in_hbm(array):
    return pltpu.with_memory_space_constraint(array, pltpu.HBM)


def fold_kernel(keep_ref, got_ref, first_ref, delta_ref, own_ref, send_ref, beside_ref):
    total = keep_ref[...].astype(jnp.float32) + got_ref[...].astype(jnp.float32)
    half = own_ref.shape[0]
    own_ref[...] = total[:half].astype(own_ref.dtype)
    send_ref[...] = total[half:].astype(send_ref.dtype)
    beside_ref[...] = jnp.concatenate(
        [first_ref[...].astype(jnp.float32), delta_ref[...].astype(jnp.float32)], axis=0
    ).astype(beside_ref.dtype)


def folded(keep, got, first, deltas):
    rows, width = keep.shape
    vmem = pl.BlockSpec(memory_space=pltpu.VMEM)
    part = jax.ShapeDtypeStruct((rows // 2, width), keep.dtype)
    return pl.pallas_call(
        fold_kernel,
        out_shape=(part, part, jax.ShapeDtypeStruct((2 * first.shape[0], width), keep.dtype)),
        in_specs=[vmem] * 4,
        out_specs=(vmem,) * 3,
        compiler_params=pltpu.CompilerParams(vmem_limit_bytes=12 * MIB),
        name="fold",
    )(keep, got, first, deltas)


def plus_kernel(own_ref, got_ref, *refs):
    out_ref = refs[-1]
    out_ref[...] = own_ref[...] + got_ref[...]


def join_kernel(own_ref, got_ref, *refs):
    out_ref = refs[-1]
    half = own_ref.shape[0] // 2
    own, got = own_ref[...].astype(jnp.float32), got_ref[...].astype(jnp.float32)
    parts = [own[:half], got[:half], own[half:], got[half:]]
    out_ref[...] = jnp.concatenate(parts, axis=0).astype(out_ref.dtype)


def chips_kernel(own_ref, got_ref, *refs):
    out_ref = refs[-1]
    own, got = own_ref[...], got_ref[...]
    upper = lax.axis_index("vocab") // 2 % 2 == 1
    rows = own.shape[0]
    out_ref[:rows, :] = jnp.where(upper, got, own)
    out_ref[rows:, :] = jnp.where(upper, own, got)


def merge_kernel(own_ref, got_ref, *refs):
    out_ref = refs[-1]
    own, got = own_ref[...], got_ref[...]
    peak = jnp.maximum(own[0:1], got[0:1])
    out_ref[0:1, :] = peak
    out_ref[1:2, :] = own[1:2] * jnp.exp(own[0:1] - peak) + got[1:2] * jnp.exp(got[0:1] - peak)


def paired(kernel, own, got, rows, name, *after):
    vmem = pl.BlockSpec(memory_space=pltpu.VMEM)
    return pl.pallas_call(
        kernel,
        out_shape=jax.ShapeDtypeStruct((rows, own.shape[1]), own.dtype),
        in_specs=[vmem] * 2 + [pl.BlockSpec(memory_space=pl.ANY)] * len(after),
        out_specs=vmem,
        compiler_params=pltpu.CompilerParams(vmem_limit_bytes=12 * MIB),
        name=name,
    )(own, got, *after)


def swapped(rows, bit):
    pairs = [(i, i ^ bit) for i in range(lax.axis_size("vocab"))]
    return lax.ppermute(rows, "vocab", pairs)


def load_kernel(first, last, table_ref, *refs):
    out_ref, token_ref, sems = refs[-3:]
    parts = sems.shape[0]
    part = (last - first) // parts
    rows = [pl.ds(first + k * part, part) for k in range(parts)]
    copies = [
        pltpu.make_async_copy(table_ref.at[at], out_ref.at[at], sems.at[k])
        for k, at in enumerate(rows)
    ]
    for copy in copies:
        copy.start()
    token_ref[...] = jnp.zeros_like(token_ref)
    for copy in copies:
        copy.wait()


def loaded(table, first, last, held, *after):
    anywhere, vmem = pl.BlockSpec(memory_space=pl.ANY), pl.BlockSpec(memory_space=pltpu.VMEM)
    held = [] if held is None else [held]
    return pl.pallas_call(
        functools.partial(load_kernel, first, last),
        out_shape=(
            jax.ShapeDtypeStruct(table.shape, table.dtype),
            jax.ShapeDtypeStruct((8, 128), jnp.float32),
        ),
        in_specs=[anywhere] * (1 + len(after)) + [vmem] * len(held),
        out_specs=(vmem, vmem),
        input_output_aliases={1 + len(after): 0} if held else {},
        scratch_shapes=[pltpu.SemaphoreType.DMA((4,))],
        compiler_params=pltpu.CompilerParams(vmem_limit_bytes=4 * MIB),
        name="load",
    )(in_hbm(table), *after, *held)


def norm_kernel(first_ref, own_ref, got_ref, delta_ref, gain_ref, *refs):
    out_ref = refs[-1]
    width = first_ref.shape[1]
    gain = gain_ref[...]

    def rescaled(hidden):
        squares = jnp.mean(hidden * hidden, axis=-1, keepdims=True)
        return hidden * lax.rsqrt(squares + 1e-06) * gain

    me = lax.axis_index("vocab")
    bits = lax.axis_size("vocab").bit_length() - 3

    def in_order(rows):
        for k in range(bits):
            size = rows.shape[0] >> k + 1
            parts = [rows[i * size : (i + 1) * size] for i in range(2 << k)]
            other = [parts[i ^ 1] for i in range(2 << k)]
            rows = jnp.where(
                me // 4 >> k & 1 != 0, jnp.concatenate(other), jnp.concatenate(parts)
            )
        return rows

    one = rescaled(in_order(first_ref[...].astype(jnp.float32)))
    picked = own_ref[...].astype(jnp.float32) + got_ref[...].astype(jnp.float32)
    embedded = (picked * math.sqrt(width)).astype(jnp.bfloat16)
    two = rescaled(
        embedded.astype(jnp.float32) + in_order(delta_ref[...].astype(jnp.float32))
    )
    out_ref[...] = jnp.concatenate([one, two], axis=0).astype(out_ref.dtype)


def normed(first, own, got, delta, gain, *after):
    rows, width = first.shape
    vmem = pl.BlockSpec(memory_space=pltpu.VMEM)
    return pl.pallas_call(
        norm_kernel,
        out_shape=jax.ShapeDtypeStruct((2 * rows, width), jnp.bfloat16),
        in_specs=[vmem] * 5 + [pl.BlockSpec(memory_space=pl.ANY)] * len(after),
        out_specs=vmem,
        compiler_params=pltpu.CompilerParams(vmem_limit_bytes=12 * MIB),
        name="norm",
    )(first, own, got, delta, gain.reshape(1, width), *after)


def head_kernel(own_ref, got_ref, table_ref, temps_ref, scaled_ref, stats_ref):
    me = lax.axis_index("vocab")
    dims = (((1,), (1,)), ((), ()))
    own, got = own_ref[...], got_ref[...]
    states = jnp.where(
        me % 2 == 1, jnp.concatenate([got, own], axis=0), jnp.concatenate([own, got], axis=0)
    )
    logits = lax.dot_general(table_ref[...], states, dims, preferred_element_type=jnp.float32)
    scaled = logits / temps_ref[...]
    scaled_ref[...] = scaled
    peak = jnp.max(scaled, axis=0, keepdims=True)
    stats_ref[0:1, :] = peak
    stats_ref[1:2, :] = jnp.sum(jnp.exp(scaled - peak), axis=0, keepdims=True)


def head(own, got, table, temps):
    voc_dev, width = table.shape
    rows = 2 * own.shape[0]
    return pl.pallas_call(
        head_kernel,
        out_shape=(
            jax.ShapeDtypeStruct((voc_dev, rows), jnp.float32),
            jax.ShapeDtypeStruct((2, rows), jnp.float32),
        ),
        in_specs=[pl.BlockSpec(memory_space=pltpu.VMEM)] * 4,
        out_specs=(pl.BlockSpec(memory_space=pltpu.VMEM),) * 2,
        compiler_params=pltpu.CompilerParams(vmem_limit_bytes=30 * MIB),
        name="head",
    )(own, got, table, temps)


def turn_kernel(order, scaled_ref, out_ref):
    turned = scaled_ref[...].T
    for place, (step, row) in enumerate(order):
        out_ref[step, row : row + 1, :] = turned[place : place + 1]


def turned(scaled, order, steps):
    voc_dev, rows = scaled.shape
    return pl.pallas_call(
        functools.partial(turn_kernel, order),
        out_shape=jax.ShapeDtypeStruct((steps, rows // steps, voc_dev), jnp.float32),
        compiler_params=pltpu.CompilerParams(vmem_limit_bytes=12 * MIB),
        name="turn",
    )(scaled)


def finish_kernel(order, scaled_ref, own_ref, got_ref, out_ref):
    own, got = own_ref[...], got_ref[...]
    peak = jnp.maximum(own[0:1], got[0:1])
    total = own[1:2] * jnp.exp(own[0:1] - peak) + got[1:2] * jnp.exp(got[0:1] - peak)
    both = jnp.concatenate([peak, jnp.log(total)], axis=0)
    rows = both.shape[1]
    spread = jnp.broadcast_to(both[:, None, :], (2, 128, rows))
    peak, log = spread[0].T, spread[1].T
    voc_dev = out_ref.shape[2]
    peak = jnp.concatenate([peak] * (voc_dev // 128), axis=1)
    log = jnp.concatenate([log] * (voc_dev // 128), axis=1)
    for place, (step, row) in enumerate(order):
        at = slice(place, place + 1)
        out_ref[step, row : row + 1, :] = scaled_ref[step, row : row + 1, :] - peak[at] - log[at]


def finished(scaled, own, got, order):
    return pl.pallas_call(
        functools.partial(finish_kernel, order),
        out_shape=jax.ShapeDtypeStruct(scaled.shape, jnp.float32),
        compiler_params=pltpu.CompilerParams(vmem_limit_bytes=12 * MIB),
        name="finish",
    )(scaled, own, got)


def merged(own, got):
    peak = jnp.maximum(own[0], got[0])
    total = own[1] * jnp.exp(own[0] - peak) + got[1] * jnp.exp(got[0] - peak)
    return jnp.stack([peak, total])


def body(first, deltas, gain, table, lookup, classes, ids):
    shards = lax.axis_size("vocab")
    rows_dev, width = first.shape
    steps, rows = ids.shape
    quarter = rows // 4
    high = [1 << k for k in range(shards.bit_length() - 2, 1, -1)]

    order = table_rows(rows, shards)
    places = [
        (step, order[pair * quarter + k])
        for pair in range(4)
        for step in range(steps)
        for k in range(quarter)
    ]

    keep, send, temps = picked_rows(ids, table, 0, places, classes, lookup)
    own, send, beside = folded(keep, swapped(send, 1), first, deltas)
    own = own + swapped(send, 2)
    keep, send = picked_rows(ids, table, 1, (), own)
    keep = keep + swapped(send, 1)
    following = keep[:quarter] + swapped(keep[quarter:], 2)
    for k, bit in enumerate(high):
        held = beside.shape[0] // 2
        moved = swapped(beside, bit)
        got = swapped(own, bit)
        if k < len(high) - 1:
            beside = paired(join_kernel, beside, moved, 4 * held, "join", own)
            own = paired(plus_kernel, own, got, quarter, "plus", send)
    state = jnp.concatenate([beside[:held], moved[:held]], axis=0)
    delta = jnp.concatenate([beside[held:], moved[held:]], axis=0)
    voc_dev = table.shape[0]
    states = normed(state, own, got, delta, gain)
    head_table, token = loaded(table, 0, voc_dev, None, states, following)
    states = paired(chips_kernel, states, swapped(states, 2), rows, "chips", token)
    others = swapped(states, 1)
    scaled, stats = head(states, others, head_table, temps)
    scaled = turned(scaled, places, steps)
    for bit in reversed(high):
        half = following.shape[0] // 2
        following = following[:half] + swapped(following[half:], bit)
    embedded = (following.astype(jnp.float32) * math.sqrt(width)).astype(jnp.bfloat16)
    for bit in high[:-1]:
        stats = merged(stats, swapped(stats, bit))
    stats = paired(merge_kernel, stats, swapped(stats, high[-1]), 2, "merge", following)
    stats = merged(stats, swapped(stats, 2))
    logprobs = finished(scaled, stats, swapped(stats, 1), places)
    return logprobs, embedded


def solution(mesh):
    in_specs = (
        P(("groups", "vocab"), None),
        P(("groups", "vocab"), None),
        P(),
        P("vocab", None),
        P(),
        P(None, "groups"),
        P(None, "groups"),
    )
    out_specs = (P(None, "groups", "vocab"), P(("groups", "vocab"), None))
    return jax.shard_map(body, mesh=mesh, in_specs=in_specs, out_specs=out_specs, check_vma=False)
```

```python
import functools
import math

import jax
import jax.numpy as jnp
from jax import lax
from jax.experimental import pallas as pl
from jax.experimental.pallas import tpu as pltpu
from jax.sharding import PartitionSpec as P

BLOCK = 16
MIB = 2**20


def reversed_bits(value, bits):
    out = 0
    for k in range(bits):
        out = out * 2 + (value >> k & 1)
    return out


def table_rows(rows, shards):
    bits = shards.bit_length() - 3
    dev = rows // shards
    return [
        (reversed_bits(q, bits) * 4 + y * 2 + c) * dev + j
        for c in range(2)
        for y in range(2)
        for q in range(shards // 4)
        for j in range(dev)
    ]


def pick_kernel(step, places, ids_ref, table_ref, *refs):
    *refs, ids, listed, slots, rows, ids_sem, sems = refs
    if places:
        class_ref, heat_ref, *outs, temps_ref, classes, heat, heat_sems = refs
        heat_copies = [
            pltpu.make_async_copy(class_ref, classes, heat_sems.at[0]),
            pltpu.make_async_copy(heat_ref, heat, heat_sems.at[1]),
        ]
    else:
        outs = refs[-2:]
    count = ids_ref.shape[1]
    held = slots.shape[0]
    voc_dev = table_ref.shape[0]
    shards = lax.axis_size("vocab")
    bits = shards.bit_length() - 3
    rows_dev = count // shards
    me = lax.axis_index("vocab")
    offset = me * voc_dev
    low = me % 4
    fetch = pltpu.make_async_copy(ids_ref, ids, ids_sem)
    fetch.start()
    if places:
        for fetched in heat_copies:
            fetched.start()
    rows[...] = jnp.zeros_like(rows)
    fetch.wait()

    def copy(n):
        base = pl.multiple_of(listed[n] // count // BLOCK * BLOCK, BLOCK)
        slot = n % held
        return pltpu.make_async_copy(
            table_ref.at[pl.ds(base, BLOCK)], slots.at[slot], sems.at[slot]
        )

    found = jnp.int32(0)
    for r in range(count):
        local = ids[step, r] - offset
        listed[found] = local * count + r
        found = found + ((local >= 0) & (local < voc_dev)).astype(jnp.int32)

    for first in range(0, count, held):
        last = jnp.minimum(found, first + held)

        @pl.loop(first, last)
        def _(n):
            copy(n).start()

        if places and first == 0:
            for fetched in heat_copies:
                fetched.wait()
            temps = jnp.ones(temps_ref.shape, jnp.float32)
            lane = lax.broadcasted_iota(jnp.int32, temps.shape, 1)
            for place, (at, row) in enumerate(places):
                temps = jnp.where(lane == place, heat[classes[at, row]], temps)
            temps_ref[...] = temps

        @pl.loop(first, last)
        def _(n):
            entry = listed[n]
            r = entry % count
            copy(n).wait()
            block = slots[n % held].astype(jnp.float32)
            sub = lax.broadcasted_iota(jnp.int32, block.shape, 0)
            picked = jnp.sum(
                jnp.where(sub == entry // count % BLOCK, block, 0.0), axis=0, keepdims=True
            )
            owner = r // rows_dev
            way = owner % 4 ^ low
            chip = owner // 4 if step == 0 else owner // 4 ^ me // 4
            order = sum((chip >> k) % 2 << (bits - 1 - k) for k in range(bits))
            place = (way % 2 * 2 + way // 2) * (shards // 4) + order
            rows[pl.ds(place * rows_dev + r % rows_dev, 1), :] = picked

    half = count // 2
    for part, out in enumerate(outs):
        out[...] = rows[part * half : (part + 1) * half].astype(out.dtype)


def picked_rows(ids, table, step, places, *others):
    count = ids.shape[1]
    width = table.shape[1]
    held = min(count, 32)
    out = (jax.ShapeDtypeStruct((count // 2, width), table.dtype),) * 2
    heat = []
    if places:
        out += (jax.ShapeDtypeStruct((1, len(places)), jnp.float32),)
        others = [in_hbm(other) for other in others]
        heat = [pltpu.SMEM(other.shape, other.dtype) for other in others]
        heat += [pltpu.SemaphoreType.DMA((2,))]
    anywhere, vmem = pl.BlockSpec(memory_space=pl.ANY), pl.BlockSpec(memory_space=pltpu.VMEM)
    return pl.pallas_call(
        functools.partial(pick_kernel, step, places),
        out_shape=out,
        in_specs=[anywhere] * (2 + len(others)),
        out_specs=(vmem,) * len(out),
        scratch_shapes=heat
        + [
            pltpu.SMEM(ids.shape, jnp.int32),
            pltpu.SMEM((count + 1,), jnp.int32),
            pltpu.VMEM((held, BLOCK, width), table.dtype),
            pltpu.VMEM((count, width), jnp.float32),
            pltpu.SemaphoreType.DMA,
            pltpu.SemaphoreType.DMA((held,)),
        ],
        compiler_params=pltpu.CompilerParams(vmem_limit_bytes=16 * MIB),
        name="pick",
    )(in_hbm(ids), in_hbm(table), *others)


def in_hbm(array):
    return pltpu.with_memory_space_constraint(array, pltpu.HBM)


def fold_kernel(keep_ref, got_ref, first_ref, delta_ref, after_ref, *outs):
    own_ref, send_ref, beside_ref = outs
    total = keep_ref[...].astype(jnp.float32) + got_ref[...].astype(jnp.float32)
    half = own_ref.shape[0]
    own_ref[...] = total[:half].astype(own_ref.dtype)
    send_ref[...] = total[half:].astype(send_ref.dtype)
    beside_ref[...] = jnp.concatenate(
        [first_ref[...].astype(jnp.float32), delta_ref[...].astype(jnp.float32)], axis=0
    ).astype(beside_ref.dtype)


def folded(keep, got, first, deltas, after):
    rows, width = keep.shape
    vmem = pl.BlockSpec(memory_space=pltpu.VMEM)
    part = jax.ShapeDtypeStruct((rows // 2, width), keep.dtype)
    return pl.pallas_call(
        fold_kernel,
        out_shape=(part, part, jax.ShapeDtypeStruct((2 * first.shape[0], width), keep.dtype)),
        in_specs=[vmem] * 4 + [pl.BlockSpec(memory_space=pl.ANY)],
        out_specs=(vmem,) * 3,
        compiler_params=pltpu.CompilerParams(vmem_limit_bytes=12 * MIB),
        name="fold",
    )(keep, got, first, deltas, after)


def plus_kernel(own_ref, got_ref, *refs):
    out_ref = refs[-1]
    out_ref[...] = own_ref[...] + got_ref[...]


def join_kernel(own_ref, got_ref, *refs):
    out_ref = refs[-1]
    half = own_ref.shape[0] // 2
    own, got = own_ref[...].astype(jnp.float32), got_ref[...].astype(jnp.float32)
    parts = [own[:half], got[:half], own[half:], got[half:]]
    out_ref[...] = jnp.concatenate(parts, axis=0).astype(out_ref.dtype)


def chips_kernel(one_ref, one_got_ref, two_ref, two_got_ref, after_ref, out_ref):
    own = [ref[...].astype(jnp.float32) for ref in (one_ref, two_ref)]
    got = [ref[...].astype(jnp.float32) for ref in (one_got_ref, two_got_ref)]
    own, got = jnp.concatenate(own, axis=0), jnp.concatenate(got, axis=0)
    upper = lax.axis_index("vocab") // 2 % 2 == 1
    rows = own.shape[0]
    out_ref[:rows, :] = jnp.where(upper, got, own).astype(out_ref.dtype)
    out_ref[rows:, :] = jnp.where(upper, own, got).astype(out_ref.dtype)


def chips(one, one_got, two, two_got, after):
    rows, width = one.shape
    vmem = pl.BlockSpec(memory_space=pltpu.VMEM)
    return pl.pallas_call(
        chips_kernel,
        out_shape=jax.ShapeDtypeStruct((4 * rows, width), one.dtype),
        in_specs=[vmem] * 4 + [pl.BlockSpec(memory_space=pl.ANY)],
        out_specs=vmem,
        compiler_params=pltpu.CompilerParams(vmem_limit_bytes=12 * MIB),
        name="chips",
    )(one, one_got, two, two_got, after)


def merge_kernel(own_ref, got_ref, *refs):
    out_ref = refs[-1]
    own, got = own_ref[...], got_ref[...]
    peak = jnp.maximum(own[0:1], got[0:1])
    out_ref[0:1, :] = peak
    out_ref[1:2, :] = own[1:2] * jnp.exp(own[0:1] - peak) + got[1:2] * jnp.exp(got[0:1] - peak)


def paired(kernel, own, got, rows, name, *after):
    vmem = pl.BlockSpec(memory_space=pltpu.VMEM)
    return pl.pallas_call(
        kernel,
        out_shape=jax.ShapeDtypeStruct((rows, own.shape[1]), own.dtype),
        in_specs=[vmem] * 2 + [pl.BlockSpec(memory_space=pl.ANY)] * len(after),
        out_specs=vmem,
        compiler_params=pltpu.CompilerParams(vmem_limit_bytes=12 * MIB),
        name=name,
    )(own, got, *after)


def swapped(rows, bit):
    pairs = [(i, i ^ bit) for i in range(lax.axis_size("vocab"))]
    return lax.ppermute(rows, "vocab", pairs)


def load_kernel(first, last, table_ref, *refs):
    out_ref, token_ref, sems = refs[-3:]
    parts = sems.shape[0]
    part = (last - first) // parts
    rows = [pl.ds(first + k * part, part) for k in range(parts)]
    copies = [
        pltpu.make_async_copy(table_ref.at[at], out_ref.at[at], sems.at[k])
        for k, at in enumerate(rows)
    ]
    for copy in copies:
        copy.start()
    token_ref[...] = jnp.zeros_like(token_ref)
    for copy in copies:
        copy.wait()


def loaded(table, first, last, held, *after):
    anywhere, vmem = pl.BlockSpec(memory_space=pl.ANY), pl.BlockSpec(memory_space=pltpu.VMEM)
    held = [] if held is None else [held]
    return pl.pallas_call(
        functools.partial(load_kernel, first, last),
        out_shape=(
            jax.ShapeDtypeStruct(table.shape, table.dtype),
            jax.ShapeDtypeStruct((8, 128), jnp.float32),
        ),
        in_specs=[anywhere] * (1 + len(after)) + [vmem] * len(held),
        out_specs=(vmem, vmem),
        input_output_aliases={1 + len(after): 0} if held else {},
        scratch_shapes=[pltpu.SemaphoreType.DMA((4,))],
        compiler_params=pltpu.CompilerParams(vmem_limit_bytes=4 * MIB),
        name="load",
    )(in_hbm(table), *after, *held)


def rescaled(hidden, gain):
    squares = jnp.mean(hidden * hidden, axis=-1, keepdims=True)
    return hidden * lax.rsqrt(squares + 1e-06) * gain


def in_order(rows):
    me = lax.axis_index("vocab")
    bits = lax.axis_size("vocab").bit_length() - 3
    for k in range(bits):
        size = rows.shape[0] >> k + 1
        parts = [rows[i * size : (i + 1) * size] for i in range(2 << k)]
        other = [parts[i ^ 1] for i in range(2 << k)]
        rows = jnp.where(me // 4 >> k & 1 != 0, jnp.concatenate(other), jnp.concatenate(parts))
    return rows


def first_kernel(hidden_ref, gain_ref, out_ref):
    hidden = in_order(hidden_ref[...].astype(jnp.float32))
    out_ref[...] = rescaled(hidden, gain_ref[...]).astype(out_ref.dtype)


def second_kernel(delta_ref, gain_ref, own_ref, got_ref, out_ref):
    width = out_ref.shape[1]
    picked = own_ref[...].astype(jnp.float32) + got_ref[...].astype(jnp.float32)
    embedded = (picked * math.sqrt(width)).astype(jnp.bfloat16)
    hidden = embedded.astype(jnp.float32) + in_order(delta_ref[...].astype(jnp.float32))
    out_ref[...] = rescaled(hidden, gain_ref[...]).astype(out_ref.dtype)


def normed(kernel, hidden, gain, *picked):
    rows, width = hidden.shape
    vmem = pl.BlockSpec(memory_space=pltpu.VMEM)
    return pl.pallas_call(
        kernel,
        out_shape=jax.ShapeDtypeStruct((rows, width), jnp.bfloat16),
        in_specs=[vmem] * (2 + len(picked)),
        out_specs=vmem,
        compiler_params=pltpu.CompilerParams(vmem_limit_bytes=12 * MIB),
        name="norm",
    )(hidden, gain.reshape(1, width), *picked)


def head_kernel(own_ref, got_ref, table_ref, temps_ref, scaled_ref, stats_ref):
    me = lax.axis_index("vocab")
    dims = (((1,), (1,)), ((), ()))
    own, got = own_ref[...], got_ref[...]
    states = jnp.where(
        me % 2 == 1, jnp.concatenate([got, own], axis=0), jnp.concatenate([own, got], axis=0)
    )
    logits = lax.dot_general(table_ref[...], states, dims, preferred_element_type=jnp.float32)
    scaled = logits / temps_ref[...]
    scaled_ref[...] = scaled
    peak = jnp.max(scaled, axis=0, keepdims=True)
    stats_ref[0:1, :] = peak
    stats_ref[1:2, :] = jnp.sum(jnp.exp(scaled - peak), axis=0, keepdims=True)


def head(own, got, table, temps):
    voc_dev, width = table.shape
    rows = 2 * own.shape[0]
    return pl.pallas_call(
        head_kernel,
        out_shape=(
            jax.ShapeDtypeStruct((voc_dev, rows), jnp.float32),
            jax.ShapeDtypeStruct((2, rows), jnp.float32),
        ),
        in_specs=[pl.BlockSpec(memory_space=pltpu.VMEM)] * 4,
        out_specs=(pl.BlockSpec(memory_space=pltpu.VMEM),) * 2,
        compiler_params=pltpu.CompilerParams(vmem_limit_bytes=30 * MIB),
        name="head",
    )(own, got, table, temps)


def turn_kernel(order, scaled_ref, out_ref):
    turned = scaled_ref[...].T
    for place, (step, row) in enumerate(order):
        out_ref[step, row : row + 1, :] = turned[place : place + 1]


def turned(scaled, order, steps):
    voc_dev, rows = scaled.shape
    return pl.pallas_call(
        functools.partial(turn_kernel, order),
        out_shape=jax.ShapeDtypeStruct((steps, rows // steps, voc_dev), jnp.float32),
        compiler_params=pltpu.CompilerParams(vmem_limit_bytes=12 * MIB),
        name="turn",
    )(scaled)


def finish_kernel(order, scaled_ref, own_ref, got_ref, out_ref):
    own, got = own_ref[...], got_ref[...]
    peak = jnp.maximum(own[0:1], got[0:1])
    total = own[1:2] * jnp.exp(own[0:1] - peak) + got[1:2] * jnp.exp(got[0:1] - peak)
    both = jnp.concatenate([peak, jnp.log(total)], axis=0)
    rows = both.shape[1]
    spread = jnp.broadcast_to(both[:, None, :], (2, 128, rows))
    peak, log = spread[0].T, spread[1].T
    voc_dev = out_ref.shape[2]
    peak = jnp.concatenate([peak] * (voc_dev // 128), axis=1)
    log = jnp.concatenate([log] * (voc_dev // 128), axis=1)
    for place, (step, row) in enumerate(order):
        at = slice(place, place + 1)
        out_ref[step, row : row + 1, :] = scaled_ref[step, row : row + 1, :] - peak[at] - log[at]


def finished(scaled, own, got, order):
    return pl.pallas_call(
        functools.partial(finish_kernel, order),
        out_shape=jax.ShapeDtypeStruct(scaled.shape, jnp.float32),
        compiler_params=pltpu.CompilerParams(vmem_limit_bytes=12 * MIB),
        name="finish",
    )(scaled, own, got)


def merged(own, got):
    peak = jnp.maximum(own[0], got[0])
    total = own[1] * jnp.exp(own[0] - peak) + got[1] * jnp.exp(got[0] - peak)
    return jnp.stack([peak, total])


def body(first, deltas, gain, table, lookup, classes, ids):
    shards = lax.axis_size("vocab")
    rows_dev, width = first.shape
    steps, rows = ids.shape
    quarter = rows // 4
    high = [1 << k for k in range(shards.bit_length() - 2, 1, -1)]

    order = table_rows(rows, shards)
    places = [
        (step, order[pair * quarter + k])
        for pair in range(4)
        for step in range(steps)
        for k in range(quarter)
    ]

    keep, send, temps = picked_rows(ids, table, 0, places, classes, lookup)
    voc_dev = table.shape[0]
    head_table, token = loaded(table, 0, voc_dev // 8, None, send)
    own, send, beside = folded(keep, swapped(send, 1), first, deltas, token)
    own = own + swapped(send, 2)
    keep, send = picked_rows(ids, table, 1, (), own)
    keep = keep + swapped(send, 1)
    following = keep[:quarter] + swapped(keep[quarter:], 2)
    for k, bit in enumerate(high):
        held = beside.shape[0] // 2
        moved = swapped(beside, bit)
        got = swapped(own, bit)
        if k < len(high) - 1:
            beside = paired(join_kernel, beside, moved, 4 * held, "join", own)
            own = paired(plus_kernel, own, got, quarter, "plus", send)
    state = jnp.concatenate([beside[:held], moved[:held]], axis=0)
    delta = jnp.concatenate([beside[held:], moved[held:]], axis=0)
    one = normed(first_kernel, state, gain)
    one_got = swapped(one, 2)
    two = normed(second_kernel, delta, gain, own, got)
    last = voc_dev // 8 * 7
    head_table, token = loaded(table, voc_dev // 8, last, head_table, two, following, one_got)
    states = chips(one, one_got, two, swapped(two, 2), token)
    head_table, token = loaded(table, last, voc_dev, head_table, states)
    others = swapped(states, 1)
    scaled, stats = head(states, others, head_table, temps)
    scaled = turned(scaled, places, steps)
    for bit in reversed(high):
        half = following.shape[0] // 2
        following = following[:half] + swapped(following[half:], bit)
    embedded = (following.astype(jnp.float32) * math.sqrt(width)).astype(jnp.bfloat16)
    for bit in high[:-1]:
        stats = merged(stats, swapped(stats, bit))
    stats = paired(merge_kernel, stats, swapped(stats, high[-1]), 2, "merge", following)
    stats = merged(stats, swapped(stats, 2))
    logprobs = finished(scaled, stats, swapped(stats, 1), places)
    return logprobs, embedded


def solution(mesh):
    in_specs = (
        P(("groups", "vocab"), None),
        P(("groups", "vocab"), None),
        P(),
        P("vocab", None),
        P(),
        P(None, "groups"),
        P(None, "groups"),
    )
    out_specs = (P(None, "groups", "vocab"), P(("groups", "vocab"), None))
    return jax.shard_map(body, mesh=mesh, in_specs=in_specs, out_specs=out_specs, check_vma=False)
```

```python
import functools
import math

import jax
import jax.numpy as jnp
from jax import lax
from jax.experimental import pallas as pl
from jax.experimental.pallas import tpu as pltpu
from jax.sharding import PartitionSpec as P

BLOCK = 16
MIB = 2**20


def reversed_bits(value, bits):
    out = 0
    for k in range(bits):
        out = out * 2 + (value >> k & 1)
    return out


def table_rows(rows, shards):
    bits = shards.bit_length() - 3
    dev = rows // shards
    return [
        (reversed_bits(q, bits) * 4 + y * 2 + c) * dev + j
        for c in range(2)
        for y in range(2)
        for q in range(shards // 4)
        for j in range(dev)
    ]


def pick_kernel(step, places, ids_ref, table_ref, *refs):
    *refs, ids, listed, slots, rows, ids_sem, sems = refs
    if places:
        class_ref, heat_ref, *outs, temps_ref, classes, heat, heat_sems = refs
        heat_copies = [
            pltpu.make_async_copy(class_ref, classes, heat_sems.at[0]),
            pltpu.make_async_copy(heat_ref, heat, heat_sems.at[1]),
        ]
    else:
        outs = refs[-2:]
    count = ids_ref.shape[1]
    held = slots.shape[0]
    voc_dev = table_ref.shape[0]
    shards = lax.axis_size("vocab")
    bits = shards.bit_length() - 3
    rows_dev = count // shards
    me = lax.axis_index("vocab")
    offset = me * voc_dev
    low = me % 4
    fetch = pltpu.make_async_copy(ids_ref, ids, ids_sem)
    fetch.start()
    if places:
        for fetched in heat_copies:
            fetched.start()
    rows[...] = jnp.zeros_like(rows)
    fetch.wait()

    def copy(n):
        base = pl.multiple_of(listed[n] // count // BLOCK * BLOCK, BLOCK)
        slot = n % held
        return pltpu.make_async_copy(
            table_ref.at[pl.ds(base, BLOCK)], slots.at[slot], sems.at[slot]
        )

    found = jnp.int32(0)
    for r in range(count):
        local = ids[step, r] - offset
        listed[found] = local * count + r
        found = found + ((local >= 0) & (local < voc_dev)).astype(jnp.int32)

    for first in range(0, count, held):
        last = jnp.minimum(found, first + held)

        @pl.loop(first, last)
        def _(n):
            copy(n).start()

        if places and first == 0:
            for fetched in heat_copies:
                fetched.wait()
            temps = jnp.ones(temps_ref.shape, jnp.float32)
            lane = lax.broadcasted_iota(jnp.int32, temps.shape, 1)
            for place, (at, row) in enumerate(places):
                temps = jnp.where(lane == place, heat[classes[at, row]], temps)
            temps_ref[...] = temps

        @pl.loop(first, last)
        def _(n):
            entry = listed[n]
            r = entry % count
            copy(n).wait()
            block = slots[n % held].astype(jnp.float32)
            sub = lax.broadcasted_iota(jnp.int32, block.shape, 0)
            picked = jnp.sum(
                jnp.where(sub == entry // count % BLOCK, block, 0.0), axis=0, keepdims=True
            )
            owner = r // rows_dev
            way = owner % 4 ^ low
            chip = owner // 4 if step == 0 else owner // 4 ^ me // 4
            order = sum((chip >> k) % 2 << (bits - 1 - k) for k in range(bits))
            place = (way % 2 * 2 + way // 2) * (shards // 4) + order
            rows[pl.ds(place * rows_dev + r % rows_dev, 1), :] = picked

    half = count // 2
    for part, out in enumerate(outs):
        out[...] = rows[part * half : (part + 1) * half].astype(out.dtype)


def picked_rows(ids, table, step, places, *others):
    count = ids.shape[1]
    width = table.shape[1]
    held = min(count, 32)
    out = (jax.ShapeDtypeStruct((count // 2, width), table.dtype),) * 2
    heat = []
    if places:
        out += (jax.ShapeDtypeStruct((1, len(places)), jnp.float32),)
        others = [in_hbm(other) for other in others]
        heat = [pltpu.SMEM(other.shape, other.dtype) for other in others]
        heat += [pltpu.SemaphoreType.DMA((2,))]
    anywhere, vmem = pl.BlockSpec(memory_space=pl.ANY), pl.BlockSpec(memory_space=pltpu.VMEM)
    return pl.pallas_call(
        functools.partial(pick_kernel, step, places),
        out_shape=out,
        in_specs=[anywhere] * (2 + len(others)),
        out_specs=(vmem,) * len(out),
        scratch_shapes=heat
        + [
            pltpu.SMEM(ids.shape, jnp.int32),
            pltpu.SMEM((count + 1,), jnp.int32),
            pltpu.VMEM((held, BLOCK, width), table.dtype),
            pltpu.VMEM((count, width), jnp.float32),
            pltpu.SemaphoreType.DMA,
            pltpu.SemaphoreType.DMA((held,)),
        ],
        compiler_params=pltpu.CompilerParams(vmem_limit_bytes=16 * MIB),
        name="pick",
    )(in_hbm(ids), in_hbm(table), *others)


def in_hbm(array):
    return pltpu.with_memory_space_constraint(array, pltpu.HBM)


def fold_kernel(keep_ref, got_ref, first_ref, delta_ref, after_ref, *outs):
    own_ref, send_ref, beside_ref = outs
    total = keep_ref[...].astype(jnp.float32) + got_ref[...].astype(jnp.float32)
    half = own_ref.shape[0]
    own_ref[...] = total[:half].astype(own_ref.dtype)
    send_ref[...] = total[half:].astype(send_ref.dtype)
    beside_ref[...] = jnp.concatenate(
        [first_ref[...].astype(jnp.float32), delta_ref[...].astype(jnp.float32)], axis=0
    ).astype(beside_ref.dtype)


def folded(keep, got, first, deltas, after):
    rows, width = keep.shape
    vmem = pl.BlockSpec(memory_space=pltpu.VMEM)
    part = jax.ShapeDtypeStruct((rows // 2, width), keep.dtype)
    return pl.pallas_call(
        fold_kernel,
        out_shape=(part, part, jax.ShapeDtypeStruct((2 * first.shape[0], width), keep.dtype)),
        in_specs=[vmem] * 4 + [pl.BlockSpec(memory_space=pl.ANY)],
        out_specs=(vmem,) * 3,
        compiler_params=pltpu.CompilerParams(vmem_limit_bytes=12 * MIB),
        name="fold",
    )(keep, got, first, deltas, after)


def plus_kernel(own_ref, got_ref, *refs):
    out_ref = refs[-1]
    out_ref[...] = own_ref[...] + got_ref[...]


def join_kernel(own_ref, got_ref, *refs):
    out_ref = refs[-1]
    half = own_ref.shape[0] // 2
    own, got = own_ref[...].astype(jnp.float32), got_ref[...].astype(jnp.float32)
    parts = [own[:half], got[:half], own[half:], got[half:]]
    out_ref[...] = jnp.concatenate(parts, axis=0).astype(out_ref.dtype)


def chips_kernel(one_ref, one_got_ref, two_ref, two_got_ref, after_ref, out_ref):
    own = [ref[...].astype(jnp.float32) for ref in (one_ref, two_ref)]
    got = [ref[...].astype(jnp.float32) for ref in (one_got_ref, two_got_ref)]
    own, got = jnp.concatenate(own, axis=0), jnp.concatenate(got, axis=0)
    upper = lax.axis_index("vocab") // 2 % 2 == 1
    rows = own.shape[0]
    out_ref[:rows, :] = jnp.where(upper, got, own).astype(out_ref.dtype)
    out_ref[rows:, :] = jnp.where(upper, own, got).astype(out_ref.dtype)


def chips(one, one_got, two, two_got, after):
    rows, width = one.shape
    vmem = pl.BlockSpec(memory_space=pltpu.VMEM)
    return pl.pallas_call(
        chips_kernel,
        out_shape=jax.ShapeDtypeStruct((4 * rows, width), one.dtype),
        in_specs=[vmem] * 4 + [pl.BlockSpec(memory_space=pl.ANY)],
        out_specs=vmem,
        compiler_params=pltpu.CompilerParams(vmem_limit_bytes=12 * MIB),
        name="chips",
    )(one, one_got, two, two_got, after)


def merge_kernel(own_ref, got_ref, *refs):
    out_ref = refs[-1]
    own, got = own_ref[...], got_ref[...]
    peak = jnp.maximum(own[0:1], got[0:1])
    out_ref[0:1, :] = peak
    out_ref[1:2, :] = own[1:2] * jnp.exp(own[0:1] - peak) + got[1:2] * jnp.exp(got[0:1] - peak)


def paired(kernel, own, got, rows, name, *after):
    vmem = pl.BlockSpec(memory_space=pltpu.VMEM)
    return pl.pallas_call(
        kernel,
        out_shape=jax.ShapeDtypeStruct((rows, own.shape[1]), own.dtype),
        in_specs=[vmem] * 2 + [pl.BlockSpec(memory_space=pl.ANY)] * len(after),
        out_specs=vmem,
        compiler_params=pltpu.CompilerParams(vmem_limit_bytes=12 * MIB),
        name=name,
    )(own, got, *after)


def swapped(rows, bit):
    pairs = [(i, i ^ bit) for i in range(lax.axis_size("vocab"))]
    return lax.ppermute(rows, "vocab", pairs)


def load_kernel(first, last, table_ref, *refs):
    out_ref, token_ref, sems = refs[-3:]
    parts = sems.shape[0]
    part = (last - first) // parts
    rows = [pl.ds(first + k * part, part) for k in range(parts)]
    copies = [
        pltpu.make_async_copy(table_ref.at[at], out_ref.at[at], sems.at[k])
        for k, at in enumerate(rows)
    ]
    for copy in copies:
        copy.start()
    token_ref[...] = jnp.zeros_like(token_ref)
    for copy in copies:
        copy.wait()


def loaded(table, first, last, held, *after):
    anywhere, vmem = pl.BlockSpec(memory_space=pl.ANY), pl.BlockSpec(memory_space=pltpu.VMEM)
    held = [] if held is None else [held]
    return pl.pallas_call(
        functools.partial(load_kernel, first, last),
        out_shape=(
            jax.ShapeDtypeStruct(table.shape, table.dtype),
            jax.ShapeDtypeStruct((8, 128), jnp.float32),
        ),
        in_specs=[anywhere] * (1 + len(after)) + [vmem] * len(held),
        out_specs=(vmem, vmem),
        input_output_aliases={1 + len(after): 0} if held else {},
        scratch_shapes=[pltpu.SemaphoreType.DMA((4,))],
        compiler_params=pltpu.CompilerParams(vmem_limit_bytes=4 * MIB),
        name="load",
    )(in_hbm(table), *after, *held)


def rescaled(hidden, gain):
    squares = jnp.mean(hidden * hidden, axis=-1, keepdims=True)
    return hidden * lax.rsqrt(squares + 1e-06) * gain


def in_order(rows):
    me = lax.axis_index("vocab")
    bits = lax.axis_size("vocab").bit_length() - 3
    for k in range(bits):
        size = rows.shape[0] >> k + 1
        parts = [rows[i * size : (i + 1) * size] for i in range(2 << k)]
        other = [parts[i ^ 1] for i in range(2 << k)]
        rows = jnp.where(me // 4 >> k & 1 != 0, jnp.concatenate(other), jnp.concatenate(parts))
    return rows


def first_kernel(hidden_ref, gain_ref, out_ref):
    hidden = in_order(hidden_ref[...].astype(jnp.float32))
    out_ref[...] = rescaled(hidden, gain_ref[...]).astype(out_ref.dtype)


def second_kernel(delta_ref, gain_ref, own_ref, got_ref, out_ref):
    width = out_ref.shape[1]
    picked = own_ref[...].astype(jnp.float32) + got_ref[...].astype(jnp.float32)
    embedded = (picked * math.sqrt(width)).astype(jnp.bfloat16)
    hidden = embedded.astype(jnp.float32) + in_order(delta_ref[...].astype(jnp.float32))
    out_ref[...] = rescaled(hidden, gain_ref[...]).astype(out_ref.dtype)


def normed(kernel, hidden, gain, *picked):
    rows, width = hidden.shape
    vmem = pl.BlockSpec(memory_space=pltpu.VMEM)
    return pl.pallas_call(
        kernel,
        out_shape=jax.ShapeDtypeStruct((rows, width), jnp.bfloat16),
        in_specs=[vmem] * (2 + len(picked)),
        out_specs=vmem,
        compiler_params=pltpu.CompilerParams(vmem_limit_bytes=12 * MIB),
        name="norm",
    )(hidden, gain.reshape(1, width), *picked)


def head_kernel(own_ref, got_ref, table_ref, temps_ref, scaled_ref, stats_ref):
    me = lax.axis_index("vocab")
    dims = (((1,), (1,)), ((), ()))
    own, got = own_ref[...], got_ref[...]
    states = jnp.where(
        me % 2 == 1, jnp.concatenate([got, own], axis=0), jnp.concatenate([own, got], axis=0)
    )
    logits = lax.dot_general(table_ref[...], states, dims, preferred_element_type=jnp.float32)
    scaled = logits / temps_ref[...]
    scaled_ref[...] = scaled
    peak = jnp.max(scaled, axis=0, keepdims=True)
    stats_ref[0:1, :] = peak
    stats_ref[1:2, :] = jnp.sum(jnp.exp(scaled - peak), axis=0, keepdims=True)


def head(own, got, table, temps):
    voc_dev, width = table.shape
    rows = 2 * own.shape[0]
    return pl.pallas_call(
        head_kernel,
        out_shape=(
            jax.ShapeDtypeStruct((voc_dev, rows), jnp.float32),
            jax.ShapeDtypeStruct((2, rows), jnp.float32),
        ),
        in_specs=[pl.BlockSpec(memory_space=pltpu.VMEM)] * 4,
        out_specs=(pl.BlockSpec(memory_space=pltpu.VMEM),) * 2,
        compiler_params=pltpu.CompilerParams(vmem_limit_bytes=30 * MIB),
        name="head",
    )(own, got, table, temps)


def turn_kernel(order, scaled_ref, out_ref):
    turned = scaled_ref[...].T
    for place, (step, row) in enumerate(order):
        out_ref[step, row : row + 1, :] = turned[place : place + 1]


def turned(scaled, order, steps):
    voc_dev, rows = scaled.shape
    return pl.pallas_call(
        functools.partial(turn_kernel, order),
        out_shape=jax.ShapeDtypeStruct((steps, rows // steps, voc_dev), jnp.float32),
        compiler_params=pltpu.CompilerParams(vmem_limit_bytes=12 * MIB),
        name="turn",
    )(scaled)


def finish_kernel(order, scaled_ref, own_ref, got_ref, out_ref):
    own, got = own_ref[...], got_ref[...]
    peak = jnp.maximum(own[0:1], got[0:1])
    total = own[1:2] * jnp.exp(own[0:1] - peak) + got[1:2] * jnp.exp(got[0:1] - peak)
    both = jnp.concatenate([peak, jnp.log(total)], axis=0)
    rows = both.shape[1]
    spread = jnp.broadcast_to(both[:, None, :], (2, 128, rows))
    peak, log = spread[0].T, spread[1].T
    voc_dev = out_ref.shape[2]
    peak = jnp.concatenate([peak] * (voc_dev // 128), axis=1)
    log = jnp.concatenate([log] * (voc_dev // 128), axis=1)
    for place, (step, row) in enumerate(order):
        at = slice(place, place + 1)
        out_ref[step, row : row + 1, :] = scaled_ref[step, row : row + 1, :] - peak[at] - log[at]


def finished(scaled, own, got, order):
    return pl.pallas_call(
        functools.partial(finish_kernel, order),
        out_shape=jax.ShapeDtypeStruct(scaled.shape, jnp.float32),
        compiler_params=pltpu.CompilerParams(vmem_limit_bytes=12 * MIB),
        name="finish",
    )(scaled, own, got)


def merged(own, got):
    peak = jnp.maximum(own[0], got[0])
    total = own[1] * jnp.exp(own[0] - peak) + got[1] * jnp.exp(got[0] - peak)
    return jnp.stack([peak, total])


def body(first, deltas, gain, table, lookup, classes, ids):
    shards = lax.axis_size("vocab")
    rows_dev, width = first.shape
    steps, rows = ids.shape
    quarter = rows // 4
    high = [1 << k for k in range(shards.bit_length() - 2, 1, -1)]

    order = table_rows(rows, shards)
    places = [
        (step, order[pair * quarter + k])
        for pair in range(4)
        for step in range(steps)
        for k in range(quarter)
    ]

    keep, send, temps = picked_rows(ids, table, 0, places, classes, lookup)
    voc_dev = table.shape[0]
    head_table, token = loaded(table, 0, voc_dev // 8, None, send)
    own, send, beside = folded(keep, swapped(send, 1), first, deltas, token)
    own = own + swapped(send, 2)
    keep, send = picked_rows(ids, table, 1, (), own)
    keep = keep + swapped(send, 1)
    following = keep[:quarter] + swapped(keep[quarter:], 2)
    for k, bit in enumerate(high):
        held = beside.shape[0] // 2
        moved = swapped(beside, bit)
        got = swapped(own, bit)
        if k < len(high) - 1:
            beside = paired(join_kernel, beside, moved, 4 * held, "join", own)
            own = paired(plus_kernel, own, got, quarter, "plus", send)
    state = jnp.concatenate([beside[:held], moved[:held]], axis=0)
    delta = jnp.concatenate([beside[held:], moved[held:]], axis=0)
    one = normed(first_kernel, state, gain)
    one_got = swapped(one, 2)
    two = normed(second_kernel, delta, gain, own, got)
    middle = voc_dev // 8 * 5
    head_table, token = loaded(table, voc_dev // 8, middle, head_table, two)
    head_table, token = loaded(table, middle, voc_dev, head_table, following, one_got)
    states = chips(one, one_got, two, swapped(two, 2), token)
    others = swapped(states, 1)
    scaled, stats = head(states, others, head_table, temps)
    scaled = turned(scaled, places, steps)
    for bit in reversed(high):
        half = following.shape[0] // 2
        following = following[:half] + swapped(following[half:], bit)
    embedded = (following.astype(jnp.float32) * math.sqrt(width)).astype(jnp.bfloat16)
    for bit in high[:-1]:
        stats = merged(stats, swapped(stats, bit))
    stats = paired(merge_kernel, stats, swapped(stats, high[-1]), 2, "merge", following)
    stats = merged(stats, swapped(stats, 2))
    logprobs = finished(scaled, stats, swapped(stats, 1), places)
    return logprobs, embedded


def solution(mesh):
    in_specs = (
        P(("groups", "vocab"), None),
        P(("groups", "vocab"), None),
        P(),
        P("vocab", None),
        P(),
        P(None, "groups"),
        P(None, "groups"),
    )
    out_specs = (P(None, "groups", "vocab"), P(("groups", "vocab"), None))
    return jax.shard_map(body, mesh=mesh, in_specs=in_specs, out_specs=out_specs, check_vma=False)
```

```python
import functools
import math

import jax
import jax.numpy as jnp
from jax import lax
from jax.experimental import pallas as pl
from jax.experimental.pallas import tpu as pltpu
from jax.sharding import PartitionSpec as P

BLOCK = 16
MIB = 2**20


def reversed_bits(value, bits):
    out = 0
    for k in range(bits):
        out = out * 2 + (value >> k & 1)
    return out


def table_rows(rows, shards):
    bits = shards.bit_length() - 3
    dev = rows // shards
    return [
        (reversed_bits(q, bits) * 4 + y * 2 + c) * dev + j
        for c in range(2)
        for y in range(2)
        for q in range(shards // 4)
        for j in range(dev)
    ]


def pick_kernel(step, places, ids_ref, table_ref, *refs):
    *refs, ids, listed, slots, rows, ids_sem, sems = refs
    if places:
        class_ref, heat_ref, *outs, temps_ref, classes, heat, heat_sems = refs
        heat_copies = [
            pltpu.make_async_copy(class_ref, classes, heat_sems.at[0]),
            pltpu.make_async_copy(heat_ref, heat, heat_sems.at[1]),
        ]
    else:
        outs = refs[-2:]
    count = ids_ref.shape[1]
    held = slots.shape[0]
    voc_dev = table_ref.shape[0]
    shards = lax.axis_size("vocab")
    bits = shards.bit_length() - 3
    rows_dev = count // shards
    me = lax.axis_index("vocab")
    offset = me * voc_dev
    low = me % 4
    fetch = pltpu.make_async_copy(ids_ref, ids, ids_sem)
    fetch.start()
    if places:
        for fetched in heat_copies:
            fetched.start()
    rows[...] = jnp.zeros_like(rows)
    fetch.wait()

    def copy(n):
        base = pl.multiple_of(listed[n] // count // BLOCK * BLOCK, BLOCK)
        slot = n % held
        return pltpu.make_async_copy(
            table_ref.at[pl.ds(base, BLOCK)], slots.at[slot], sems.at[slot]
        )

    found = jnp.int32(0)
    for r in range(count):
        local = ids[step, r] - offset
        listed[found] = local * count + r
        found = found + ((local >= 0) & (local < voc_dev)).astype(jnp.int32)

    for first in range(0, count, held):
        last = jnp.minimum(found, first + held)

        @pl.loop(first, last)
        def _(n):
            copy(n).start()

        if places and first == 0:
            for fetched in heat_copies:
                fetched.wait()
            temps = jnp.ones(temps_ref.shape, jnp.float32)
            lane = lax.broadcasted_iota(jnp.int32, temps.shape, 1)
            for place, (at, row) in enumerate(places):
                temps = jnp.where(lane == place, heat[classes[at, row]], temps)
            temps_ref[...] = temps

        @pl.loop(first, last)
        def _(n):
            entry = listed[n]
            r = entry % count
            copy(n).wait()
            block = slots[n % held].astype(jnp.float32)
            sub = lax.broadcasted_iota(jnp.int32, block.shape, 0)
            picked = jnp.sum(
                jnp.where(sub == entry // count % BLOCK, block, 0.0), axis=0, keepdims=True
            )
            owner = r // rows_dev
            way = owner % 4 ^ low
            chip = owner // 4 if step == 0 else owner // 4 ^ me // 4
            order = sum((chip >> k) % 2 << (bits - 1 - k) for k in range(bits))
            place = (way % 2 * 2 + way // 2) * (shards // 4) + order
            rows[pl.ds(place * rows_dev + r % rows_dev, 1), :] = picked

    half = count // 2
    for part, out in enumerate(outs):
        out[...] = rows[part * half : (part + 1) * half].astype(out.dtype)


def picked_rows(ids, table, step, places, *others):
    count = ids.shape[1]
    width = table.shape[1]
    held = min(count, 32)
    out = (jax.ShapeDtypeStruct((count // 2, width), table.dtype),) * 2
    heat = []
    if places:
        out += (jax.ShapeDtypeStruct((1, len(places)), jnp.float32),)
        others = [in_hbm(other) for other in others]
        heat = [pltpu.SMEM(other.shape, other.dtype) for other in others]
        heat += [pltpu.SemaphoreType.DMA((2,))]
    anywhere, vmem = pl.BlockSpec(memory_space=pl.ANY), pl.BlockSpec(memory_space=pltpu.VMEM)
    return pl.pallas_call(
        functools.partial(pick_kernel, step, places),
        out_shape=out,
        in_specs=[anywhere] * (2 + len(others)),
        out_specs=(vmem,) * len(out),
        scratch_shapes=heat
        + [
            pltpu.SMEM(ids.shape, jnp.int32),
            pltpu.SMEM((count + 1,), jnp.int32),
            pltpu.VMEM((held, BLOCK, width), table.dtype),
            pltpu.VMEM((count, width), jnp.float32),
            pltpu.SemaphoreType.DMA,
            pltpu.SemaphoreType.DMA((held,)),
        ],
        compiler_params=pltpu.CompilerParams(vmem_limit_bytes=16 * MIB),
        name="pick",
    )(in_hbm(ids), in_hbm(table), *others)


def in_hbm(array):
    return pltpu.with_memory_space_constraint(array, pltpu.HBM)


def fold_kernel(keep_ref, got_ref, first_ref, delta_ref, after_ref, *outs):
    own_ref, send_ref, beside_ref = outs
    total = keep_ref[...].astype(jnp.float32) + got_ref[...].astype(jnp.float32)
    half = own_ref.shape[0]
    own_ref[...] = total[:half].astype(own_ref.dtype)
    send_ref[...] = total[half:].astype(send_ref.dtype)
    beside_ref[...] = jnp.concatenate(
        [first_ref[...].astype(jnp.float32), delta_ref[...].astype(jnp.float32)], axis=0
    ).astype(beside_ref.dtype)


def folded(keep, got, first, deltas, after):
    rows, width = keep.shape
    vmem = pl.BlockSpec(memory_space=pltpu.VMEM)
    part = jax.ShapeDtypeStruct((rows // 2, width), keep.dtype)
    return pl.pallas_call(
        fold_kernel,
        out_shape=(part, part, jax.ShapeDtypeStruct((2 * first.shape[0], width), keep.dtype)),
        in_specs=[vmem] * 4 + [pl.BlockSpec(memory_space=pl.ANY)],
        out_specs=(vmem,) * 3,
        compiler_params=pltpu.CompilerParams(vmem_limit_bytes=12 * MIB),
        name="fold",
    )(keep, got, first, deltas, after)


def plus_kernel(own_ref, got_ref, *refs):
    out_ref = refs[-1]
    out_ref[...] = own_ref[...] + got_ref[...]


def join_kernel(own_ref, got_ref, *refs):
    out_ref = refs[-1]
    half = own_ref.shape[0] // 2
    own, got = own_ref[...].astype(jnp.float32), got_ref[...].astype(jnp.float32)
    parts = [own[:half], got[:half], own[half:], got[half:]]
    out_ref[...] = jnp.concatenate(parts, axis=0).astype(out_ref.dtype)


def chips_kernel(one_ref, one_got_ref, two_ref, two_got_ref, *refs):
    out_ref = refs[-1]
    own = [ref[...].astype(jnp.float32) for ref in (one_ref, two_ref)]
    got = [ref[...].astype(jnp.float32) for ref in (one_got_ref, two_got_ref)]
    own, got = jnp.concatenate(own, axis=0), jnp.concatenate(got, axis=0)
    upper = lax.axis_index("vocab") // 2 % 2 == 1
    rows = own.shape[0]
    out_ref[:rows, :] = jnp.where(upper, got, own).astype(out_ref.dtype)
    out_ref[rows:, :] = jnp.where(upper, own, got).astype(out_ref.dtype)


def chips(one, one_got, two, two_got, *after):
    rows, width = one.shape
    vmem = pl.BlockSpec(memory_space=pltpu.VMEM)
    return pl.pallas_call(
        chips_kernel,
        out_shape=jax.ShapeDtypeStruct((4 * rows, width), one.dtype),
        in_specs=[vmem] * 4 + [pl.BlockSpec(memory_space=pl.ANY)] * len(after),
        out_specs=vmem,
        compiler_params=pltpu.CompilerParams(vmem_limit_bytes=12 * MIB),
        name="chips",
    )(one, one_got, two, two_got, *after)


def merge_kernel(own_ref, got_ref, *refs):
    out_ref = refs[-1]
    own, got = own_ref[...], got_ref[...]
    peak = jnp.maximum(own[0:1], got[0:1])
    out_ref[0:1, :] = peak
    out_ref[1:2, :] = own[1:2] * jnp.exp(own[0:1] - peak) + got[1:2] * jnp.exp(got[0:1] - peak)


def paired(kernel, own, got, rows, name, *after):
    vmem = pl.BlockSpec(memory_space=pltpu.VMEM)
    return pl.pallas_call(
        kernel,
        out_shape=jax.ShapeDtypeStruct((rows, own.shape[1]), own.dtype),
        in_specs=[vmem] * 2 + [pl.BlockSpec(memory_space=pl.ANY)] * len(after),
        out_specs=vmem,
        compiler_params=pltpu.CompilerParams(vmem_limit_bytes=12 * MIB),
        name=name,
    )(own, got, *after)


def swapped(rows, bit):
    pairs = [(i, i ^ bit) for i in range(lax.axis_size("vocab"))]
    return lax.ppermute(rows, "vocab", pairs)


def load_kernel(first, last, table_ref, *refs):
    out_ref, token_ref, sems = refs[-3:]
    parts = sems.shape[0]
    part = (last - first) // parts
    rows = [pl.ds(first + k * part, part) for k in range(parts)]
    copies = [
        pltpu.make_async_copy(table_ref.at[at], out_ref.at[at], sems.at[k])
        for k, at in enumerate(rows)
    ]
    for copy in copies:
        copy.start()
    token_ref[...] = jnp.zeros_like(token_ref)
    for copy in copies:
        copy.wait()


def loaded(table, first, last, held, *after):
    anywhere, vmem = pl.BlockSpec(memory_space=pl.ANY), pl.BlockSpec(memory_space=pltpu.VMEM)
    held = [] if held is None else [held]
    return pl.pallas_call(
        functools.partial(load_kernel, first, last),
        out_shape=(
            jax.ShapeDtypeStruct(table.shape, table.dtype),
            jax.ShapeDtypeStruct((8, 128), jnp.float32),
        ),
        in_specs=[anywhere] * (1 + len(after)) + [vmem] * len(held),
        out_specs=(vmem, vmem),
        input_output_aliases={1 + len(after): 0} if held else {},
        scratch_shapes=[pltpu.SemaphoreType.DMA((4,))],
        compiler_params=pltpu.CompilerParams(vmem_limit_bytes=4 * MIB),
        name="load",
    )(in_hbm(table), *after, *held)


def rescaled(hidden, gain):
    squares = jnp.mean(hidden * hidden, axis=-1, keepdims=True)
    return hidden * lax.rsqrt(squares + 1e-06) * gain


def in_order(rows):
    me = lax.axis_index("vocab")
    bits = lax.axis_size("vocab").bit_length() - 3
    for k in range(bits):
        size = rows.shape[0] >> k + 1
        parts = [rows[i * size : (i + 1) * size] for i in range(2 << k)]
        other = [parts[i ^ 1] for i in range(2 << k)]
        rows = jnp.where(me // 4 >> k & 1 != 0, jnp.concatenate(other), jnp.concatenate(parts))
    return rows


def first_kernel(hidden_ref, gain_ref, out_ref):
    hidden = in_order(hidden_ref[...].astype(jnp.float32))
    out_ref[...] = rescaled(hidden, gain_ref[...]).astype(out_ref.dtype)


def second_kernel(delta_ref, gain_ref, own_ref, got_ref, out_ref):
    width = out_ref.shape[1]
    picked = own_ref[...].astype(jnp.float32) + got_ref[...].astype(jnp.float32)
    embedded = (picked * math.sqrt(width)).astype(jnp.bfloat16)
    hidden = embedded.astype(jnp.float32) + in_order(delta_ref[...].astype(jnp.float32))
    out_ref[...] = rescaled(hidden, gain_ref[...]).astype(out_ref.dtype)


def normed(kernel, hidden, gain, *picked):
    rows, width = hidden.shape
    vmem = pl.BlockSpec(memory_space=pltpu.VMEM)
    return pl.pallas_call(
        kernel,
        out_shape=jax.ShapeDtypeStruct((rows, width), jnp.bfloat16),
        in_specs=[vmem] * (2 + len(picked)),
        out_specs=vmem,
        compiler_params=pltpu.CompilerParams(vmem_limit_bytes=12 * MIB),
        name="norm",
    )(hidden, gain.reshape(1, width), *picked)


def head_kernel(own_ref, got_ref, table_ref, temps_ref, scaled_ref, stats_ref):
    me = lax.axis_index("vocab")
    dims = (((1,), (1,)), ((), ()))
    own, got = own_ref[...], got_ref[...]
    states = jnp.where(
        me % 2 == 1, jnp.concatenate([got, own], axis=0), jnp.concatenate([own, got], axis=0)
    )
    logits = lax.dot_general(table_ref[...], states, dims, preferred_element_type=jnp.float32)
    scaled = logits / temps_ref[...]
    scaled_ref[...] = scaled
    peak = jnp.max(scaled, axis=0, keepdims=True)
    stats_ref[0:1, :] = peak
    stats_ref[1:2, :] = jnp.sum(jnp.exp(scaled - peak), axis=0, keepdims=True)


def head(own, got, table, temps):
    voc_dev, width = table.shape
    rows = 2 * own.shape[0]
    return pl.pallas_call(
        head_kernel,
        out_shape=(
            jax.ShapeDtypeStruct((voc_dev, rows), jnp.float32),
            jax.ShapeDtypeStruct((2, rows), jnp.float32),
        ),
        in_specs=[pl.BlockSpec(memory_space=pltpu.VMEM)] * 4,
        out_specs=(pl.BlockSpec(memory_space=pltpu.VMEM),) * 2,
        compiler_params=pltpu.CompilerParams(vmem_limit_bytes=30 * MIB),
        name="head",
    )(own, got, table, temps)


def turn_kernel(order, scaled_ref, out_ref):
    turned = scaled_ref[...].T
    for place, (step, row) in enumerate(order):
        out_ref[step, row : row + 1, :] = turned[place : place + 1]


def turned(scaled, order, steps):
    voc_dev, rows = scaled.shape
    return pl.pallas_call(
        functools.partial(turn_kernel, order),
        out_shape=jax.ShapeDtypeStruct((steps, rows // steps, voc_dev), jnp.float32),
        compiler_params=pltpu.CompilerParams(vmem_limit_bytes=12 * MIB),
        name="turn",
    )(scaled)


def finish_kernel(order, scaled_ref, own_ref, got_ref, out_ref):
    own, got = own_ref[...], got_ref[...]
    peak = jnp.maximum(own[0:1], got[0:1])
    total = own[1:2] * jnp.exp(own[0:1] - peak) + got[1:2] * jnp.exp(got[0:1] - peak)
    both = jnp.concatenate([peak, jnp.log(total)], axis=0)
    rows = both.shape[1]
    spread = jnp.broadcast_to(both[:, None, :], (2, 128, rows))
    peak, log = spread[0].T, spread[1].T
    voc_dev = out_ref.shape[2]
    peak = jnp.concatenate([peak] * (voc_dev // 128), axis=1)
    log = jnp.concatenate([log] * (voc_dev // 128), axis=1)
    for place, (step, row) in enumerate(order):
        at = slice(place, place + 1)
        out_ref[step, row : row + 1, :] = scaled_ref[step, row : row + 1, :] - peak[at] - log[at]


def finished(scaled, own, got, order):
    return pl.pallas_call(
        functools.partial(finish_kernel, order),
        out_shape=jax.ShapeDtypeStruct(scaled.shape, jnp.float32),
        compiler_params=pltpu.CompilerParams(vmem_limit_bytes=12 * MIB),
        name="finish",
    )(scaled, own, got)


def merged(own, got):
    peak = jnp.maximum(own[0], got[0])
    total = own[1] * jnp.exp(own[0] - peak) + got[1] * jnp.exp(got[0] - peak)
    return jnp.stack([peak, total])


def body(first, deltas, gain, table, lookup, classes, ids):
    shards = lax.axis_size("vocab")
    rows_dev, width = first.shape
    steps, rows = ids.shape
    quarter = rows // 4
    high = [1 << k for k in range(shards.bit_length() - 2, 1, -1)]

    order = table_rows(rows, shards)
    places = [
        (step, order[pair * quarter + k])
        for pair in range(4)
        for step in range(steps)
        for k in range(quarter)
    ]

    keep, send, temps = picked_rows(ids, table, 0, places, classes, lookup)
    voc_dev = table.shape[0]
    head_table, token = loaded(table, 0, voc_dev // 8, None, send)
    own, send, beside = folded(keep, swapped(send, 1), first, deltas, token)
    own = own + swapped(send, 2)
    keep, send = picked_rows(ids, table, 1, (), own)
    keep = keep + swapped(send, 1)
    following = keep[:quarter] + swapped(keep[quarter:], 2)
    for k, bit in enumerate(high):
        held = beside.shape[0] // 2
        moved = swapped(beside, bit)
        got = swapped(own, bit)
        if k < len(high) - 1:
            beside = paired(join_kernel, beside, moved, 4 * held, "join", own)
            own = paired(plus_kernel, own, got, quarter, "plus", send)
    state = jnp.concatenate([beside[:held], moved[:held]], axis=0)
    delta = jnp.concatenate([beside[held:], moved[held:]], axis=0)
    one = normed(first_kernel, state, gain)
    one_got = swapped(one, 2)
    two = normed(second_kernel, delta, gain, own, got)
    head_table, token = loaded(table, voc_dev // 8, voc_dev, head_table, two)
    states = chips(one, one_got, two, swapped(two, 2), token, following)
    others = swapped(states, 1)
    scaled, stats = head(states, others, head_table, temps)
    scaled = turned(scaled, places, steps)
    for bit in reversed(high):
        half = following.shape[0] // 2
        following = following[:half] + swapped(following[half:], bit)
    embedded = (following.astype(jnp.float32) * math.sqrt(width)).astype(jnp.bfloat16)
    for bit in high[:-1]:
        stats = merged(stats, swapped(stats, bit))
    stats = paired(merge_kernel, stats, swapped(stats, high[-1]), 2, "merge", following)
    stats = merged(stats, swapped(stats, 2))
    logprobs = finished(scaled, stats, swapped(stats, 1), places)
    return logprobs, embedded


def solution(mesh):
    in_specs = (
        P(("groups", "vocab"), None),
        P(("groups", "vocab"), None),
        P(),
        P("vocab", None),
        P(),
        P(None, "groups"),
        P(None, "groups"),
    )
    out_specs = (P(None, "groups", "vocab"), P(("groups", "vocab"), None))
    return jax.shard_map(body, mesh=mesh, in_specs=in_specs, out_specs=out_specs, check_vma=False)
```

```python
import functools
import math

import jax
import jax.numpy as jnp
from jax import lax
from jax.experimental import pallas as pl
from jax.experimental.pallas import tpu as pltpu
from jax.sharding import PartitionSpec as P

BLOCK = 16
MIB = 2**20


def reversed_bits(value, bits):
    out = 0
    for k in range(bits):
        out = out * 2 + (value >> k & 1)
    return out


def table_rows(rows, shards):
    bits = shards.bit_length() - 3
    dev = rows // shards
    return [
        (reversed_bits(q, bits) * 4 + y * 2 + c) * dev + j
        for c in range(2)
        for y in range(2)
        for q in range(shards // 4)
        for j in range(dev)
    ]


def pick_kernel(step, places, ids_ref, table_ref, *refs):
    *refs, ids, listed, slots, rows, ids_sem, sems = refs
    if places:
        class_ref, heat_ref, *outs, temps_ref, classes, heat, heat_sems = refs
        heat_copies = [
            pltpu.make_async_copy(class_ref, classes, heat_sems.at[0]),
            pltpu.make_async_copy(heat_ref, heat, heat_sems.at[1]),
        ]
    else:
        outs = refs[-2:]
    count = ids_ref.shape[1]
    held = slots.shape[0]
    voc_dev = table_ref.shape[0]
    shards = lax.axis_size("vocab")
    bits = shards.bit_length() - 3
    rows_dev = count // shards
    me = lax.axis_index("vocab")
    offset = me * voc_dev
    low = me % 4
    fetch = pltpu.make_async_copy(ids_ref, ids, ids_sem)
    fetch.start()
    if places:
        for fetched in heat_copies:
            fetched.start()
    rows[...] = jnp.zeros_like(rows)
    fetch.wait()

    def copy(n):
        base = pl.multiple_of(listed[n] // count // BLOCK * BLOCK, BLOCK)
        slot = n % held
        return pltpu.make_async_copy(
            table_ref.at[pl.ds(base, BLOCK)], slots.at[slot], sems.at[slot]
        )

    found = jnp.int32(0)
    for r in range(count):
        local = ids[step, r] - offset
        listed[found] = local * count + r
        found = found + ((local >= 0) & (local < voc_dev)).astype(jnp.int32)

    for first in range(0, count, held):
        last = jnp.minimum(found, first + held)

        @pl.loop(first, last)
        def _(n):
            copy(n).start()

        if places and first == 0:
            for fetched in heat_copies:
                fetched.wait()
            temps = jnp.ones(temps_ref.shape, jnp.float32)
            lane = lax.broadcasted_iota(jnp.int32, temps.shape, 1)
            for place, (at, row) in enumerate(places):
                temps = jnp.where(lane == place, heat[classes[at, row]], temps)
            temps_ref[...] = temps

        @pl.loop(first, last)
        def _(n):
            entry = listed[n]
            r = entry % count
            copy(n).wait()
            block = slots[n % held].astype(jnp.float32)
            sub = lax.broadcasted_iota(jnp.int32, block.shape, 0)
            picked = jnp.sum(
                jnp.where(sub == entry // count % BLOCK, block, 0.0), axis=0, keepdims=True
            )
            owner = r // rows_dev
            way = owner % 4 ^ low
            chip = owner // 4 if step == 0 else owner // 4 ^ me // 4
            order = sum((chip >> k) % 2 << (bits - 1 - k) for k in range(bits))
            place = (way % 2 * 2 + way // 2) * (shards // 4) + order
            rows[pl.ds(place * rows_dev + r % rows_dev, 1), :] = picked

    half = count // 2
    for part, out in enumerate(outs):
        out[...] = rows[part * half : (part + 1) * half].astype(out.dtype)


def picked_rows(ids, table, step, places, *others):
    count = ids.shape[1]
    width = table.shape[1]
    held = min(count, 32)
    out = (jax.ShapeDtypeStruct((count // 2, width), table.dtype),) * 2
    heat = []
    if places:
        out += (jax.ShapeDtypeStruct((1, len(places)), jnp.float32),)
        others = [in_hbm(other) for other in others]
        heat = [pltpu.SMEM(other.shape, other.dtype) for other in others]
        heat += [pltpu.SemaphoreType.DMA((2,))]
    anywhere, vmem = pl.BlockSpec(memory_space=pl.ANY), pl.BlockSpec(memory_space=pltpu.VMEM)
    return pl.pallas_call(
        functools.partial(pick_kernel, step, places),
        out_shape=out,
        in_specs=[anywhere] * (2 + len(others)),
        out_specs=(vmem,) * len(out),
        scratch_shapes=heat
        + [
            pltpu.SMEM(ids.shape, jnp.int32),
            pltpu.SMEM((count + 1,), jnp.int32),
            pltpu.VMEM((held, BLOCK, width), table.dtype),
            pltpu.VMEM((count, width), jnp.float32),
            pltpu.SemaphoreType.DMA,
            pltpu.SemaphoreType.DMA((held,)),
        ],
        compiler_params=pltpu.CompilerParams(vmem_limit_bytes=16 * MIB),
        name="pick",
    )(in_hbm(ids), in_hbm(table), *others)


def in_hbm(array):
    return pltpu.with_memory_space_constraint(array, pltpu.HBM)


def fold_kernel(keep_ref, got_ref, first_ref, delta_ref, after_ref, *outs):
    own_ref, send_ref, beside_ref = outs
    total = keep_ref[...].astype(jnp.float32) + got_ref[...].astype(jnp.float32)
    half = own_ref.shape[0]
    own_ref[...] = total[:half].astype(own_ref.dtype)
    send_ref[...] = total[half:].astype(send_ref.dtype)
    beside_ref[...] = jnp.concatenate(
        [first_ref[...].astype(jnp.float32), delta_ref[...].astype(jnp.float32)], axis=0
    ).astype(beside_ref.dtype)


def folded(keep, got, first, deltas, after):
    rows, width = keep.shape
    vmem = pl.BlockSpec(memory_space=pltpu.VMEM)
    part = jax.ShapeDtypeStruct((rows // 2, width), keep.dtype)
    return pl.pallas_call(
        fold_kernel,
        out_shape=(part, part, jax.ShapeDtypeStruct((2 * first.shape[0], width), keep.dtype)),
        in_specs=[vmem] * 4 + [pl.BlockSpec(memory_space=pl.ANY)],
        out_specs=(vmem,) * 3,
        compiler_params=pltpu.CompilerParams(vmem_limit_bytes=12 * MIB),
        name="fold",
    )(keep, got, first, deltas, after)


def plus_kernel(own_ref, got_ref, *refs):
    out_ref = refs[-1]
    out_ref[...] = own_ref[...] + got_ref[...]


def join_kernel(own_ref, got_ref, *refs):
    out_ref = refs[-1]
    half = own_ref.shape[0] // 2
    own, got = own_ref[...].astype(jnp.float32), got_ref[...].astype(jnp.float32)
    parts = [own[:half], got[:half], own[half:], got[half:]]
    out_ref[...] = jnp.concatenate(parts, axis=0).astype(out_ref.dtype)


def chips_kernel(one_ref, one_got_ref, two_ref, two_got_ref, *refs):
    out_ref = refs[-1]
    own = [ref[...].astype(jnp.float32) for ref in (one_ref, two_ref)]
    got = [ref[...].astype(jnp.float32) for ref in (one_got_ref, two_got_ref)]
    own, got = jnp.concatenate(own, axis=0), jnp.concatenate(got, axis=0)
    upper = lax.axis_index("vocab") // 2 % 2 == 1
    rows = own.shape[0]
    out_ref[:rows, :] = jnp.where(upper, got, own).astype(out_ref.dtype)
    out_ref[rows:, :] = jnp.where(upper, own, got).astype(out_ref.dtype)


def chips(one, one_got, two, two_got, *after):
    rows, width = one.shape
    vmem = pl.BlockSpec(memory_space=pltpu.VMEM)
    return pl.pallas_call(
        chips_kernel,
        out_shape=jax.ShapeDtypeStruct((4 * rows, width), one.dtype),
        in_specs=[vmem] * 4 + [pl.BlockSpec(memory_space=pl.ANY)] * len(after),
        out_specs=vmem,
        compiler_params=pltpu.CompilerParams(vmem_limit_bytes=12 * MIB),
        name="chips",
    )(one, one_got, two, two_got, *after)


def merge_kernel(own_ref, got_ref, *refs):
    out_ref = refs[-1]
    own, got = own_ref[...], got_ref[...]
    peak = jnp.maximum(own[0:1], got[0:1])
    out_ref[0:1, :] = peak
    out_ref[1:2, :] = own[1:2] * jnp.exp(own[0:1] - peak) + got[1:2] * jnp.exp(got[0:1] - peak)


def paired(kernel, own, got, rows, name, *after):
    vmem = pl.BlockSpec(memory_space=pltpu.VMEM)
    return pl.pallas_call(
        kernel,
        out_shape=jax.ShapeDtypeStruct((rows, own.shape[1]), own.dtype),
        in_specs=[vmem] * 2 + [pl.BlockSpec(memory_space=pl.ANY)] * len(after),
        out_specs=vmem,
        compiler_params=pltpu.CompilerParams(vmem_limit_bytes=12 * MIB),
        name=name,
    )(own, got, *after)


def swapped(rows, bit):
    pairs = [(i, i ^ bit) for i in range(lax.axis_size("vocab"))]
    return lax.ppermute(rows, "vocab", pairs)


def load_kernel(first, last, table_ref, *refs):
    out_ref, token_ref, sems = refs[-3:]
    parts = sems.shape[0]
    part = (last - first) // parts
    rows = [pl.ds(first + k * part, part) for k in range(parts)]
    copies = [
        pltpu.make_async_copy(table_ref.at[at], out_ref.at[at], sems.at[k])
        for k, at in enumerate(rows)
    ]
    for copy in copies:
        copy.start()
    token_ref[...] = jnp.zeros_like(token_ref)
    for copy in copies:
        copy.wait()


def loaded(table, first, last, held, *after):
    anywhere, vmem = pl.BlockSpec(memory_space=pl.ANY), pl.BlockSpec(memory_space=pltpu.VMEM)
    held = [] if held is None else [held]
    return pl.pallas_call(
        functools.partial(load_kernel, first, last),
        out_shape=(
            jax.ShapeDtypeStruct(table.shape, table.dtype),
            jax.ShapeDtypeStruct((8, 128), jnp.float32),
        ),
        in_specs=[anywhere] * (1 + len(after)) + [vmem] * len(held),
        out_specs=(vmem, vmem),
        input_output_aliases={1 + len(after): 0} if held else {},
        scratch_shapes=[pltpu.SemaphoreType.DMA((8,))],
        compiler_params=pltpu.CompilerParams(vmem_limit_bytes=4 * MIB),
        name="load",
    )(in_hbm(table), *after, *held)


def rescaled(hidden, gain):
    squares = jnp.mean(hidden * hidden, axis=-1, keepdims=True)
    return hidden * lax.rsqrt(squares + 1e-06) * gain


def in_order(rows):
    me = lax.axis_index("vocab")
    bits = lax.axis_size("vocab").bit_length() - 3
    for k in range(bits):
        size = rows.shape[0] >> k + 1
        parts = [rows[i * size : (i + 1) * size] for i in range(2 << k)]
        other = [parts[i ^ 1] for i in range(2 << k)]
        rows = jnp.where(me // 4 >> k & 1 != 0, jnp.concatenate(other), jnp.concatenate(parts))
    return rows


def first_kernel(hidden_ref, gain_ref, out_ref):
    hidden = in_order(hidden_ref[...].astype(jnp.float32))
    out_ref[...] = rescaled(hidden, gain_ref[...]).astype(out_ref.dtype)


def second_kernel(delta_ref, gain_ref, own_ref, got_ref, out_ref):
    width = out_ref.shape[1]
    picked = own_ref[...].astype(jnp.float32) + got_ref[...].astype(jnp.float32)
    embedded = (picked * math.sqrt(width)).astype(jnp.bfloat16)
    hidden = embedded.astype(jnp.float32) + in_order(delta_ref[...].astype(jnp.float32))
    out_ref[...] = rescaled(hidden, gain_ref[...]).astype(out_ref.dtype)


def normed(kernel, hidden, gain, *picked):
    rows, width = hidden.shape
    vmem = pl.BlockSpec(memory_space=pltpu.VMEM)
    return pl.pallas_call(
        kernel,
        out_shape=jax.ShapeDtypeStruct((rows, width), jnp.bfloat16),
        in_specs=[vmem] * (2 + len(picked)),
        out_specs=vmem,
        compiler_params=pltpu.CompilerParams(vmem_limit_bytes=12 * MIB),
        name="norm",
    )(hidden, gain.reshape(1, width), *picked)


def head_kernel(own_ref, got_ref, table_ref, temps_ref, scaled_ref, stats_ref):
    me = lax.axis_index("vocab")
    dims = (((1,), (1,)), ((), ()))
    own, got = own_ref[...], got_ref[...]
    states = jnp.where(
        me % 2 == 1, jnp.concatenate([got, own], axis=0), jnp.concatenate([own, got], axis=0)
    )
    logits = lax.dot_general(table_ref[...], states, dims, preferred_element_type=jnp.float32)
    scaled = logits / temps_ref[...]
    scaled_ref[...] = scaled
    peak = jnp.max(scaled, axis=0, keepdims=True)
    stats_ref[0:1, :] = peak
    stats_ref[1:2, :] = jnp.sum(jnp.exp(scaled - peak), axis=0, keepdims=True)


def head(own, got, table, temps):
    voc_dev, width = table.shape
    rows = 2 * own.shape[0]
    return pl.pallas_call(
        head_kernel,
        out_shape=(
            jax.ShapeDtypeStruct((voc_dev, rows), jnp.float32),
            jax.ShapeDtypeStruct((2, rows), jnp.float32),
        ),
        in_specs=[pl.BlockSpec(memory_space=pltpu.VMEM)] * 4,
        out_specs=(pl.BlockSpec(memory_space=pltpu.VMEM),) * 2,
        compiler_params=pltpu.CompilerParams(vmem_limit_bytes=30 * MIB),
        name="head",
    )(own, got, table, temps)


def turn_kernel(order, scaled_ref, out_ref):
    turned = scaled_ref[...].T
    for place, (step, row) in enumerate(order):
        out_ref[step, row : row + 1, :] = turned[place : place + 1]


def turned(scaled, order, steps):
    voc_dev, rows = scaled.shape
    return pl.pallas_call(
        functools.partial(turn_kernel, order),
        out_shape=jax.ShapeDtypeStruct((steps, rows // steps, voc_dev), jnp.float32),
        compiler_params=pltpu.CompilerParams(vmem_limit_bytes=12 * MIB),
        name="turn",
    )(scaled)


def finish_kernel(order, scaled_ref, own_ref, got_ref, out_ref):
    own, got = own_ref[...], got_ref[...]
    peak = jnp.maximum(own[0:1], got[0:1])
    total = own[1:2] * jnp.exp(own[0:1] - peak) + got[1:2] * jnp.exp(got[0:1] - peak)
    both = jnp.concatenate([peak, jnp.log(total)], axis=0)
    rows = both.shape[1]
    spread = jnp.broadcast_to(both[:, None, :], (2, 128, rows))
    peak, log = spread[0].T, spread[1].T
    voc_dev = out_ref.shape[2]
    peak = jnp.concatenate([peak] * (voc_dev // 128), axis=1)
    log = jnp.concatenate([log] * (voc_dev // 128), axis=1)
    for place, (step, row) in enumerate(order):
        at = slice(place, place + 1)
        out_ref[step, row : row + 1, :] = scaled_ref[step, row : row + 1, :] - peak[at] - log[at]


def finished(scaled, own, got, order):
    return pl.pallas_call(
        functools.partial(finish_kernel, order),
        out_shape=jax.ShapeDtypeStruct(scaled.shape, jnp.float32),
        compiler_params=pltpu.CompilerParams(vmem_limit_bytes=12 * MIB),
        name="finish",
    )(scaled, own, got)


def merged(own, got):
    peak = jnp.maximum(own[0], got[0])
    total = own[1] * jnp.exp(own[0] - peak) + got[1] * jnp.exp(got[0] - peak)
    return jnp.stack([peak, total])


def body(first, deltas, gain, table, lookup, classes, ids):
    shards = lax.axis_size("vocab")
    rows_dev, width = first.shape
    steps, rows = ids.shape
    quarter = rows // 4
    high = [1 << k for k in range(shards.bit_length() - 2, 1, -1)]

    order = table_rows(rows, shards)
    places = [
        (step, order[pair * quarter + k])
        for pair in range(4)
        for step in range(steps)
        for k in range(quarter)
    ]

    keep, send, temps = picked_rows(ids, table, 0, places, classes, lookup)
    voc_dev = table.shape[0]
    head_table, token = loaded(table, 0, voc_dev // 8, None, send)
    own, send, beside = folded(keep, swapped(send, 1), first, deltas, token)
    own = own + swapped(send, 2)
    keep, send = picked_rows(ids, table, 1, (), own)
    keep = keep + swapped(send, 1)
    following = keep[:quarter] + swapped(keep[quarter:], 2)
    for k, bit in enumerate(high):
        held = beside.shape[0] // 2
        moved = swapped(beside, bit)
        got = swapped(own, bit)
        if k < len(high) - 1:
            beside = paired(join_kernel, beside, moved, 4 * held, "join", own)
            own = paired(plus_kernel, own, got, quarter, "plus", send)
    state = jnp.concatenate([beside[:held], moved[:held]], axis=0)
    delta = jnp.concatenate([beside[held:], moved[held:]], axis=0)
    one = normed(first_kernel, state, gain)
    one_got = swapped(one, 2)
    two = normed(second_kernel, delta, gain, own, got)
    head_table, token = loaded(table, voc_dev // 8, voc_dev, head_table, two)
    states = chips(one, one_got, two, swapped(two, 2), token, following)
    others = swapped(states, 1)
    scaled, stats = head(states, others, head_table, temps)
    scaled = turned(scaled, places, steps)
    for bit in reversed(high):
        half = following.shape[0] // 2
        following = following[:half] + swapped(following[half:], bit)
    embedded = (following.astype(jnp.float32) * math.sqrt(width)).astype(jnp.bfloat16)
    for bit in high[:-1]:
        stats = merged(stats, swapped(stats, bit))
    stats = paired(merge_kernel, stats, swapped(stats, high[-1]), 2, "merge", following)
    stats = merged(stats, swapped(stats, 2))
    logprobs = finished(scaled, stats, swapped(stats, 1), places)
    return logprobs, embedded


def solution(mesh):
    in_specs = (
        P(("groups", "vocab"), None),
        P(("groups", "vocab"), None),
        P(),
        P("vocab", None),
        P(),
        P(None, "groups"),
        P(None, "groups"),
    )
    out_specs = (P(None, "groups", "vocab"), P(("groups", "vocab"), None))
    return jax.shard_map(body, mesh=mesh, in_specs=in_specs, out_specs=out_specs, check_vma=False)
```

```python
import functools
import math

import jax
import jax.numpy as jnp
from jax import lax
from jax.experimental import pallas as pl
from jax.experimental.pallas import tpu as pltpu
from jax.sharding import PartitionSpec as P

BLOCK = 16
MIB = 2**20


def reversed_bits(value, bits):
    out = 0
    for k in range(bits):
        out = out * 2 + (value >> k & 1)
    return out


def table_rows(rows, shards):
    bits = shards.bit_length() - 3
    dev = rows // shards
    return [
        (reversed_bits(q, bits) * 4 + y * 2 + c) * dev + j
        for c in range(2)
        for y in range(2)
        for q in range(shards // 4)
        for j in range(dev)
    ]


def pick_kernel(step, places, ids_ref, table_ref, *refs):
    *refs, ids, listed, slots, rows, ids_sem, sems = refs
    if places:
        class_ref, heat_ref, *outs, temps_ref, classes, heat, heat_sems = refs
        heat_copies = [
            pltpu.make_async_copy(class_ref, classes, heat_sems.at[0]),
            pltpu.make_async_copy(heat_ref, heat, heat_sems.at[1]),
        ]
    else:
        outs = refs[-2:]
    count = ids_ref.shape[1]
    held = slots.shape[0]
    voc_dev = table_ref.shape[0]
    shards = lax.axis_size("vocab")
    bits = shards.bit_length() - 3
    rows_dev = count // shards
    me = lax.axis_index("vocab")
    offset = me * voc_dev
    low = me % 4
    fetch = pltpu.make_async_copy(ids_ref, ids, ids_sem)
    fetch.start()
    if places:
        for fetched in heat_copies:
            fetched.start()
    rows[...] = jnp.zeros_like(rows)
    fetch.wait()

    def copy(n):
        base = pl.multiple_of(listed[n] // count // BLOCK * BLOCK, BLOCK)
        slot = n % held
        return pltpu.make_async_copy(
            table_ref.at[pl.ds(base, BLOCK)], slots.at[slot], sems.at[slot]
        )

    found = jnp.int32(0)
    for r in range(count):
        local = ids[step, r] - offset
        listed[found] = local * count + r
        found = found + ((local >= 0) & (local < voc_dev)).astype(jnp.int32)

    for first in range(0, count, held):
        last = jnp.minimum(found, first + held)

        @pl.loop(first, last)
        def _(n):
            copy(n).start()

        if places and first == 0:
            for fetched in heat_copies:
                fetched.wait()
            temps = jnp.ones(temps_ref.shape, jnp.float32)
            lane = lax.broadcasted_iota(jnp.int32, temps.shape, 1)
            for place, (at, row) in enumerate(places):
                temps = jnp.where(lane == place, heat[classes[at, row]], temps)
            temps_ref[...] = temps

        @pl.loop(first, last)
        def _(n):
            entry = listed[n]
            r = entry % count
            copy(n).wait()
            block = slots[n % held].astype(jnp.float32)
            sub = lax.broadcasted_iota(jnp.int32, block.shape, 0)
            picked = jnp.sum(
                jnp.where(sub == entry // count % BLOCK, block, 0.0), axis=0, keepdims=True
            )
            owner = r // rows_dev
            way = owner % 4 ^ low
            chip = owner // 4 if step == 0 else owner // 4 ^ me // 4
            order = sum((chip >> k) % 2 << (bits - 1 - k) for k in range(bits))
            place = (way % 2 * 2 + way // 2) * (shards // 4) + order
            rows[pl.ds(place * rows_dev + r % rows_dev, 1), :] = picked

    half = count // 2
    for part, out in enumerate(outs):
        out[...] = rows[part * half : (part + 1) * half].astype(out.dtype)


def picked_rows(ids, table, step, places, *others):
    count = ids.shape[1]
    width = table.shape[1]
    held = min(count, 32)
    out = (jax.ShapeDtypeStruct((count // 2, width), table.dtype),) * 2
    heat = []
    if places:
        out += (jax.ShapeDtypeStruct((1, len(places)), jnp.float32),)
        others = [in_hbm(other) for other in others]
        heat = [pltpu.SMEM(other.shape, other.dtype) for other in others]
        heat += [pltpu.SemaphoreType.DMA((2,))]
    anywhere, vmem = pl.BlockSpec(memory_space=pl.ANY), pl.BlockSpec(memory_space=pltpu.VMEM)
    return pl.pallas_call(
        functools.partial(pick_kernel, step, places),
        out_shape=out,
        in_specs=[anywhere] * (2 + len(others)),
        out_specs=(vmem,) * len(out),
        scratch_shapes=heat
        + [
            pltpu.SMEM(ids.shape, jnp.int32),
            pltpu.SMEM((count + 1,), jnp.int32),
            pltpu.VMEM((held, BLOCK, width), table.dtype),
            pltpu.VMEM((count, width), jnp.float32),
            pltpu.SemaphoreType.DMA,
            pltpu.SemaphoreType.DMA((held,)),
        ],
        compiler_params=pltpu.CompilerParams(vmem_limit_bytes=16 * MIB),
        name="pick",
    )(in_hbm(ids), in_hbm(table), *others)


def in_hbm(array):
    return pltpu.with_memory_space_constraint(array, pltpu.HBM)


def fold_kernel(keep_ref, got_ref, first_ref, delta_ref, after_ref, *outs):
    own_ref, send_ref, beside_ref = outs
    total = keep_ref[...].astype(jnp.float32) + got_ref[...].astype(jnp.float32)
    half = own_ref.shape[0]
    own_ref[...] = total[:half].astype(own_ref.dtype)
    send_ref[...] = total[half:].astype(send_ref.dtype)
    beside_ref[...] = jnp.concatenate(
        [first_ref[...].astype(jnp.float32), delta_ref[...].astype(jnp.float32)], axis=0
    ).astype(beside_ref.dtype)


def folded(keep, got, first, deltas, after):
    rows, width = keep.shape
    vmem = pl.BlockSpec(memory_space=pltpu.VMEM)
    part = jax.ShapeDtypeStruct((rows // 2, width), keep.dtype)
    return pl.pallas_call(
        fold_kernel,
        out_shape=(part, part, jax.ShapeDtypeStruct((2 * first.shape[0], width), keep.dtype)),
        in_specs=[vmem] * 4 + [pl.BlockSpec(memory_space=pl.ANY)],
        out_specs=(vmem,) * 3,
        compiler_params=pltpu.CompilerParams(vmem_limit_bytes=12 * MIB),
        name="fold",
    )(keep, got, first, deltas, after)


def plus_kernel(own_ref, got_ref, *refs):
    out_ref = refs[-1]
    out_ref[...] = own_ref[...] + got_ref[...]


def join_kernel(own_ref, got_ref, *refs):
    out_ref = refs[-1]
    half = own_ref.shape[0] // 2
    own, got = own_ref[...].astype(jnp.float32), got_ref[...].astype(jnp.float32)
    parts = [own[:half], got[:half], own[half:], got[half:]]
    out_ref[...] = jnp.concatenate(parts, axis=0).astype(out_ref.dtype)


def chips_kernel(one_ref, one_got_ref, two_ref, two_got_ref, *refs):
    out_ref = refs[-1]
    own = [ref[...].astype(jnp.float32) for ref in (one_ref, two_ref)]
    got = [ref[...].astype(jnp.float32) for ref in (one_got_ref, two_got_ref)]
    own, got = jnp.concatenate(own, axis=0), jnp.concatenate(got, axis=0)
    upper = lax.axis_index("vocab") // 2 % 2 == 1
    rows = own.shape[0]
    out_ref[:rows, :] = jnp.where(upper, got, own).astype(out_ref.dtype)
    out_ref[rows:, :] = jnp.where(upper, own, got).astype(out_ref.dtype)


def chips(one, one_got, two, two_got, *after):
    rows, width = one.shape
    vmem = pl.BlockSpec(memory_space=pltpu.VMEM)
    return pl.pallas_call(
        chips_kernel,
        out_shape=jax.ShapeDtypeStruct((4 * rows, width), one.dtype),
        in_specs=[vmem] * 4 + [pl.BlockSpec(memory_space=pl.ANY)] * len(after),
        out_specs=vmem,
        compiler_params=pltpu.CompilerParams(vmem_limit_bytes=12 * MIB),
        name="chips",
    )(one, one_got, two, two_got, *after)


def merge_kernel(own_ref, got_ref, *refs):
    out_ref = refs[-1]
    own, got = own_ref[...], got_ref[...]
    peak = jnp.maximum(own[0:1], got[0:1])
    out_ref[0:1, :] = peak
    out_ref[1:2, :] = own[1:2] * jnp.exp(own[0:1] - peak) + got[1:2] * jnp.exp(got[0:1] - peak)


def paired(kernel, own, got, rows, name, *after):
    vmem = pl.BlockSpec(memory_space=pltpu.VMEM)
    return pl.pallas_call(
        kernel,
        out_shape=jax.ShapeDtypeStruct((rows, own.shape[1]), own.dtype),
        in_specs=[vmem] * 2 + [pl.BlockSpec(memory_space=pl.ANY)] * len(after),
        out_specs=vmem,
        compiler_params=pltpu.CompilerParams(vmem_limit_bytes=12 * MIB),
        name=name,
    )(own, got, *after)


def swapped(rows, bit):
    pairs = [(i, i ^ bit) for i in range(lax.axis_size("vocab"))]
    return lax.ppermute(rows, "vocab", pairs)


def load_kernel(first, last, table_ref, *refs):
    out_ref, token_ref, sems = refs[-3:]
    parts = sems.shape[0]
    part = (last - first) // parts
    rows = [pl.ds(first + k * part, part) for k in range(parts)]
    copies = [
        pltpu.make_async_copy(table_ref.at[at], out_ref.at[at], sems.at[k])
        for k, at in enumerate(rows)
    ]
    for copy in copies:
        copy.start()
    token_ref[...] = jnp.zeros_like(token_ref)
    for copy in copies:
        copy.wait()


def loaded(table, first, last, held, *after):
    anywhere, vmem = pl.BlockSpec(memory_space=pl.ANY), pl.BlockSpec(memory_space=pltpu.VMEM)
    held = [] if held is None else [held]
    return pl.pallas_call(
        functools.partial(load_kernel, first, last),
        out_shape=(
            jax.ShapeDtypeStruct(table.shape, table.dtype),
            jax.ShapeDtypeStruct((8, 128), jnp.float32),
        ),
        in_specs=[anywhere] * (1 + len(after)) + [vmem] * len(held),
        out_specs=(vmem, vmem),
        input_output_aliases={1 + len(after): 0} if held else {},
        scratch_shapes=[pltpu.SemaphoreType.DMA((4,))],
        compiler_params=pltpu.CompilerParams(vmem_limit_bytes=4 * MIB),
        name="load",
    )(in_hbm(table), *after, *held)


def rescaled(hidden, gain):
    squares = jnp.mean(hidden * hidden, axis=-1, keepdims=True)
    return hidden * lax.rsqrt(squares + 1e-06) * gain


def in_order(rows):
    me = lax.axis_index("vocab")
    bits = lax.axis_size("vocab").bit_length() - 3
    for k in range(bits):
        size = rows.shape[0] >> k + 1
        parts = [rows[i * size : (i + 1) * size] for i in range(2 << k)]
        other = [parts[i ^ 1] for i in range(2 << k)]
        rows = jnp.where(me // 4 >> k & 1 != 0, jnp.concatenate(other), jnp.concatenate(parts))
    return rows


def first_kernel(hidden_ref, gain_ref, out_ref):
    hidden = in_order(hidden_ref[...].astype(jnp.float32))
    out_ref[...] = rescaled(hidden, gain_ref[...]).astype(out_ref.dtype)


def second_kernel(delta_ref, gain_ref, own_ref, got_ref, out_ref):
    width = out_ref.shape[1]
    picked = own_ref[...].astype(jnp.float32) + got_ref[...].astype(jnp.float32)
    embedded = (picked * math.sqrt(width)).astype(jnp.bfloat16)
    hidden = embedded.astype(jnp.float32) + in_order(delta_ref[...].astype(jnp.float32))
    out_ref[...] = rescaled(hidden, gain_ref[...]).astype(out_ref.dtype)


def normed(kernel, hidden, gain, *picked):
    rows, width = hidden.shape
    vmem = pl.BlockSpec(memory_space=pltpu.VMEM)
    return pl.pallas_call(
        kernel,
        out_shape=jax.ShapeDtypeStruct((rows, width), jnp.bfloat16),
        in_specs=[vmem] * (2 + len(picked)),
        out_specs=vmem,
        compiler_params=pltpu.CompilerParams(vmem_limit_bytes=12 * MIB),
        name="norm",
    )(hidden, gain.reshape(1, width), *picked)


def head_kernel(own_ref, got_ref, table_ref, temps_ref, scaled_ref, stats_ref):
    me = lax.axis_index("vocab")
    dims = (((1,), (1,)), ((), ()))
    own, got = own_ref[...], got_ref[...]
    states = jnp.where(
        me % 2 == 1, jnp.concatenate([got, own], axis=0), jnp.concatenate([own, got], axis=0)
    )
    logits = lax.dot_general(table_ref[...], states, dims, preferred_element_type=jnp.float32)
    scaled = logits / temps_ref[...]
    scaled_ref[...] = scaled
    peak = jnp.max(scaled, axis=0, keepdims=True)
    stats_ref[0:1, :] = peak
    stats_ref[1:2, :] = jnp.sum(jnp.exp(scaled - peak), axis=0, keepdims=True)


def head(own, got, table, temps):
    voc_dev, width = table.shape
    rows = 2 * own.shape[0]
    return pl.pallas_call(
        head_kernel,
        out_shape=(
            jax.ShapeDtypeStruct((voc_dev, rows), jnp.float32),
            jax.ShapeDtypeStruct((2, rows), jnp.float32),
        ),
        in_specs=[pl.BlockSpec(memory_space=pltpu.VMEM)] * 4,
        out_specs=(pl.BlockSpec(memory_space=pltpu.VMEM),) * 2,
        compiler_params=pltpu.CompilerParams(vmem_limit_bytes=30 * MIB),
        name="head",
    )(own, got, table, temps)


def turn_kernel(order, scaled_ref, out_ref):
    turned = scaled_ref[...].T
    for place, (step, row) in enumerate(order):
        out_ref[step, row : row + 1, :] = turned[place : place + 1]


def turned(scaled, order, steps):
    voc_dev, rows = scaled.shape
    return pl.pallas_call(
        functools.partial(turn_kernel, order),
        out_shape=jax.ShapeDtypeStruct((steps, rows // steps, voc_dev), jnp.float32),
        compiler_params=pltpu.CompilerParams(vmem_limit_bytes=12 * MIB),
        name="turn",
    )(scaled)


def finish_kernel(order, scaled_ref, own_ref, got_ref, out_ref, held, sems):
    own, got = own_ref[...], got_ref[...]
    peak = jnp.maximum(own[0:1], got[0:1])
    total = own[1:2] * jnp.exp(own[0:1] - peak) + got[1:2] * jnp.exp(got[0:1] - peak)
    both = jnp.concatenate([peak, jnp.log(total)], axis=0)
    rows = both.shape[1]
    spread = jnp.broadcast_to(both[:, None, :], (2, 128, rows))
    peak, log = spread[0].T, spread[1].T
    voc_dev = out_ref.shape[2]
    peak = jnp.concatenate([peak] * (voc_dev // 128), axis=1)
    log = jnp.concatenate([log] * (voc_dev // 128), axis=1)
    copies = []
    for now in range(held.shape[0]):
        for place, (step, row) in enumerate(order):
            if step == now:
                at = slice(place, place + 1)
                held[step, row : row + 1, :] = scaled_ref[step, row : row + 1, :] - peak[at] - log[at]
        copies.append(pltpu.make_async_copy(held.at[now], out_ref.at[now], sems.at[now]))
        copies[-1].start()
    for copy in copies:
        copy.wait()


def finished(scaled, own, got, order):
    return pl.pallas_call(
        functools.partial(finish_kernel, order),
        out_shape=jax.ShapeDtypeStruct(scaled.shape, jnp.float32),
        in_specs=[pl.BlockSpec(memory_space=pltpu.VMEM)] * 3,
        out_specs=pl.BlockSpec(memory_space=pl.ANY),
        scratch_shapes=[
            pltpu.VMEM(scaled.shape, jnp.float32),
            pltpu.SemaphoreType.DMA(scaled.shape[:1]),
        ],
        compiler_params=pltpu.CompilerParams(vmem_limit_bytes=12 * MIB),
        name="finish",
    )(scaled, own, got)


def merged(own, got):
    peak = jnp.maximum(own[0], got[0])
    total = own[1] * jnp.exp(own[0] - peak) + got[1] * jnp.exp(got[0] - peak)
    return jnp.stack([peak, total])


def body(first, deltas, gain, table, lookup, classes, ids):
    shards = lax.axis_size("vocab")
    rows_dev, width = first.shape
    steps, rows = ids.shape
    quarter = rows // 4
    high = [1 << k for k in range(shards.bit_length() - 2, 1, -1)]

    order = table_rows(rows, shards)
    places = [
        (step, order[pair * quarter + k])
        for pair in range(4)
        for step in range(steps)
        for k in range(quarter)
    ]

    keep, send, temps = picked_rows(ids, table, 0, places, classes, lookup)
    voc_dev = table.shape[0]
    head_table, token = loaded(table, 0, voc_dev // 8, None, send)
    own, send, beside = folded(keep, swapped(send, 1), first, deltas, token)
    own = own + swapped(send, 2)
    keep, send = picked_rows(ids, table, 1, (), own)
    keep = keep + swapped(send, 1)
    following = keep[:quarter] + swapped(keep[quarter:], 2)
    for k, bit in enumerate(high):
        held = beside.shape[0] // 2
        moved = swapped(beside, bit)
        got = swapped(own, bit)
        if k < len(high) - 1:
            beside = paired(join_kernel, beside, moved, 4 * held, "join", own)
            own = paired(plus_kernel, own, got, quarter, "plus", send)
    state = jnp.concatenate([beside[:held], moved[:held]], axis=0)
    delta = jnp.concatenate([beside[held:], moved[held:]], axis=0)
    one = normed(first_kernel, state, gain)
    one_got = swapped(one, 2)
    two = normed(second_kernel, delta, gain, own, got)
    head_table, token = loaded(table, voc_dev // 8, voc_dev, head_table, two)
    states = chips(one, one_got, two, swapped(two, 2), token, following)
    others = swapped(states, 1)
    scaled, stats = head(states, others, head_table, temps)
    scaled = turned(scaled, places, steps)
    for bit in reversed(high):
        half = following.shape[0] // 2
        following = following[:half] + swapped(following[half:], bit)
    embedded = (following.astype(jnp.float32) * math.sqrt(width)).astype(jnp.bfloat16)
    for bit in high[:-1]:
        stats = merged(stats, swapped(stats, bit))
    stats = paired(merge_kernel, stats, swapped(stats, high[-1]), 2, "merge", following)
    stats = merged(stats, swapped(stats, 2))
    logprobs = finished(scaled, stats, swapped(stats, 1), places)
    return logprobs, embedded


def solution(mesh):
    in_specs = (
        P(("groups", "vocab"), None),
        P(("groups", "vocab"), None),
        P(),
        P("vocab", None),
        P(),
        P(None, "groups"),
        P(None, "groups"),
    )
    out_specs = (P(None, "groups", "vocab"), P(("groups", "vocab"), None))
    return jax.shard_map(body, mesh=mesh, in_specs=in_specs, out_specs=out_specs, check_vma=False)
```
